32 devices in a mesh: ens: 2 (over y), gx: 4 (over z), gy: 2 (over x), gz: 2 (over core).
Axes of the slice: x: 2, y: 2, z: 4, core: 2. Of those that a mesh axis runs over, the one named last changes fastest.
Arguments:
- ocean_temp: float32 [128, 128, 512], P(('ens', 'gz'), 'gx', 'gy'), parts along dimension 0, may hold values from -6 to 6
- bathy_levels: int32 [256, 512], P(('ens', 'gx'), 'gy'), parts along dimension 0, may hold values from 0 to 64
- mixing: float32 [256, 512], P(('ens', 'gx'), 'gy'), parts along dimension 0, may hold values from 0.02 to 0.3
- atm_flux: bfloat16 [128, 2, 128], P(('ens', 'gx', 'gy')), parts along dimension 0, may hold values from -6 to 6
- send_tiles: int32 [8, 8, 1], replicated, may hold values from -1 to 7, as said below
- regrid_slots: int32 [2, 1024], P(None, ('gx', 'gy', 'gz')), may hold values from 0 to 63, as said below
- regrid_weights: bfloat16 [1024, 128, 128], P(('gx', 'gy', 'gz'))
Outputs:
- ocean_final: float32 [128, 128, 512], P(('ens', 'gz'), 'gx', 'gy'), parts along dimension 0
- atm_surface: float32 [128, 128], P(('ens', 'gx', 'gy')), parts along dimension 0
The draws below stay inside these ranges and needn't reach their ends.
There are 2 independent parts, one for each index of `ens`. The reference program is written for one: setup_inputs(seed, part) draws one part's arguments, and reference() takes and returns one part's arrays. A program takes and returns all parts, laid end to end along the dimension named above; an argument that names none is the same for every part. Nothing has to cross between parts.
Inputs may be any that keep to these rules, and one draw needn't show every extreme that they name: send_tiles[b, d, c] is the atmosphere tile of block b sent to block d in slot c, -1 where nothing is sent; a block sends at most 1 tiles to one destination, and each block receives 4 tiles. `regrid_slots`: row 0 holds the received position b * 1 + c of each slot, always a sent position, and every position sent to a block is named by some slot of it; row 1 the destination ocean tile.
All inputs are finite; a program needn't handle non-finite values.
Results may differ from the reference program's by a relative error of at most 0.00044.
Values may be sent and summed in bfloat16 or wider, within the bound.
No kernel may reach another device: no remote copies, remote signals or barrier semaphores. Data moves between devices by JAX's collectives and lax.ppermute only.
A program may use at most 64 MiB of HBM per device.

```python
import math
import jax
import jax.numpy as jnp
from jax import lax

NORTHSOUTH_SPAN = 32
EASTWEST_SPAN = 256
STEPS = 4
AT = 8
TA = 128
PATCH_AREA_SIZE = 128
CAP = 1
K = 128
LEV = 64
NX = 128
NY = 512
ATM_TILES = 64
SLOTS = 1024
N_GX = 4
N_GY = 2


def regrid_plan(key):
    number_partitions = N_GX * N_GY
    reach_count = number_partitions // 2
    total_tiles = number_partitions * AT
    owners = jax.random.permutation(key, number_partitions).astype(jnp.int32)
    dest = jnp.arange(number_partitions, dtype=jnp.int32)[:, None]
    offset = jnp.arange(reach_count, dtype=jnp.int32)[None, :]
    placed = (dest * AT + offset) % total_tiles
    sender = owners[placed % number_partitions]
    local_tile = placed // number_partitions
    dest_full = jnp.broadcast_to(dest, placed.shape)
    sending = jnp.full((number_partitions, number_partitions, CAP), -1, jnp.int32)
    sending = sending.at[sender, dest_full, 0].set(local_tile.astype(jnp.int32))
    slot_index = jnp.arange(K, dtype=jnp.int32)[None, :]
    ocean_tile = slot_index // 2
    reach = slot_index * reach_count // K
    slot_place = (dest * AT + reach) % total_tiles
    positions = owners[slot_place % number_partitions] * CAP
    targets = jnp.broadcast_to(ocean_tile, positions.shape)
    return (sending, jnp.stack([positions.reshape(-1), targets.reshape(-1)]).astype(jnp.int32))


def draw_send_tiles(key, part):
    return regrid_plan(key)[0]


def draw_regrid_slots(key, part):
    return regrid_plan(key)[1]


def draw_regrid_weights(key, part):
    key = jax.random.fold_in(key, 7)
    base = jax.random.uniform(key, (SLOTS, TA, PATCH_AREA_SIZE), jnp.float32)
    tile_weights = base / TA
    return tile_weights.astype(jnp.bfloat16)


def plant(drawn, stream_key, smallest, high):
    longest = drawn.shape.index(max(drawn.shape))
    spots = []
    for shift in (0, 1):
        where = [jax.random.randint(jax.random.fold_in(stream_key, axis), (), 0, length) for axis, length in enumerate(drawn.shape)]
        where[longest] = (where[longest] + shift) % drawn.shape[longest]
        spots.append(tuple(where))
    return drawn.at[spots[0]].set(smallest).at[spots[1]].set(high)


def level_of(key, dims, cuts, least, high):
    loudness, own = 1.0, jax.random.fold_in(key, 6)
    for dim, shards_of in cuts:
        steps = jnp.exp(jax.random.uniform(jax.random.fold_in(own, dim), (shards_of,), jnp.float32, least / len(cuts), high / len(cuts)))
        loudness = loudness * jnp.repeat(steps, dims[dim] // shards_of).reshape([-1 if axis == dim else 1 for axis in range(len(dims))])
    return loudness


def bell_draw(rng, shape, scale, most, pieces=(), kind=jnp.bfloat16):
    level = level_of(rng, shape, pieces, -0.22, 0.18) if pieces else 1.0
    result = jax.random.normal(rng, shape, jnp.float32) * scale * level
    return jnp.minimum(jnp.maximum(result, -most), most).astype(kind)


def setup_inputs(seed: int = 0, part: int = 0) -> dict:
    key_of = jax.random.split(jax.random.key(seed), 8)
    part_splits = jax.random.split(jax.random.fold_in(key_of[7], part), 8)
    return {
        "ocean_temp": bell_draw(part_splits[0], (LEV, NX, NY), 1.0, 6.0, ((0, 2), (1, 4), (2, 2)), jnp.float32),
        "bathy_levels": plant(jax.random.randint(part_splits[1], (NX, NY), 0, LEV + 1), jax.random.fold_in(part_splits[1], 1), 0, LEV).astype(jnp.int32),
        "mixing": jnp.clip(jnp.exp(math.log(0.3) - 2.7080503 * jax.random.uniform(part_splits[2], (NX, NY), jnp.float32) ** level_of(part_splits[2], (NX, NY), ((0, 4), (1, 2)), -0.2, 0.2)), 0.02, 0.3),
        "atm_flux": bell_draw(part_splits[3], (ATM_TILES, 2, TA), 1.0, 6.0, ((0, 8),)),
        "send_tiles": draw_send_tiles(jax.random.fold_in(key_of[7], 71), part),
        "regrid_slots": draw_regrid_slots(jax.random.fold_in(key_of[7], 71), part),
        "regrid_weights": draw_regrid_weights(jax.random.fold_in(key_of[7], 71), part),
    }


def wet_levels(levels_float, first_level, level_count):
    level_index = (first_level + jnp.arange(level_count)).astype(jnp.float32)[:, None, None]
    inside = (level_index >= 0.0) & (level_index < levels_float[None])
    return jnp.where(inside, 1.0, 0.0).astype(jnp.float32)


def level_forcing(surface, first_level, level_count, total_levels):
    level_index = (first_level + jnp.arange(level_count)).astype(jnp.float32)[:, None, None]
    top_only = jnp.where(level_index == 0.0, 1.0, 0.0).astype(jnp.float32)
    depth_share = jnp.exp(-4.0 * level_index / total_levels)
    return top_only * surface[0][None] + depth_share * surface[1][None]


def advance(padded_temp, padded_wet, mixing, forcing):
    center = padded_temp[1:-1, 1:-1, 1:-1]
    water_indicator = padded_wet[1:-1, 1:-1, 1:-1]
    lateral = (padded_temp[1:-1, 2:, 1:-1] - center) * padded_wet[1:-1, 2:, 1:-1]
    lateral = lateral + (padded_temp[1:-1, :-2, 1:-1] - center) * padded_wet[1:-1, :-2, 1:-1]
    lateral = lateral + (padded_temp[1:-1, 1:-1, 2:] - center) * padded_wet[1:-1, 1:-1, 2:]
    lateral = lateral + (padded_temp[1:-1, 1:-1, :-2] - center) * padded_wet[1:-1, 1:-1, :-2]
    vertical = (padded_temp[2:, 1:-1, 1:-1] - center) * padded_wet[2:, 1:-1, 1:-1]
    vertical = vertical + (padded_temp[:-2, 1:-1, 1:-1] - center) * padded_wet[:-2, 1:-1, 1:-1]
    return center + water_indicator * (0.1 * lateral + mixing * vertical + 0.1 * forcing)


def reference(ocean_temp, bathy_levels, mixing, atm_flux, send_tiles, regrid_slots, regrid_weights):
    number_partitions = N_GX * N_GY
    number_patches = NORTHSOUTH_SPAN * EASTWEST_SPAN // PATCH_AREA_SIZE

    def slot_info(marine_partition):
        listed = lax.dynamic_slice_in_dim(regrid_slots, marine_partition * K, K, 1)
        sender = listed[0] // CAP
        slot_cap = listed[0] % CAP
        src_tile = send_tiles[sender, marine_partition, slot_cap]
        is_live = src_tile >= 0
        flat_tile = (sender * AT + jnp.maximum(src_tile, 0)).astype(jnp.int32)
        weights_block = lax.dynamic_slice_in_dim(regrid_weights, marine_partition * K, K, 0)
        return listed[1], flat_tile, is_live, weights_block

    def forward(marine_partition):
        target_patch, flat_tile, is_live, weights_block = slot_info(marine_partition)
        flux_rows = atm_flux[flat_tile] * is_live[:, None, None].astype(jnp.bfloat16)
        contrib = jnp.einsum('kfa,kao->kfo', flux_rows.astype(jnp.float32), weights_block.astype(jnp.float32))
        collect = (target_patch[None, :] == jnp.arange(number_patches)[:, None]).astype(jnp.float32)
        summed = jnp.dot(collect, contrib.reshape(K, 2 * PATCH_AREA_SIZE), precision=lax.Precision.HIGHEST)
        return summed.reshape(number_patches, 2, PATCH_AREA_SIZE).transpose(1, 0, 2).reshape(2, NORTHSOUTH_SPAN, EASTWEST_SPAN)

    per_block = lax.map(forward, jnp.arange(number_partitions, dtype=jnp.int32))
    surface = per_block.reshape(N_GX, N_GY, 2, NORTHSOUTH_SPAN, EASTWEST_SPAN).transpose(2, 0, 3, 1, 4).reshape(2, NX, NY)
    levels_float = bathy_levels.astype(jnp.float32)
    water_indicator = wet_levels(levels_float, 0, LEV)
    forcing = level_forcing(surface, 0, LEV, LEV)
    padded_wet = jnp.pad(water_indicator, 1)
    current_reading = ocean_temp
    for section in range(STEPS):
        current_reading = advance(jnp.pad(current_reading, 1), padded_wet, mixing, forcing)
    skin_heat_grid = (current_reading[0] * water_indicator[0]).astype(jnp.bfloat16)
    skin_heat_partitions = skin_heat_grid.reshape(N_GX, NORTHSOUTH_SPAN, N_GY, EASTWEST_SPAN).transpose(0, 2, 1, 3).reshape(number_partitions, number_patches, PATCH_AREA_SIZE)

    def give_back(marine_partition, total_sum):
        target_patch, flat_tile, is_live, weights_block = slot_info(marine_partition)
        chosen_patch = skin_heat_partitions[marine_partition][target_patch]
        back = jnp.einsum('kao,ko->ka', weights_block.astype(jnp.float32), chosen_patch.astype(jnp.float32))
        back = back * is_live[:, None].astype(jnp.float32)
        return total_sum.at[flat_tile].add(back)

    start_sum = jnp.zeros((number_partitions * AT, TA), jnp.float32)
    atm_surface = lax.fori_loop(0, number_partitions, give_back, start_sum)
    return current_reading, atm_surface
```

```python
import functools

import jax
import jax.numpy as jnp
from jax import lax
from jax.experimental import pallas as pl
from jax.experimental.pallas import tpu as pltpu
from jax.sharding import PartitionSpec as P

STEPS = 4
HALO = STEPS
TOP = STEPS + 1
LANES = 128
GROUP = LANES // HALO
FEW = 16
BLOCKS_AXES = ("gx", "gy")
ALL_AXES = ("gx", "gy", "gz")
VMEM_LIMIT = 48 * 1024 * 1024


def side_tile(left, right, index):
    lane = lax.broadcasted_iota(jnp.int32, left.shape, 1)
    from_right = pltpu.roll(right, lax.rem(LANES - HALO * index, LANES), 1)
    from_left = pltpu.roll(left, lax.rem(2 * LANES - HALO - HALO * index, LANES), 1)
    zero = jnp.zeros_like(left)
    return jnp.where(lane < HALO, from_right, jnp.where(lane >= LANES - HALO, from_left, zero))


def put_slab(ref, own, after, before, tile):
    rows, columns = own.shape
    ref[0:rows, 0:columns] = own
    ref[rows : rows + HALO, 0:columns] = after
    ref[rows + HALO : rows + 2 * HALO, 0:columns] = before
    ref[:, columns:] = tile


def neighbour_levels(levels):
    rows, lanes = levels.shape
    return (
        pltpu.roll(levels, 1, 0),
        pltpu.roll(levels, rows - 1, 0),
        pltpu.roll(levels, 1, 1),
        pltpu.roll(levels, lanes - 1, 1),
    )


def keep_share(levels_ref, around_ref, mixing_ref, level):
    wet_around = jnp.where(around_ref[0] > level, 0.1, 0.0)
    for side in range(1, 4):
        wet_around = wet_around + jnp.where(around_ref[side] > level, 0.1, 0.0)
    above = jnp.where(level > 0.0, 1.0, 0.0)
    vertical = above + jnp.where(levels_ref[...] > level + 1.0, 1.0, 0.0)
    return 1.0 - wet_around - mixing_ref[...] * vertical


def step_slab(center, over, under, keep, mixing, levels, level, forcing):
    rows, lanes = center.shape
    lateral = pltpu.roll(center, 1, 0) + pltpu.roll(center, rows - 1, 0)
    lateral = lateral + (pltpu.roll(center, 1, 1) + pltpu.roll(center, lanes - 1, 1))
    new = center * keep + 0.1 * (lateral + forcing) + mixing * (over + under)
    return jnp.where(levels > level, new, 0.0)


def prepare(bathy_ref, mixing_ref, next_ref, prev_ref, left_ref, right_ref, info_ref, fields, levels_ref, mix_ref, around_ref):
    rows, columns = bathy_ref.shape
    size = rows + 2 * HALO
    lane = lax.broadcasted_iota(jnp.int32, (size, LANES), 1)
    tile = side_tile(left_ref[1], right_ref[1], fields % GROUP)
    tile = jnp.where((lane < HALO) & (info_ref[2] == 0), 0.0, tile)
    tile = jnp.where((lane >= LANES - HALO) & (info_ref[1] == 0), 0.0, tile)
    put_slab(levels_ref, bathy_ref[...].astype(jnp.float32), next_ref[fields], prev_ref[fields], tile)
    tile = side_tile(left_ref[1], right_ref[1], (fields + 1) % GROUP)
    put_slab(mix_ref, mixing_ref[...], next_ref[fields + 1], prev_ref[fields + 1], tile)
    for side, values in enumerate(neighbour_levels(levels_ref[...])):
        around_ref[side] = values


def skin_kernel(
    info_ref, temp_ref, shared_ref, bathy_ref, mixing_ref, next_ref, prev_ref, left_ref, right_ref, surface_ref,
    skin_ref, first_ref, second_ref, keep_ref, levels_ref, mix_ref, around_ref, *, total_levels,
):
    layers = temp_ref.shape[0]
    fields = layers + shared_ref.shape[0]
    prepare(bathy_ref, mixing_ref, next_ref, prev_ref, left_ref, right_ref, info_ref, fields, levels_ref, mix_ref, around_ref)
    gz = info_ref[0]
    shift = gz * layers
    levels = levels_ref[...]
    for level in range(TOP):
        slot = level + shift
        own = jnp.where(gz == 0, temp_ref[level], shared_ref[level])
        tile = side_tile(left_ref[gz], right_ref[gz], level)
        put_slab(first_ref.at[level], own, next_ref[slot], prev_ref[slot], tile)
        first_ref[level] = jnp.where(levels > float(level), first_ref[level], 0.0)
        if level < STEPS:
            keep_ref[level] = keep_share(levels_ref, around_ref, mix_ref, jnp.float32(level))
    zero = jnp.zeros_like(levels)
    source, target = first_ref, second_ref
    for step in range(1, STEPS + 1):
        for level in range(TOP - step):
            depth_share = jnp.exp(jnp.full((1, 1), -4.0 * level / total_levels, jnp.float32))
            forcing = depth_share * surface_ref[1]
            if level == 0:
                forcing = forcing + surface_ref[0]
            over = source[level - 1] if level else zero
            target[level] = step_slab(
                source[level], over, source[level + 1], keep_ref[level], mix_ref[...], levels, float(level), forcing
            )
        source, target = target, source
    rows, columns = bathy_ref.shape
    skin_ref[...] = source[0, 0:rows, 0:columns].astype(jnp.bfloat16)


def ocean_kernel(
    info_ref, temp_ref, shared_ref, bathy_ref, mixing_ref, next_ref, prev_ref, left_ref, right_ref, surface_ref,
    ocean_ref, first_ref, second_ref, keep_ref, levels_ref, mix_ref, around_ref, *, total_levels,
):
    layers, rows, columns = temp_ref.shape
    fields = layers + shared_ref.shape[0]
    prepare(bathy_ref, mixing_ref, next_ref, prev_ref, left_ref, right_ref, info_ref, fields, levels_ref, mix_ref, around_ref)
    gz = info_ref[0]
    first_level = gz * layers - HALO

    def level_of(place):
        return (first_level + place).astype(jnp.float32)

    def settle(place):
        level = level_of(place)
        first_ref[place] = jnp.where(levels_ref[...] > level, first_ref[place], 0.0)
        keep_ref[place] = keep_share(levels_ref, around_ref, mix_ref, level)

    def own_level(index, carry):
        tile = side_tile(left_ref[0], right_ref[0], index)
        put_slab(first_ref.at[index + HALO], temp_ref[index], next_ref[index], prev_ref[index], tile)
        settle(index + HALO)
        return carry

    lax.fori_loop(0, layers, own_level, 0)

    def shared_level(index, carry):
        slot = jnp.where(gz == 0, index, TOP + index)
        place = jnp.where(gz == 0, HALO + layers + index, index)
        tile = side_tile(left_ref[1], right_ref[1], slot)
        put_slab(first_ref.at[place], shared_ref[slot], next_ref[layers + slot], prev_ref[layers + slot], tile)
        settle(place)
        return carry

    lax.fori_loop(0, HALO, shared_level, 0)
    edge = jnp.where(gz == 0, HALO - 1, HALO + layers)
    first_ref[edge] = jnp.zeros_like(first_ref[0])
    second_ref[edge] = jnp.zeros_like(first_ref[0])
    source, target = first_ref, second_ref
    for step in range(1, STEPS + 1):
        base = jnp.where(gz == 0, HALO, step)

        def one(index, carry, source=source, target=target, base=base):
            place = base + index
            level = level_of(place)
            depth_share = jnp.exp(jnp.full((1, 1), -4.0 / total_levels, jnp.float32) * level)
            target[place] = step_slab(
                source[place], source[place - 1], source[place + 1], keep_ref[place], mix_ref[...], levels_ref[...],
                level, depth_share * surface_ref[1],
            )
            return carry

        lax.fori_loop(0, layers + HALO - step, one, 0)

        @pl.when(gz == 0)
        def _(target=target):
            target[HALO] = target[HALO] + jnp.where(levels_ref[...] > 0.0, 0.1 * surface_ref[0], 0.0)

        source, target = target, source

    def write(index, carry):
        wet = levels_ref[0:rows, 0:columns] > level_of(index + HALO)
        ocean_ref[index] = jnp.where(wet, source[index + HALO, 0:rows, 0:columns], temp_ref[index])
        return carry

    lax.fori_loop(0, layers, write, 0)


def pack_kernel(side_ref, temp_ref, shared_ref, bathy_ref, mixing_ref, next_ref, prev_ref, packed_ref):
    layers, rows, columns = temp_ref.shape
    shared = shared_ref.shape[0]
    right = side_ref[0]
    start = pl.multiple_of(right * (columns - LANES), LANES)
    base = jnp.where(right == 1, HALO, 0)
    window = pl.ds(start, LANES)
    lane = lax.broadcasted_iota(jnp.int32, (rows + 2 * HALO, LANES), 1)

    def add(carry, index, own, slot):
        slab = jnp.concatenate([own, next_ref[slot, :, window], prev_ref[slot, :, window]], axis=0)
        place = index * HALO
        moved = pltpu.roll(slab, lax.rem(place + base, LANES), 1)
        return jnp.where((lane >= place) & (lane < place + HALO), moved, carry)

    packed_ref[0] = lax.fori_loop(
        0, layers, lambda i, c: add(c, i, temp_ref[i, :, window], i), jnp.zeros(lane.shape, jnp.float32)
    )
    second = lax.fori_loop(
        0, shared, lambda i, c: add(c, i, shared_ref[i, :, window], layers + i), jnp.zeros(lane.shape, jnp.float32)
    )
    second = add(second, shared, bathy_ref[:, window].astype(jnp.float32), layers + shared)
    packed_ref[1] = add(second, shared + 1, mixing_ref[:, window], layers + shared + 1)


def vmem_call(body, out_shape, scratch=(), arguments=1, **options):
    vmem = pl.BlockSpec(memory_space=pltpu.VMEM)
    return pl.pallas_call(
        body,
        out_shape=out_shape,
        in_specs=[pl.BlockSpec(memory_space=pltpu.SMEM)] + [vmem] * arguments,
        out_specs=vmem,
        scratch_shapes=list(scratch),
        compiler_params=pltpu.CompilerParams(vmem_limit_bytes=VMEM_LIMIT),
        **options,
    )


def line(count):
    forward = [(i, i + 1) for i in range(count - 1)]
    return forward, [(target, source) for source, target in forward]


def outgoing_tiles(my_sends, atm_flux):
    own_tiles = atm_flux.shape[0]
    chooser = (my_sends.reshape(-1)[:, None] == jnp.arange(own_tiles)[None, :]).astype(jnp.bfloat16)
    flat_flux = atm_flux.reshape(own_tiles, atm_flux.shape[1] * atm_flux.shape[2])
    return jnp.dot(chooser, flat_flux, preferred_element_type=jnp.float32).astype(jnp.bfloat16)


def edge_frame(surface, after, before, left, right):
    fields, rows, columns = surface.shape
    width = STEPS - 1
    gap = jnp.zeros((fields, HALO - width, columns), jnp.float32)
    body = jnp.concatenate([surface, after, gap, gap, before], axis=1)
    middle = jnp.zeros((fields, rows + 2 * HALO, LANES - 2 * width), jnp.float32)
    return jnp.concatenate([body, right, middle, left], axis=2)


def frame_rows(own, after, before):
    gap = jnp.zeros(own.shape[:1] + (HALO - after.shape[1],) + own.shape[2:], jnp.float32)
    return jnp.concatenate([own, after, gap, gap, before], axis=1)


def surface_frame_few(surface, gx_count, gy_count):
    fields, rows, columns = surface.shape
    width = STEPS - 1
    gx, gy = lax.axis_index("gx"), lax.axis_index("gy")
    block = jnp.arange(gx_count * gy_count)
    dx, dy = block // gy_count - gx, block % gy_count - gy
    columns_low = jnp.pad(surface[:, :, :width].transpose(0, 2, 1), ((0, 0), (0, 0), (0, columns - rows)))
    columns_high = jnp.pad(surface[:, :, -width:].transpose(0, 2, 1), ((0, 0), (0, 0), (0, columns - rows)))
    strips = jnp.stack([surface[:, :width], surface[:, -width:], columns_low, columns_high])
    choice = jnp.where(dx < 0, 0, jnp.where(dx > 0, 1, jnp.where(dy < 0, 2, 3)))
    message = strips[choice]
    got = lax.all_to_all(message, BLOCKS_AXES, split_axis=0, concat_axis=0, tiled=True)

    def of(x, y):
        index = jnp.clip(x, 0, gx_count - 1) * gy_count + jnp.clip(y, 0, gy_count - 1)
        return lax.dynamic_index_in_dim(got, index, 0, keepdims=False)

    after, before = of(gx + 1, gy), of(gx - 1, gy)
    right = frame_rows(
        of(gx, gy + 1)[:, :, :rows].transpose(0, 2, 1),
        of(gx + 1, gy + 1)[:, :, :width],
        of(gx - 1, gy + 1)[:, :, :width],
    )
    left = frame_rows(
        of(gx, gy - 1)[:, :, :rows].transpose(0, 2, 1),
        of(gx + 1, gy - 1)[:, :, -width:],
        of(gx - 1, gy - 1)[:, :, -width:],
    )
    return edge_frame(surface, after, before, left, right)


def surface_frame_many(surface, gx_count, gy_count):
    width = STEPS - 1
    forward, backward = line(gx_count)
    before = lax.ppermute(surface[:, -width:], "gx", forward)
    after = lax.ppermute(surface[:, :width], "gx", backward)
    forward, backward = line(gy_count)
    low, high = surface[:, :, :width], surface[:, :, -width:]
    left = lax.ppermute(
        frame_rows(high, after[:, :, -width:], before[:, :, -width:]).transpose(0, 2, 1), "gy", forward
    )
    right = lax.ppermute(
        frame_rows(low, after[:, :, :width], before[:, :, :width]).transpose(0, 2, 1), "gy", backward
    )
    return edge_frame(surface, after, before, left.transpose(0, 2, 1), right.transpose(0, 2, 1))


def per_device(
    ocean_temp, bathy_levels, mixing, atm_flux, send_tiles, regrid_slots, regrid_weights
):
    layers, row_count, columns = ocean_temp.shape
    gx_count, gy_count, gz_count = (lax.axis_size(axis) for axis in ALL_AXES)
    assert gz_count == 2 and layers == GROUP
    total_levels = layers * gz_count
    number_partitions = gx_count * gy_count
    gx, gy, gz = (lax.axis_index(axis) for axis in ALL_AXES)
    self_block = gx * gy_count + gy
    own_tiles, fields, tile_atm = atm_flux.shape
    caps = send_tiles.shape[2]
    slot_count, unused_rows, patch_marine = regrid_weights.shape
    number_patches = row_count * columns // patch_marine
    position = regrid_slots[0]
    target_patch = regrid_slots[1]
    my_sends = send_tiles[self_block]

    edge_levels = jnp.concatenate([ocean_temp[:TOP], ocean_temp[layers - HALO :]])
    shared = lax.ppermute(edge_levels, "gz", [(0, 1), (1, 0)])
    levels_float = bathy_levels.astype(jnp.float32)

    def strip(low):
        part = slice(0, HALO) if low else slice(row_count - HALO, row_count)
        return jnp.concatenate(
            [ocean_temp[:, part], shared[:, part], levels_float[None, part], mixing[None, part]]
        )

    forward, backward = line(gx_count)
    before_rows = lax.ppermute(strip(False), "gx", forward)
    after_rows = lax.ppermute(strip(True), "gx", backward)
    padded_rows = row_count + 2 * HALO
    lanes = columns + LANES

    def packed(right_side):
        return vmem_call(
            pack_kernel, jax.ShapeDtypeStruct((2, padded_rows, LANES), jnp.float32), arguments=6
        )(right_side.reshape(1), ocean_temp, shared, bathy_levels, mixing, after_rows, before_rows)

    if gy_count == 2 and FEW:
        from_left = from_right = lax.ppermute(packed(1 - gy), "gy", [(0, 1), (1, 0)])
    else:
        forward, backward = line(gy_count)
        one = jnp.int32(1)
        from_left = lax.ppermute(packed(one), "gy", forward)
        from_right = lax.ppermute(packed(one - 1), "gy", backward)

    outgoing = outgoing_tiles(my_sends, atm_flux).reshape(
        number_partitions, caps, fields * tile_atm
    )
    incoming = lax.all_to_all(outgoing, BLOCKS_AXES, split_axis=0, concat_axis=0, tiled=True)
    picked = incoming.reshape(number_partitions * caps, fields, tile_atm)[position]
    contrib = jnp.einsum("kfa,kao->kfo", picked, regrid_weights, preferred_element_type=jnp.float32)
    collect = (target_patch[None, :] == jnp.arange(number_patches)[:, None]).astype(jnp.float32)
    summed = jnp.dot(
        collect, contrib.reshape(slot_count, fields * patch_marine), precision=lax.Precision.HIGHEST
    )
    partial_surface = (
        summed.reshape(number_patches, fields, patch_marine)
        .transpose(1, 0, 2)
        .reshape(fields, row_count, columns)
    )
    surface = partial_surface + lax.ppermute(partial_surface, "gz", [(0, 1), (1, 0)])
    few = number_partitions <= FEW
    surface = (surface_frame_few if few else surface_frame_many)(surface, gx_count, gy_count)

    info = jnp.stack([gz, (gy > 0).astype(jnp.int32), (gy < gy_count - 1).astype(jnp.int32)])
    operands = (
        info, ocean_temp, shared, bathy_levels, mixing, after_rows, before_rows, from_left, from_right, surface,
    )
    slab = (padded_rows, lanes)
    flat = [pltpu.VMEM(slab, jnp.float32), pltpu.VMEM(slab, jnp.float32), pltpu.VMEM((4,) + slab, jnp.float32)]
    top_scratch = [pltpu.VMEM((TOP,) + slab, jnp.float32)] * 3 + flat
    skin = vmem_call(
        functools.partial(skin_kernel, total_levels=total_levels),
        jax.ShapeDtypeStruct((row_count, columns), jnp.bfloat16), top_scratch, arguments=9,
        cost_estimate=pl.CostEstimate(flops=10 * 20 * padded_rows * lanes, bytes_accessed=1 << 21, transcendentals=0),
    )(*operands)
    full_scratch = [pltpu.VMEM((layers + 2 * HALO,) + slab, jnp.float32)] * 3 + flat
    ocean = vmem_call(
        functools.partial(ocean_kernel, total_levels=total_levels),
        jax.ShapeDtypeStruct(ocean_temp.shape, jnp.float32), full_scratch, arguments=9,
        cost_estimate=pl.CostEstimate(
            flops=140 * 20 * padded_rows * lanes, bytes_accessed=1 << 24, transcendentals=0
        ),
    )(*operands)

    chosen_patch = skin.reshape(number_patches, patch_marine)[target_patch]
    back = jnp.einsum(
        "kao,ko->ka", regrid_weights, chosen_patch, preferred_element_type=jnp.float32
    )
    placer = (jnp.arange(number_partitions * caps)[:, None] == position[None, :]).astype(
        jnp.float32
    )
    buffer = jnp.dot(placer, back, precision=lax.Precision.HIGHEST).reshape(
        number_partitions, 1, caps * tile_atm
    )
    buffer = jnp.broadcast_to(buffer, (number_partitions, gz_count, caps * tile_atm)).reshape(
        number_partitions * gz_count, caps * tile_atm
    )
    returned = lax.all_to_all(buffer, ALL_AXES, split_axis=0, concat_axis=0, tiled=True)
    sends = jnp.broadcast_to(my_sends[:, None], (number_partitions, gz_count, caps)).reshape(-1)
    gatherer = (jnp.arange(own_tiles)[:, None] == sends[None, :]).astype(jnp.float32)
    atm_surface = jnp.dot(
        gatherer, returned.reshape(-1, tile_atm), precision=lax.Precision.HIGHEST
    )
    return (ocean, atm_surface)


def solution(mesh):
    return jax.shard_map(
        per_device,
        mesh=mesh,
        in_specs=(
            P(("ens", "gz"), "gx", "gy"),
            P(("ens", "gx"), "gy"),
            P(("ens", "gx"), "gy"),
            P(("ens", "gx", "gy"), None, None),
            P(),
            P(None, ("gx", "gy", "gz")),
            P(("gx", "gy", "gz"), None, None),
        ),
        out_specs=(P(("ens", "gz"), "gx", "gy"), P(("ens", "gx", "gy"), None)),
        check_vma=False,
    )
```

```python
import functools

import jax
import jax.numpy as jnp
from jax import lax
from jax.experimental import pallas as pl
from jax.experimental.pallas import tpu as pltpu
from jax.sharding import PartitionSpec as P

STEPS = 4
HALO = STEPS
WIDTH = STEPS - 1
TOP = STEPS + 1
LANES = 128
TILE = 8
GROUP = LANES // HALO
FEW = 16
UNROLL = 8
CHUNKS = 4
BLOCKS_AXES = ("gx", "gy")
ALL_AXES = ("gx", "gy", "gz")
VMEM_LIMIT = 24 * 1024 * 1024


def position_of(few, dx, dy):
    if not few:
        return (dx + 1) * 2 + (1 if dy > 0 else 0)
    gx_count, gy_count = lax.axis_size("gx"), lax.axis_size("gy")
    x = jnp.clip(lax.axis_index("gx") + dx, 0, gx_count - 1)
    y = jnp.clip(lax.axis_index("gy") + dy, 0, gy_count - 1)
    return x * gy_count + y


def side_tile(left, right, index):
    lane = lax.broadcasted_iota(jnp.int32, left.shape, 1)
    from_right = pltpu.roll(right, lax.rem(LANES - HALO * index, LANES), 1)
    from_left = pltpu.roll(left, lax.rem(2 * LANES - HALO - HALO * index, LANES), 1)
    zero = jnp.zeros_like(left)
    return jnp.where(lane < HALO, from_right, jnp.where(lane >= LANES - HALO, from_left, zero))


def put_slab(ref, own, after, before, tile):
    rows, columns = own.shape
    ref[0:rows, 0:columns] = own
    ref[rows : rows + HALO, 0:columns] = after
    ref[rows + HALO : rows + 2 * HALO, 0:columns] = before
    ref[:, columns:] = tile


def wet_around(levels, level):
    rows, lanes = levels.shape
    wet = jnp.where(levels > level, 0.1, 0.0)
    total = pltpu.roll(wet, 1, 0) + pltpu.roll(wet, rows - 1, 0)
    return total + (pltpu.roll(wet, 1, 1) + pltpu.roll(wet, lanes - 1, 1))


def keep_share(levels, mixing, level):
    above = jnp.where(level > 0.0, 1.0, 0.0)
    vertical = above + jnp.where(levels > level + 1.0, 1.0, 0.0)
    return 1.0 - wet_around(levels, level) - mixing * vertical


def step_slab(center, over, under, keep, mixing, levels, level, forcing):
    rows, lanes = center.shape
    lateral = pltpu.roll(center, 1, 0) + pltpu.roll(center, rows - 1, 0)
    lateral = lateral + (pltpu.roll(center, 1, 1) + pltpu.roll(center, lanes - 1, 1))
    if forcing is not None:
        lateral = lateral + forcing
    new = center * keep + 0.1 * lateral + mixing * (over + under)
    return jnp.where(levels > level, new, 0.0)


def depth_share(level, total_levels):
    return jnp.exp(jnp.full((1, 1), -4.0 / total_levels, jnp.float32) * level)


def begin(copies, semaphores, first=0):
    started = []
    for index, (source, target) in enumerate(copies):
        copy = pltpu.make_async_copy(source, target, semaphores.at[first + index])
        copy.start()
        started.append(copy)
    return started


def finish(copies):
    for copy in copies:
        copy.wait()


def in_order(start, count, body):
    whole = count // UNROLL

    def group(index, carry):
        for offset in range(UNROLL):
            body(start + index * UNROLL + offset)
        return carry

    lax.fori_loop(0, whole, group, 0)
    for index in range(whole * UNROLL, count):
        body(start + index)


def rows_kernel(temp_ref, bathy_ref, mixing_ref, low_ref, high_ref, temp_rows, bathy_rows, mixing_rows, semaphores):
    layers, rows, columns = temp_ref.shape
    copies = []
    for side in range(2):
        part = pl.ds(side * (rows - TILE), TILE)
        copies += [(temp_ref.at[:, part], temp_rows.at[side]), (bathy_ref.at[part], bathy_rows.at[side])]
        copies += [(mixing_ref.at[part], mixing_rows.at[side])]
    finish(begin(copies, semaphores))
    for side, (out_ref, part) in enumerate(((low_ref, slice(0, HALO)), (high_ref, slice(TILE - HALO, TILE)))):
        out_ref[0:layers] = temp_rows[side, :, part]
        out_ref[layers] = bathy_rows[side, part].astype(jnp.float32)
        out_ref[layers + 1] = mixing_rows[side, part]


def send_kernel(sends_hbm, flux_hbm, temp_hbm, bathy_hbm, mixing_hbm, after_ref, *refs, few, sides):
    if few:
        message_ref, sends_ref, flux_ref, temp_ref, bathy_ref, mixing_ref, semaphores, flux_scratch, strips_ref = refs
        fluxes_ref = message_ref
    else:
        (
            fluxes_ref, strips_ref, sends_ref, flux_ref, temp_ref, bathy_ref, mixing_ref, semaphores, flux_scratch,
        ) = refs
    layers, rows, columns = temp_hbm.shape
    gy, gy_count = lax.axis_index("gy"), lax.axis_size("gy")
    me = lax.axis_index("gx") * gy_count + gy
    copies = [(sends_hbm, sends_ref), (flux_hbm, flux_ref)]
    for place in range(sides):
        side = 1 - gy if sides == 1 else place
        window = pl.ds(pl.multiple_of(side * (columns - LANES), LANES), LANES)
        copies += [(bathy_hbm.at[:, window], bathy_ref.at[place]), (mixing_hbm.at[:, window], mixing_ref.at[place])]
        copies += [(temp_hbm.at[:, :, window], temp_ref.at[place])]
    copies = begin(copies, semaphores)
    lane = lax.broadcasted_iota(jnp.int32, (rows, LANES), 1)
    short = lax.broadcasted_iota(jnp.int32, (TILE, LANES), 1)
    finish(copies)
    for side in range(sides):
        base = HALO * (1 - gy) if sides == 1 else HALO * side
        strip = jnp.zeros((rows, LANES), jnp.float32)
        for index in range(layers):
            place = HALO * index
            moved = pltpu.roll(temp_ref[side, index], lax.rem(place + base, LANES), 1)
            strip = jnp.where((lane >= place) & (lane < place + HALO), moved, strip)
        strips_ref[side, 2 * TILE : 2 * TILE + rows] = strip
        plain = jnp.zeros((TILE, LANES), jnp.float32)
        for part in range(rows // TILE):
            here = slice(part * TILE, (part + 1) * TILE)
            for which, values in enumerate((bathy_ref[side, here].astype(jnp.float32), mixing_ref[side, here])):
                place = 2 * HALO * part + HALO * which
                moved = pltpu.roll(values, lax.rem(place + base, LANES), 1)
                plain = jnp.where((short >= place) & (short < place + HALO), moved, plain)
        strips_ref[side, TILE : 2 * TILE] = plain
        strips_ref[side, 0:TILE] = jnp.zeros((TILE, LANES), jnp.float32)
    flux_scratch[...] = flux_ref[...].astype(jnp.float32)
    fields = flux_ref.shape[1]

    def one(block, carry):
        tile = sends_ref[me, block]
        if few:
            side = 0 if sides == 1 else (lax.rem(block, gy_count) > gy).astype(jnp.int32)
            message_ref[block] = strips_ref[side]
        else:
            fluxes_ref[block] = jnp.zeros(fluxes_ref.shape[1:], jnp.float32)
        sent = jnp.where(tile >= 0, flux_scratch[jnp.maximum(tile, 0)], 0.0)
        fluxes_ref[block, 0:fields] = sent
        return carry

    if few:
        for block in range(fluxes_ref.shape[0]):
            one(block, 0)
    else:
        lax.fori_loop(0, fluxes_ref.shape[0], one, 0)


def regrid_kernel(slots_hbm, *refs, few):
    if few:
        sides_ref, *refs = refs
        flux_ref = sides_ref
    else:
        flux_ref, sides_ref, *refs = refs
    (
        weights_hbm, temp_hbm, bathy_hbm, mixing_hbm, next_ref, prev_ref,
        partial_ref, edges_ref, shared_ref, levels_hbm, mix_hbm, packed_hbm,
        slots_ref, weights_ref, temp_ref, bathy_ref, mixing_ref, levels_ref, mix_ref, packed_ref, semaphores,
        sums_ref, *strip_scratch,
    ) = refs
    layers, rows, columns = temp_hbm.shape
    slot_count, tile_atm, patch = weights_ref.shape
    halves = columns // LANES
    lasts = pl.ds(layers - HALO, HALO)
    needed = begin([
        (temp_hbm.at[pl.ds(0, TOP)], temp_ref.at[pl.ds(0, TOP)]), (temp_hbm.at[lasts], temp_ref.at[pl.ds(TOP, HALO)]),
        (bathy_hbm, bathy_ref), (mixing_hbm, mixing_ref), (slots_hbm, slots_ref),
    ], semaphores)
    chunk = slot_count // CHUNKS
    arriving = begin([
        (weights_hbm.at[pl.ds(part * chunk, chunk)], weights_ref.at[pl.ds(part * chunk, chunk)])
        for part in range(CHUNKS)
    ], semaphores, len(needed))
    sums_ref[...] = jnp.zeros_like(sums_ref)

    gx, gx_count = lax.axis_index("gx"), lax.axis_size("gx")
    gy, gy_count = lax.axis_index("gy"), lax.axis_size("gy")
    plain = []
    for side, dy in ((0, -1), (1, 1)):
        own, after, before = (position_of(few, dx, dy) for dx in (0, 1, -1))
        packed_ref[side, 0:rows] = sides_ref[own, 2 * TILE : 2 * TILE + rows]
        packed_ref[side, rows : rows + HALO] = sides_ref[after, 2 * TILE : 2 * TILE + HALO]
        packed_ref[side, rows + HALO :] = sides_ref[before, 2 * TILE + rows - HALO : 2 * TILE + rows]
        tile = sides_ref[own, TILE : 2 * TILE]
        parts = [tile] + [pltpu.roll(tile, LANES - 2 * HALO * part, 1) for part in range(1, rows // TILE)]
        last = pltpu.roll(sides_ref[before, TILE : 2 * TILE], LANES - 2 * HALO * (rows // TILE - 1), 1)
        row = lax.broadcasted_iota(jnp.int32, (TILE, LANES), 0)
        parts.append(jnp.where(row < HALO, sides_ref[after, TILE : 2 * TILE], last))
        plain.append(jnp.concatenate(parts, axis=0))
    finish(needed)
    size = (rows + 2 * HALO, LANES)
    lane, row = (lax.broadcasted_iota(jnp.int32, size, dim) for dim in (1, 0))
    there = (lane < HALO) & (gy < gy_count - 1) | (lane >= HALO) & (gy > 0)
    there = there & ((row < rows) | (row < rows + HALO) & (gx < gx_count - 1) | (row >= rows + HALO) & (gx > 0))
    tile = jnp.where(there, side_tile(plain[0], plain[1], 0), 0.0)
    put_slab(levels_ref, bathy_ref[...].astype(jnp.float32), next_ref[layers], prev_ref[layers], tile)
    tile = side_tile(plain[0], plain[1], 1)
    put_slab(mix_ref, mixing_ref[...], next_ref[layers + 1], prev_ref[layers + 1], tile)
    for place, level in enumerate(list(range(TOP)) + list(range(layers - HALO, layers))):
        tile = side_tile(packed_ref[0], packed_ref[1], level)
        put_slab(shared_ref.at[place], temp_ref[place], next_ref[level], prev_ref[level], tile)
    leaving = begin(
        [(levels_ref, levels_hbm), (mix_ref, mix_hbm), (packed_ref, packed_hbm)], semaphores, len(needed) + CHUNKS
    )
    for slot in range(slot_count):
        if slot % chunk == 0:
            arriving[slot // chunk].wait()
        fluxes = flux_ref[slots_ref[0, slot], 0:TILE, :].astype(jnp.bfloat16)
        got = jnp.dot(fluxes, weights_ref[slot], preferred_element_type=jnp.float32)
        place = pl.multiple_of(slots_ref[1, slot] * TILE, TILE)
        sums_ref[pl.ds(place, TILE)] += got

    strips_ref = strip_scratch[0] if few else edges_ref
    strips_ref[...] = jnp.zeros_like(strips_ref)
    short = lax.broadcasted_iota(jnp.int32, (TILE, LANES), 1)
    columns_low = jnp.zeros((TILE, LANES), jnp.float32)
    columns_high = jnp.zeros((TILE, LANES), jnp.float32)
    for field in range(2):
        for half in range(halves):
            values = sums_ref[pl.ds(half * TILE + field, rows, stride=halves * TILE), :]
            partial_ref[field, :, half * LANES : (half + 1) * LANES] = values
            place = (field * 2 + half) * HALO
            strips_ref[0, place : place + WIDTH] = values[0:WIDTH]
            strips_ref[1, place : place + WIDTH] = values[rows - WIDTH : rows]
            for part in range(rows // TILE):
                block = values[part * TILE : (part + 1) * TILE]
                place = 2 * HALO * part + HALO * field
                inside = (short >= place) & (short < place + HALO)
                if half == 0:
                    columns_low = jnp.where(inside, pltpu.roll(block, place % LANES, 1), columns_low)
                if half == halves - 1:
                    columns_high = jnp.where(inside, pltpu.roll(block, (place + HALO) % LANES, 1), columns_high)
    strips_ref[2, 0:TILE] = columns_low
    strips_ref[3, 0:TILE] = columns_high
    if few:
        gx, gy, gy_count = lax.axis_index("gx"), lax.axis_index("gy"), lax.axis_size("gy")
        for entry in range(edges_ref.shape[0]):
            x, y = entry // 2 // gy_count, entry // 2 % gy_count
            choice = jnp.where(x < gx, 0, jnp.where(x > gx, 1, jnp.where(y < gy, 2, 3)))
            edges_ref[entry] = strips_ref[choice]

    finish(leaving)


def first_kernel(
    temp_hbm, next_hbm, prev_hbm, packed_hbm, other_hbm, levels_hbm, mix_hbm,
    moved_hbm, keep_hbm, top_hbm, top_keep_hbm,
    temp_ref, next_ref, prev_ref, packed_ref, other_ref, levels_ref, mix_ref,
    moved_ref, keep_ref, top_ref, top_keep_ref, first_ref, skin_ref, semaphores,
):
    layers = temp_hbm.shape[0]
    gz = lax.axis_index("gz")
    first_level = gz * layers - HALO
    needed = begin([
        (next_hbm, next_ref), (prev_hbm, prev_ref), (packed_hbm, packed_ref), (levels_hbm, levels_ref),
        (mix_hbm, mix_ref), (other_hbm, other_ref),
    ], semaphores)
    chunk = layers // CHUNKS
    parts = [pl.ds(part * chunk, chunk) for part in range(CHUNKS)]
    used = len(needed)
    arriving = begin([(temp_hbm.at[part], temp_ref.at[part]) for part in parts], semaphores, used)
    used += CHUNKS
    finish(needed)

    def level_of(place):
        return (first_level + place).astype(jnp.float32)

    def settle(place):
        level = level_of(place)
        first_ref[place] = jnp.where(levels_ref[...] > level, first_ref[place], 0.0)
        keep_ref[place] = keep_share(levels_ref[...], mix_ref[...], level)

    def own_level(index):
        tile = side_tile(packed_ref[0], packed_ref[1], index)
        put_slab(first_ref.at[index + HALO], temp_ref[index], next_ref[index], prev_ref[index], tile)
        settle(index + HALO)

    for part in range(CHUNKS):
        arriving[part].wait()
        in_order(part * chunk, chunk, own_level)

    for index in range(HALO):
        slot = jnp.where(gz == 0, index, TOP + index)
        place = jnp.where(gz == 0, HALO + layers + index, index)
        first_ref[place] = other_ref[slot]
        settle(place)

    base = jnp.where(gz == 0, HALO, 1)
    count = layers + HALO - 1
    span = pl.ds(base, count)
    leaving = begin([(keep_ref.at[span], keep_hbm.at[span])], semaphores, used)
    used += 1
    levels = levels_ref[...]
    for level in range(TOP):
        slab = jnp.where(gz == 0, first_ref[HALO + level], other_ref[level])
        skin_ref[level] = jnp.where(levels > float(level), slab, 0.0)
    for level in range(STEPS):
        top_keep_ref[level] = keep_share(levels, mix_ref[...], jnp.float32(level))
        over = skin_ref[level - 1] if level else jnp.zeros_like(levels)
        top_ref[level] = step_slab(
            skin_ref[level], over, skin_ref[level + 1], top_keep_ref[level], mix_ref[...], levels, float(level), None
        )
    leaving += begin([(top_ref, top_hbm), (top_keep_ref, top_keep_hbm)], semaphores, used)
    used += 2
    edge = jnp.where(gz == 0, HALO - 1, HALO + layers)
    first_ref[edge] = jnp.zeros_like(first_ref[0])

    def one(place):
        moved_ref[place] = step_slab(
            first_ref[place], first_ref[place - 1], first_ref[place + 1], keep_ref[place], mix_ref[...],
            levels_ref[...], level_of(place), None,
        )

    for start, size in pieces(count):
        in_order(base + start, size, one)
        here = pl.ds(base + start, size)
        leaving += begin([(moved_ref.at[here], moved_hbm.at[here])], semaphores, used)
        used += 1
    finish(leaving)


def pieces(count):
    return [(start, min(UNROLL, count - start)) for start in range(0, count, UNROLL)]


def skin_kernel(
    slots_hbm, partial_hbm, other_hbm, edges_ref, weights_hbm, levels_hbm, mix_hbm, top_hbm, top_keep_hbm,
    surface_hbm, back_ref,
    slots_ref, partial_ref, other_ref, weights_ref, levels_ref, mix_ref, top_ref, top_keep_ref, surface_ref, semaphores,
    first_ref, second_ref, sst_ref, rows_ref, *sums_scratch, few, total_levels,
):
    fields, rows, columns = partial_ref.shape
    slot_count, tile_atm, patch = weights_ref.shape
    halves = columns // LANES
    needed = begin([
        (partial_hbm, partial_ref), (other_hbm, other_ref), (levels_hbm, levels_ref), (mix_hbm, mix_ref),
        (top_hbm, top_ref), (top_keep_hbm, top_keep_ref), (slots_hbm, slots_ref),
    ], semaphores)
    chunk = slot_count // CHUNKS
    used = len(needed)
    arriving = begin([
        (weights_hbm.at[pl.ds(part * chunk, chunk)], weights_ref.at[pl.ds(part * chunk, chunk)])
        for part in range(CHUNKS)
    ], semaphores, used)
    used += CHUNKS

    def edge(dx, dy):
        if few:
            where = position_of(few, dx, dy)
            return edges_ref[2 * where] + edges_ref[2 * where + 1]
        where = EDGES.index((dx, dy))
        return edges_ref[2 * where] + edges_ref[2 * where + 1]

    after, before = edge(1, 0), edge(-1, 0)
    right, left = edge(0, 1), edge(0, -1)
    corners = {(dx, dy): edge(dx, dy) for dx in (1, -1) for dy in (1, -1)}
    lane = lax.broadcasted_iota(jnp.int32, (TILE, LANES), 1)
    short = lax.broadcasted_iota(jnp.int32, (HALO, LANES), 1)
    surface_ref[...] = jnp.zeros_like(surface_ref)
    finish(needed)
    for field in range(fields):
        surface_ref[field, 0:rows, 0:columns] = partial_ref[field] + other_ref[field]
        for half in range(halves):
            place = (field * 2 + half) * HALO
            here = slice(half * LANES, (half + 1) * LANES)
            surface_ref[field, rows : rows + WIDTH, here] = after[place : place + WIDTH]
            surface_ref[field, rows + 2 * HALO - WIDTH :, here] = before[place : place + WIDTH]
        for part in range(rows // TILE):
            place = 2 * HALO * part + HALO * field
            from_right = pltpu.roll(right[0:TILE], (LANES - place) % LANES, 1)
            from_left = pltpu.roll(left[0:TILE], (2 * LANES - HALO - place) % LANES, 1)
            tile = jnp.where(lane < HALO, from_right, jnp.where(lane >= LANES - HALO, from_left, 0.0))
            surface_ref[field, part * TILE : (part + 1) * TILE, columns:] = tile
        low, high = field * 2 * HALO, (field * 2 + halves - 1) * HALO
        for dx in (1, -1):
            from_right, from_left = corners[dx, 1][low : low + HALO], corners[dx, -1][high : high + HALO]
            tile = jnp.where(short < HALO, from_right, jnp.where(short >= LANES - HALO, from_left, 0.0))
            if dx == 1:
                surface_ref[field, rows : rows + WIDTH, columns:] = tile[0:WIDTH]
            else:
                surface_ref[field, rows + 2 * HALO - WIDTH :, columns:] = tile[0:WIDTH]

    leaving = begin([(surface_ref, surface_hbm)], semaphores, used)
    levels = levels_ref[...]
    forcings = [depth_share(jnp.float32(level), total_levels) * surface_ref[1] for level in range(STEPS)]
    forcings[0] = forcings[0] + surface_ref[0]
    for level in range(STEPS):
        first_ref[level] = top_ref[level] + jnp.where(levels > float(level), 0.1 * forcings[level], 0.0)
    source, target = first_ref, second_ref
    zero = jnp.zeros_like(levels)
    for step in range(2, STEPS + 1):
        for level in range(TOP - step):
            over = source[level - 1] if level else zero
            target[level] = step_slab(
                source[level], over, source[level + 1], top_keep_ref[level], mix_ref[...], levels, float(level),
                forcings[level],
            )
        source, target = target, source
    for half in range(halves):
        values = source[0, 0:rows, half * LANES : (half + 1) * LANES]
        sst_ref[half * rows : (half + 1) * rows] = values.astype(jnp.bfloat16).astype(jnp.float32)

    for slot in range(slot_count):
        tile = slots_ref[1, slot]
        place = lax.rem(tile, halves) * rows + lax.div(tile, halves)
        rows_ref[pl.ds(slot, 1)] = sst_ref[pl.ds(place, 1)]
    sums_ref = sums_scratch[0]
    sums_ref[...] = jnp.zeros_like(sums_ref)
    for group in range(slot_count // TILE):
        given = rows_ref[group * TILE : (group + 1) * TILE].astype(jnp.bfloat16)
        for row in range(TILE):
            slot = group * TILE + row
            if slot % chunk == 0:
                arriving[slot // chunk].wait()
            got = lax.dot_general(
                given, weights_ref[slot], (((1,), (1,)), ((), ())), preferred_element_type=jnp.float32
            )
            sums_ref[pl.ds(slots_ref[0, slot], 1)] += got[row : row + 1]
    if few:
        for block in range(sums_ref.shape[0]):
            both = jnp.broadcast_to(sums_ref[block : block + 1], (2, LANES))
            back_ref[2 * block : 2 * block + 2] = both
    else:
        back_ref[...] = sums_ref[...]
    finish(leaving)


def ocean_kernel(
    temp_hbm, moved_hbm, keep_hbm, levels_hbm, mix_hbm, surface_hbm, ocean_hbm,
    temp_ref, keep_ref, levels_ref, mix_ref, surface_ref, semaphores, first_ref, second_ref, *, total_levels,
):
    layers, rows, columns = temp_hbm.shape
    gz = lax.axis_index("gz")
    first_level = gz * layers - HALO
    base = jnp.where(gz == 0, HALO, 1)
    count = layers + HALO - 1
    needed = begin(
        [(levels_hbm, levels_ref), (mix_hbm, mix_ref), (surface_hbm, surface_ref)], semaphores
    )
    used = len(needed)
    spans = [pl.ds(base + start, size) for start, size in pieces(count)]
    arriving = begin([(moved_hbm.at[span], first_ref.at[span]) for span in spans], semaphores, used)
    used += len(spans)
    later = begin([
        (keep_hbm.at[pl.ds(base, count)], keep_ref.at[pl.ds(base, count)]), (temp_hbm, temp_ref)
    ], semaphores, used)
    used += len(later)
    edge = jnp.where(gz == 0, HALO - 1, HALO + layers)
    first_ref[edge] = jnp.zeros_like(first_ref[0])
    second_ref[edge] = jnp.zeros_like(first_ref[0])
    finish(needed)

    def level_of(place):
        return (first_level + place).astype(jnp.float32)

    def add(place):
        level = level_of(place)
        forcing = (0.1 * depth_share(level, total_levels)) * surface_ref[1]
        first_ref[place] = first_ref[place] + jnp.where(levels_ref[...] > level, forcing, 0.0)

    for (start, size), copy in zip(pieces(count), arriving):
        copy.wait()
        in_order(base + start, size, add)

    def top_forcing():
        return jnp.where(levels_ref[...] > 0.0, 0.1 * surface_ref[0], 0.0)

    @pl.when(gz == 0)
    def _():
        first_ref[HALO] = first_ref[HALO] + top_forcing()

    later[0].wait()
    source, target = first_ref, second_ref
    for step in range(2, STEPS + 1):
        if step == STEPS:
            later[1].wait()

        def one(place, source=source, target=target, step=step):
            level = level_of(place)
            new = step_slab(
                source[place], source[place - 1], source[place + 1], keep_ref[place], mix_ref[...], levels_ref[...],
                level, depth_share(level, total_levels) * surface_ref[1],
            )
            if step < STEPS:
                target[place] = new
            else:
                index = place - HALO
                wet = levels_ref[0:rows, 0:columns] > level
                temp_ref[index] = jnp.where(wet, new[0:rows, 0:columns], temp_ref[index])

        if step < STEPS:
            in_order(jnp.where(gz == 0, HALO, step), layers + HALO - step, one)

            @pl.when(gz == 0)
            def _(target=target):
                target[HALO] = target[HALO] + top_forcing()
        else:
            leaving = []
            for start, size in pieces(layers):
                in_order(HALO + start, size, one)
                if start == 0:
                    @pl.when(gz == 0)
                    def _():
                        temp_ref[0] = temp_ref[0] + top_forcing()[0:rows, 0:columns]

                here = pl.ds(start, size)
                leaving += begin([(temp_ref.at[here], ocean_hbm.at[here])], semaphores, used)
                used += 1
            finish(leaving)
        source, target = target, source


def gather_kernel(sends_ref, returned_ref, surface_ref):
    me = lax.axis_index("gx") * lax.axis_size("gy") + lax.axis_index("gy")
    surface_ref[...] = jnp.zeros_like(surface_ref)
    blocks = sends_ref.shape[0]
    copies = returned_ref.shape[0] // blocks

    def one(block, carry):
        tile = sends_ref[me, block]
        place = jnp.maximum(tile, 0)
        got = returned_ref[pl.ds(block * copies, 1)]
        for copy in range(1, copies):
            got = got + returned_ref[pl.ds(block * copies + copy, 1)]
        surface_ref[pl.ds(place, 1)] += jnp.where(tile >= 0, got, 0.0)
        return carry

    lax.fori_loop(0, blocks, one, 0)


def call(body, outs, scratch, operands, places, out_places, cost=0):
    space = {"v": pltpu.VMEM, "s": pltpu.SMEM, "h": pl.ANY}
    assert len(places) == len(operands) and len(out_places) == len(outs)
    scratch_shapes = []
    for item in scratch:
        if isinstance(item, int):
            scratch_shapes.append(pltpu.SemaphoreType.DMA((item,)))
        elif isinstance(item, tuple):
            scratch_shapes.append(pltpu.VMEM(item, jnp.float32))
        else:
            scratch_shapes.append(item)
    return pl.pallas_call(
        body,
        out_shape=[jax.ShapeDtypeStruct(out, jnp.float32) for out in outs],
        in_specs=[pl.BlockSpec(memory_space=space[place]) for place in places],
        out_specs=[pl.BlockSpec(memory_space=space[place]) for place in out_places],
        scratch_shapes=scratch_shapes,
        compiler_params=pltpu.CompilerParams(vmem_limit_bytes=VMEM_LIMIT),
        cost_estimate=pl.CostEstimate(flops=cost, bytes_accessed=4 * cost // 16, transcendentals=0),
    )(*operands)


def like(array):
    return pltpu.VMEM(array.shape, array.dtype)


EDGES = [(dx, dy) for dx in (-1, 0, 1) for dy in (-1, 0, 1) if (dx, dy) != (0, 0)]


def toward(gx_count, gy_count, dx, dy):
    pairs = []
    for x in range(gx_count):
        for y in range(gy_count):
            if 0 <= x + dx < gx_count and 0 <= y + dy < gy_count:
                pairs.append(((x + dx) * gy_count + y + dy, x * gy_count + y))
    return pairs


def per_device(
    ocean_temp, bathy_levels, mixing, atm_flux, send_tiles, regrid_slots, regrid_weights
):
    layers, rows, columns = ocean_temp.shape
    gx_count, gy_count, gz_count = (lax.axis_size(axis) for axis in ALL_AXES)
    blocks = gx_count * gy_count
    own_tiles, fields, tile_atm = atm_flux.shape
    caps = send_tiles.shape[2]
    assert gz_count == 2 and caps == 1 and layers == GROUP and tile_atm == LANES
    assert columns == 2 * LANES and rows == 4 * TILE and regrid_weights.shape[2] == LANES
    total_levels = layers * gz_count
    few = blocks <= FEW
    sends = send_tiles.reshape(blocks, blocks)
    swap = [(0, 1), (1, 0)]
    tall = 2 * TILE + rows
    strip = (layers + 2, HALO, columns)
    slab = (rows + 2 * HALO, columns + LANES)
    slab_cost = 20 * slab[0] * slab[1]
    deep = (layers + 2 * HALO,) + slab

    high_rows = (2, layers, TILE, columns)
    low, high = call(
        rows_kernel, [strip, strip],
        [high_rows, pltpu.VMEM((2, TILE, columns), jnp.int32), (2, TILE, columns), 6],
        (ocean_temp, bathy_levels, mixing), "hhh", "vv", cost=slab_cost,
    )
    forward = [(i, i + 1) for i in range(gx_count - 1)]
    backward = [(target, source) for source, target in forward]
    before_rows = lax.ppermute(high, "gx", forward)
    after_rows = lax.ppermute(low, "gx", backward)
    outs = [(blocks, tall, LANES)] if few else [(blocks, TILE, LANES), (2, tall, LANES)]
    sides = 1 if few and gy_count == 2 else 2
    scratch = [
        pltpu.SMEM(sends.shape, jnp.int32), like(atm_flux), (sides, layers, rows, LANES),
        pltpu.VMEM((sides, rows, LANES), jnp.int32), (sides, rows, LANES), 2 + 3 * sides,
        (own_tiles, fields, LANES),
    ]
    sent = call(
        functools.partial(send_kernel, few=few, sides=sides), outs, scratch + ([(sides, tall, LANES)] if few else []),
        (sends, atm_flux, ocean_temp, bathy_levels, mixing, low), "hhhhhh", "v" * len(outs), cost=2 * slab_cost,
    )
    got = [lax.all_to_all(sent[0], BLOCKS_AXES, split_axis=0, concat_axis=0, tiled=True)]
    if not few:
        got.append(jnp.stack([
            lax.ppermute(sent[1][0 if dy > 0 else 1], BLOCKS_AXES, toward(gx_count, gy_count, dx, dy))
            for dx in (-1, 0, 1) for dy in (-1, 1)
        ]))

    strips = (4, 2 * TILE, LANES)
    packed_shape = (2, slab[0], LANES)
    partial, edges, shared, levels, mix, packed = call(
        functools.partial(regrid_kernel, few=few),
        [
            (fields, rows, columns), (2 * blocks, 2 * TILE, LANES) if few else strips,
            (TOP + HALO,) + slab, slab, slab, packed_shape,
        ],
        [
            pltpu.SMEM(regrid_slots.shape, jnp.int32), like(regrid_weights), (TOP + HALO, rows, columns),
            like(bathy_levels), like(mixing), slab, slab, packed_shape, 8 + CHUNKS,
            (rows * columns // LANES * TILE, LANES),
        ] + ([strips] if few else []),
        (
            regrid_slots, *got, regrid_weights, ocean_temp, bathy_levels, mixing, after_rows, before_rows,
        ), "h" + "v" * len(got) + "hhhhvv", "vvvhhh", cost=10 * slab_cost,
    )
    other_partial = lax.ppermute(partial, "gz", swap)
    other_shared = lax.ppermute(shared, "gz", swap)
    if few:
        edges = lax.all_to_all(edges, ALL_AXES, split_axis=0, concat_axis=0, tiled=True)
    else:
        choice = {-1: 1, 1: 0}
        around = jnp.stack([
            lax.ppermute(
                edges[choice[dx] if dx else (3 if dy < 0 else 2)], BLOCKS_AXES, toward(gx_count, gy_count, dx, dy)
            )
            for dx, dy in EDGES
        ])
        edges = jnp.stack([around, lax.ppermute(around, "gz", swap)], axis=1)
        edges = edges.reshape((2 * len(EDGES),) + strips[1:])

    top = (STEPS,) + slab
    parts = len(pieces(layers + HALO - 1))
    moved, keep, top_moved, top_keep = call(
        first_kernel, [deep, deep, top, top],
        [
            like(ocean_temp), strip, strip, packed_shape, (TOP + HALO,) + slab, slab, slab,
            deep, deep, top, top, deep, (TOP,) + slab, 9 + CHUNKS + parts,
        ],
        (ocean_temp, after_rows, before_rows, packed, other_shared, levels, mix), "h" * 7, "hhhh", cost=80 * slab_cost,
    )
    surface, back = call(
        functools.partial(skin_kernel, few=few, total_levels=total_levels),
        [(fields,) + slab, ((2 if few else 1) * blocks, LANES)],
        [
            pltpu.SMEM(regrid_slots.shape, jnp.int32), like(partial), like(partial), like(regrid_weights), slab, slab,
            top, top, (fields,) + slab, 8 + CHUNKS,
            top, top, (rows * columns // LANES, LANES), (regrid_weights.shape[0], LANES), (blocks, LANES),
        ],
        (regrid_slots, partial, other_partial, edges, regrid_weights, levels, mix, top_moved, top_keep),
        "hhhvhhhhh", "hv", cost=20 * slab_cost,
    )
    if few:
        returned = lax.all_to_all(back, ALL_AXES, split_axis=0, concat_axis=0, tiled=True)
    else:
        returned = lax.all_to_all(back, BLOCKS_AXES, split_axis=0, concat_axis=0, tiled=True)
        returned = returned + lax.ppermute(returned, "gz", swap)
    ocean, = call(
        functools.partial(ocean_kernel, total_levels=total_levels), [ocean_temp.shape],
        [like(ocean_temp), deep, slab, slab, (fields,) + slab, 5 + parts + len(pieces(layers)), deep, deep],
        (ocean_temp, moved, keep, levels, mix, surface), "h" * 6, "h", cost=120 * slab_cost,
    )
    atm_surface, = call(gather_kernel, [(own_tiles, LANES)], [], (sends, returned), "sv", "v", cost=slab_cost // 10)
    return (ocean, atm_surface)


def solution(mesh):
    return jax.shard_map(
        per_device,
        mesh=mesh,
        in_specs=(
            P(("ens", "gz"), "gx", "gy"),
            P(("ens", "gx"), "gy"),
            P(("ens", "gx"), "gy"),
            P(("ens", "gx", "gy"), None, None),
            P(),
            P(None, ("gx", "gy", "gz")),
            P(("gx", "gy", "gz"), None, None),
        ),
        out_specs=(P(("ens", "gz"), "gx", "gy"), P(("ens", "gx", "gy"), None)),
        check_vma=False,
    )
```

```python
import functools

import jax
import jax.numpy as jnp
from jax import lax
from jax.experimental import pallas as pl
from jax.experimental.pallas import tpu as pltpu
from jax.sharding import PartitionSpec as P

STEPS = 4
HALO = STEPS
WIDTH = STEPS - 1
TOP = STEPS + 1
LANES = 128
TILE = 8
GROUP = LANES // HALO
FEW = 16
UNROLL = 8
CHUNKS = 4
BLOCKS_AXES = ("gx", "gy")
ALL_AXES = ("gx", "gy", "gz")
VMEM_LIMIT = 60 * 1024 * 1024


def position_of(few, dx, dy):
    if not few:
        return (dx + 1) * 2 + (1 if dy > 0 else 0)
    gx_count, gy_count = lax.axis_size("gx"), lax.axis_size("gy")
    x = jnp.clip(lax.axis_index("gx") + dx, 0, gx_count - 1)
    y = jnp.clip(lax.axis_index("gy") + dy, 0, gy_count - 1)
    return x * gy_count + y


def side_tile(left, right, index):
    lane = lax.broadcasted_iota(jnp.int32, left.shape, 1)
    from_right = pltpu.roll(right, lax.rem(LANES - HALO * index, LANES), 1)
    from_left = pltpu.roll(left, lax.rem(2 * LANES - HALO - HALO * index, LANES), 1)
    zero = jnp.zeros_like(left)
    return jnp.where(lane < HALO, from_right, jnp.where(lane >= LANES - HALO, from_left, zero))


def put_slab(ref, own, after, before, tile):
    rows, columns = own.shape
    ref[0:rows, 0:columns] = own
    ref[rows : rows + HALO, 0:columns] = after
    ref[rows + HALO : rows + 2 * HALO, 0:columns] = before
    ref[:, columns:] = tile


def wet_around(levels, level):
    rows, lanes = levels.shape
    wet = jnp.where(levels > level, 0.1, 0.0)
    total = pltpu.roll(wet, 1, 0) + pltpu.roll(wet, rows - 1, 0)
    return total + (pltpu.roll(wet, 1, 1) + pltpu.roll(wet, lanes - 1, 1))


def keep_share(levels, mixing, level):
    above = jnp.where(level > 0.0, 1.0, 0.0)
    vertical = above + jnp.where(levels > level + 1.0, 1.0, 0.0)
    return 1.0 - wet_around(levels, level) - mixing * vertical


def step_slab(center, over, under, keep, mixing, levels, level, forcing):
    rows, lanes = center.shape
    lateral = pltpu.roll(center, 1, 0) + pltpu.roll(center, rows - 1, 0)
    lateral = lateral + (pltpu.roll(center, 1, 1) + pltpu.roll(center, lanes - 1, 1))
    if forcing is not None:
        lateral = lateral + forcing
    new = center * keep + 0.1 * lateral + mixing * (over + under)
    return jnp.where(levels > level, new, 0.0)


def depth_share(level, total_levels):
    return jnp.exp(jnp.full((1, 1), -4.0 / total_levels, jnp.float32) * level)


def begin(copies, semaphores, first=0):
    started = []
    for index, (source, target) in enumerate(copies):
        copy = pltpu.make_async_copy(source, target, semaphores.at[first + index])
        copy.start()
        started.append(copy)
    return started


def finish(copies):
    for copy in copies:
        copy.wait()


def in_order(start, count, body):
    whole = count // UNROLL

    def group(index, carry):
        for offset in range(UNROLL):
            body(start + index * UNROLL + offset)
        return carry

    lax.fori_loop(0, whole, group, 0)
    for index in range(whole * UNROLL, count):
        body(start + index)


def rows_kernel(temp_ref, bathy_ref, mixing_ref, low_ref, high_ref, temp_rows, bathy_rows, mixing_rows, semaphores):
    layers, rows, columns = temp_ref.shape
    copies = []
    for side in range(2):
        part = pl.ds(side * (rows - TILE), TILE)
        copies += [(temp_ref.at[:, part], temp_rows.at[side]), (bathy_ref.at[part], bathy_rows.at[side])]
        copies += [(mixing_ref.at[part], mixing_rows.at[side])]
    finish(begin(copies, semaphores))
    for side, (out_ref, part) in enumerate(((low_ref, slice(0, HALO)), (high_ref, slice(TILE - HALO, TILE)))):
        out_ref[0:layers] = temp_rows[side, :, part]
        out_ref[layers] = bathy_rows[side, part].astype(jnp.float32)
        out_ref[layers + 1] = mixing_rows[side, part]


def send_kernel(sends_hbm, flux_hbm, temp_hbm, bathy_hbm, mixing_hbm, after_ref, *refs, few, sides):
    if few:
        message_ref, sends_ref, flux_ref, temp_ref, bathy_ref, mixing_ref, semaphores, flux_scratch, strips_ref = refs
        fluxes_ref = message_ref
    else:
        (
            fluxes_ref, strips_ref, sends_ref, flux_ref, temp_ref, bathy_ref, mixing_ref, semaphores, flux_scratch,
        ) = refs
    layers, rows, columns = temp_hbm.shape
    gy, gy_count = lax.axis_index("gy"), lax.axis_size("gy")
    me = lax.axis_index("gx") * gy_count + gy
    copies = [(sends_hbm, sends_ref), (flux_hbm, flux_ref)]
    for place in range(sides):
        side = 1 - gy if sides == 1 else place
        window = pl.ds(pl.multiple_of(side * (columns - LANES), LANES), LANES)
        copies += [(bathy_hbm.at[:, window], bathy_ref.at[place]), (mixing_hbm.at[:, window], mixing_ref.at[place])]
        copies += [(temp_hbm.at[:, :, window], temp_ref.at[place])]
    copies = begin(copies, semaphores)
    lane = lax.broadcasted_iota(jnp.int32, (rows, LANES), 1)
    short = lax.broadcasted_iota(jnp.int32, (TILE, LANES), 1)
    finish(copies)
    for side in range(sides):
        base = HALO * (1 - gy) if sides == 1 else HALO * side
        strip = jnp.zeros((rows, LANES), jnp.float32)
        for index in range(layers):
            place = HALO * index
            moved = pltpu.roll(temp_ref[side, index], lax.rem(place + base, LANES), 1)
            strip = jnp.where((lane >= place) & (lane < place + HALO), moved, strip)
        strips_ref[side, 2 * TILE : 2 * TILE + rows] = strip
        plain = jnp.zeros((TILE, LANES), jnp.float32)
        for part in range(rows // TILE):
            here = slice(part * TILE, (part + 1) * TILE)
            for which, values in enumerate((bathy_ref[side, here].astype(jnp.float32), mixing_ref[side, here])):
                place = 2 * HALO * part + HALO * which
                moved = pltpu.roll(values, lax.rem(place + base, LANES), 1)
                plain = jnp.where((short >= place) & (short < place + HALO), moved, plain)
        strips_ref[side, TILE : 2 * TILE] = plain
        strips_ref[side, 0:TILE] = jnp.zeros((TILE, LANES), jnp.float32)
    flux_scratch[...] = flux_ref[...].astype(jnp.float32)
    fields = flux_ref.shape[1]

    def one(block, carry):
        tile = sends_ref[me, block]
        if few:
            side = 0 if sides == 1 else (lax.rem(block, gy_count) > gy).astype(jnp.int32)
            message_ref[block] = strips_ref[side]
        else:
            fluxes_ref[block] = jnp.zeros(fluxes_ref.shape[1:], jnp.float32)
        sent = jnp.where(tile >= 0, flux_scratch[jnp.maximum(tile, 0)], 0.0)
        fluxes_ref[block, 0:fields] = sent
        return carry

    if few:
        for block in range(fluxes_ref.shape[0]):
            one(block, 0)
    else:
        lax.fori_loop(0, fluxes_ref.shape[0], one, 0)


def regrid_kernel(slots_hbm, *refs, few):
    if few:
        sides_ref, *refs = refs
        flux_ref = sides_ref
    else:
        flux_ref, sides_ref, *refs = refs
    (
        weights_hbm, temp_hbm, bathy_hbm, mixing_hbm, next_ref, prev_ref,
        partial_ref, edges_ref, shared_ref, levels_hbm, mix_hbm, packed_hbm,
        slots_ref, weights_ref, temp_ref, bathy_ref, mixing_ref, levels_ref, mix_ref, packed_ref, semaphores,
        sums_ref, *strip_scratch,
    ) = refs
    layers, rows, columns = temp_hbm.shape
    slot_count, tile_atm, patch = weights_ref.shape
    halves = columns // LANES
    lasts = pl.ds(layers - HALO, HALO)
    needed = begin([
        (temp_hbm.at[pl.ds(0, TOP)], temp_ref.at[pl.ds(0, TOP)]), (temp_hbm.at[lasts], temp_ref.at[pl.ds(TOP, HALO)]),
        (bathy_hbm, bathy_ref), (mixing_hbm, mixing_ref), (slots_hbm, slots_ref),
    ], semaphores)
    chunk = slot_count // CHUNKS
    arriving = begin([
        (weights_hbm.at[pl.ds(part * chunk, chunk)], weights_ref.at[pl.ds(part * chunk, chunk)])
        for part in range(CHUNKS)
    ], semaphores, len(needed))
    sums_ref[...] = jnp.zeros_like(sums_ref)

    gx, gx_count = lax.axis_index("gx"), lax.axis_size("gx")
    gy, gy_count = lax.axis_index("gy"), lax.axis_size("gy")
    plain = []
    for side, dy in ((0, -1), (1, 1)):
        own, after, before = (position_of(few, dx, dy) for dx in (0, 1, -1))
        packed_ref[side, 0:rows] = sides_ref[own, 2 * TILE : 2 * TILE + rows]
        packed_ref[side, rows : rows + HALO] = sides_ref[after, 2 * TILE : 2 * TILE + HALO]
        packed_ref[side, rows + HALO :] = sides_ref[before, 2 * TILE + rows - HALO : 2 * TILE + rows]
        tile = sides_ref[own, TILE : 2 * TILE]
        parts = [tile] + [pltpu.roll(tile, LANES - 2 * HALO * part, 1) for part in range(1, rows // TILE)]
        last = pltpu.roll(sides_ref[before, TILE : 2 * TILE], LANES - 2 * HALO * (rows // TILE - 1), 1)
        row = lax.broadcasted_iota(jnp.int32, (TILE, LANES), 0)
        parts.append(jnp.where(row < HALO, sides_ref[after, TILE : 2 * TILE], last))
        plain.append(jnp.concatenate(parts, axis=0))
    finish(needed)
    size = (rows + 2 * HALO, LANES)
    lane, row = (lax.broadcasted_iota(jnp.int32, size, dim) for dim in (1, 0))
    there = (lane < HALO) & (gy < gy_count - 1) | (lane >= HALO) & (gy > 0)
    there = there & ((row < rows) | (row < rows + HALO) & (gx < gx_count - 1) | (row >= rows + HALO) & (gx > 0))
    tile = jnp.where(there, side_tile(plain[0], plain[1], 0), 0.0)
    put_slab(levels_ref, bathy_ref[...].astype(jnp.float32), next_ref[layers], prev_ref[layers], tile)
    tile = side_tile(plain[0], plain[1], 1)
    put_slab(mix_ref, mixing_ref[...], next_ref[layers + 1], prev_ref[layers + 1], tile)
    for place, level in enumerate(list(range(TOP)) + list(range(layers - HALO, layers))):
        tile = side_tile(packed_ref[0], packed_ref[1], level)
        put_slab(shared_ref.at[place], temp_ref[place], next_ref[level], prev_ref[level], tile)
    leaving = begin(
        [(levels_ref, levels_hbm), (mix_ref, mix_hbm), (packed_ref, packed_hbm)], semaphores, len(needed) + CHUNKS
    )
    for slot in range(slot_count):
        if slot % chunk == 0:
            arriving[slot // chunk].wait()
        fluxes = flux_ref[slots_ref[0, slot], 0:TILE, :].astype(jnp.bfloat16)
        got = jnp.dot(fluxes, weights_ref[slot], preferred_element_type=jnp.float32)
        place = pl.multiple_of(slots_ref[1, slot] * TILE, TILE)
        sums_ref[pl.ds(place, TILE)] += got

    strips_ref = strip_scratch[0] if few else edges_ref
    strips_ref[...] = jnp.zeros_like(strips_ref)
    short = lax.broadcasted_iota(jnp.int32, (TILE, LANES), 1)
    columns_low = jnp.zeros((TILE, LANES), jnp.float32)
    columns_high = jnp.zeros((TILE, LANES), jnp.float32)
    for field in range(2):
        for half in range(halves):
            values = sums_ref[pl.ds(half * TILE + field, rows, stride=halves * TILE), :]
            partial_ref[field, :, half * LANES : (half + 1) * LANES] = values
            place = (field * 2 + half) * HALO
            strips_ref[0, place : place + WIDTH] = values[0:WIDTH]
            strips_ref[1, place : place + WIDTH] = values[rows - WIDTH : rows]
            for part in range(rows // TILE):
                block = values[part * TILE : (part + 1) * TILE]
                place = 2 * HALO * part + HALO * field
                inside = (short >= place) & (short < place + HALO)
                if half == 0:
                    columns_low = jnp.where(inside, pltpu.roll(block, place % LANES, 1), columns_low)
                if half == halves - 1:
                    columns_high = jnp.where(inside, pltpu.roll(block, (place + HALO) % LANES, 1), columns_high)
    strips_ref[2, 0:TILE] = columns_low
    strips_ref[3, 0:TILE] = columns_high
    if few:
        gx, gy, gy_count = lax.axis_index("gx"), lax.axis_index("gy"), lax.axis_size("gy")
        for entry in range(edges_ref.shape[0]):
            x, y = entry // 2 // gy_count, entry // 2 % gy_count
            choice = jnp.where(x < gx, 0, jnp.where(x > gx, 1, jnp.where(y < gy, 2, 3)))
            edges_ref[entry] = strips_ref[choice]

    finish(leaving)


def first_kernel(
    temp_hbm, next_hbm, prev_hbm, packed_hbm, other_hbm, levels_hbm, mix_hbm,
    moved_hbm, keep_hbm, top_hbm, top_keep_hbm,
    temp_ref, next_ref, prev_ref, packed_ref, other_ref, levels_ref, mix_ref,
    moved_ref, keep_ref, top_ref, top_keep_ref, first_ref, skin_ref, semaphores,
):
    layers = temp_hbm.shape[0]
    gz = lax.axis_index("gz")
    first_level = gz * layers - HALO
    needed = begin([
        (next_hbm, next_ref), (prev_hbm, prev_ref), (packed_hbm, packed_ref), (levels_hbm, levels_ref),
        (mix_hbm, mix_ref), (other_hbm, other_ref),
    ], semaphores)
    chunk = layers // CHUNKS
    parts = [pl.ds(part * chunk, chunk) for part in range(CHUNKS)]
    used = len(needed)
    arriving = begin([(temp_hbm.at[part], temp_ref.at[part]) for part in parts], semaphores, used)
    used += CHUNKS
    finish(needed)

    def level_of(place):
        return (first_level + place).astype(jnp.float32)

    def settle(place):
        level = level_of(place)
        first_ref[place] = jnp.where(levels_ref[...] > level, first_ref[place], 0.0)
        keep_ref[place] = keep_share(levels_ref[...], mix_ref[...], level)

    def own_level(index):
        tile = side_tile(packed_ref[0], packed_ref[1], index)
        put_slab(first_ref.at[index + HALO], temp_ref[index], next_ref[index], prev_ref[index], tile)
        settle(index + HALO)

    for part in range(CHUNKS):
        arriving[part].wait()
        in_order(part * chunk, chunk, own_level)

    for index in range(HALO):
        slot = jnp.where(gz == 0, index, TOP + index)
        place = jnp.where(gz == 0, HALO + layers + index, index)
        first_ref[place] = other_ref[slot]
        settle(place)

    base = jnp.where(gz == 0, HALO, 1)
    count = layers + HALO - 1
    span = pl.ds(base, count)
    leaving = begin([(keep_ref.at[span], keep_hbm.at[span])], semaphores, used)
    used += 1
    levels = levels_ref[...]
    for level in range(TOP):
        slab = jnp.where(gz == 0, first_ref[HALO + level], other_ref[level])
        skin_ref[level] = jnp.where(levels > float(level), slab, 0.0)
    for level in range(STEPS):
        top_keep_ref[level] = keep_share(levels, mix_ref[...], jnp.float32(level))
        over = skin_ref[level - 1] if level else jnp.zeros_like(levels)
        top_ref[level] = step_slab(
            skin_ref[level], over, skin_ref[level + 1], top_keep_ref[level], mix_ref[...], levels, float(level), None
        )
    leaving += begin([(top_ref, top_hbm), (top_keep_ref, top_keep_hbm)], semaphores, used)
    used += 2
    edge = jnp.where(gz == 0, HALO - 1, HALO + layers)
    first_ref[edge] = jnp.zeros_like(first_ref[0])

    def one(place):
        moved_ref[place] = step_slab(
            first_ref[place], first_ref[place - 1], first_ref[place + 1], keep_ref[place], mix_ref[...],
            levels_ref[...], level_of(place), None,
        )

    for start, size in pieces(count):
        in_order(base + start, size, one)
        here = pl.ds(base + start, size)
        leaving += begin([(moved_ref.at[here], moved_hbm.at[here])], semaphores, used)
        used += 1
    finish(leaving)


def pieces(count):
    return [(start, min(UNROLL, count - start)) for start in range(0, count, UNROLL)]


def skin_kernel(
    slots_hbm, partial_hbm, other_hbm, edges_ref, weights_hbm, levels_hbm, mix_hbm, top_hbm, top_keep_hbm,
    surface_hbm, back_ref,
    slots_ref, partial_ref, other_ref, weights_ref, levels_ref, mix_ref, top_ref, top_keep_ref, surface_ref, semaphores,
    first_ref, second_ref, sst_ref, rows_ref, *sums_scratch, few, total_levels,
):
    fields, rows, columns = partial_ref.shape
    slot_count, tile_atm, patch = weights_ref.shape
    halves = columns // LANES
    needed = begin([
        (partial_hbm, partial_ref), (other_hbm, other_ref), (levels_hbm, levels_ref), (mix_hbm, mix_ref),
        (top_hbm, top_ref), (top_keep_hbm, top_keep_ref), (slots_hbm, slots_ref),
    ], semaphores)
    chunk = slot_count // CHUNKS
    used = len(needed)
    arriving = begin([
        (weights_hbm.at[pl.ds(part * chunk, chunk)], weights_ref.at[pl.ds(part * chunk, chunk)])
        for part in range(CHUNKS)
    ], semaphores, used)
    used += CHUNKS

    def edge(dx, dy):
        if few:
            where = position_of(few, dx, dy)
            return edges_ref[2 * where] + edges_ref[2 * where + 1]
        where = EDGES.index((dx, dy))
        return edges_ref[2 * where] + edges_ref[2 * where + 1]

    after, before = edge(1, 0), edge(-1, 0)
    right, left = edge(0, 1), edge(0, -1)
    corners = {(dx, dy): edge(dx, dy) for dx in (1, -1) for dy in (1, -1)}
    lane = lax.broadcasted_iota(jnp.int32, (TILE, LANES), 1)
    short = lax.broadcasted_iota(jnp.int32, (HALO, LANES), 1)
    surface_ref[...] = jnp.zeros_like(surface_ref)
    finish(needed)
    for field in range(fields):
        surface_ref[field, 0:rows, 0:columns] = partial_ref[field] + other_ref[field]
        for half in range(halves):
            place = (field * 2 + half) * HALO
            here = slice(half * LANES, (half + 1) * LANES)
            surface_ref[field, rows : rows + WIDTH, here] = after[place : place + WIDTH]
            surface_ref[field, rows + 2 * HALO - WIDTH :, here] = before[place : place + WIDTH]
        for part in range(rows // TILE):
            place = 2 * HALO * part + HALO * field
            from_right = pltpu.roll(right[0:TILE], (LANES - place) % LANES, 1)
            from_left = pltpu.roll(left[0:TILE], (2 * LANES - HALO - place) % LANES, 1)
            tile = jnp.where(lane < HALO, from_right, jnp.where(lane >= LANES - HALO, from_left, 0.0))
            surface_ref[field, part * TILE : (part + 1) * TILE, columns:] = tile
        low, high = field * 2 * HALO, (field * 2 + halves - 1) * HALO
        for dx in (1, -1):
            from_right, from_left = corners[dx, 1][low : low + HALO], corners[dx, -1][high : high + HALO]
            tile = jnp.where(short < HALO, from_right, jnp.where(short >= LANES - HALO, from_left, 0.0))
            if dx == 1:
                surface_ref[field, rows : rows + WIDTH, columns:] = tile[0:WIDTH]
            else:
                surface_ref[field, rows + 2 * HALO - WIDTH :, columns:] = tile[0:WIDTH]

    leaving = begin([(surface_ref, surface_hbm)], semaphores, used)
    levels = levels_ref[...]
    forcings = [depth_share(jnp.float32(level), total_levels) * surface_ref[1] for level in range(STEPS)]
    forcings[0] = forcings[0] + surface_ref[0]
    for level in range(STEPS):
        first_ref[level] = top_ref[level] + jnp.where(levels > float(level), 0.1 * forcings[level], 0.0)
    source, target = first_ref, second_ref
    zero = jnp.zeros_like(levels)
    for step in range(2, STEPS + 1):
        for level in range(TOP - step):
            over = source[level - 1] if level else zero
            target[level] = step_slab(
                source[level], over, source[level + 1], top_keep_ref[level], mix_ref[...], levels, float(level),
                forcings[level],
            )
        source, target = target, source
    for half in range(halves):
        values = source[0, 0:rows, half * LANES : (half + 1) * LANES]
        sst_ref[half * rows : (half + 1) * rows] = values.astype(jnp.bfloat16).astype(jnp.float32)

    for slot in range(slot_count):
        tile = slots_ref[1, slot]
        place = lax.rem(tile, halves) * rows + lax.div(tile, halves)
        rows_ref[pl.ds(slot, 1)] = sst_ref[pl.ds(place, 1)]
    sums_ref = sums_scratch[0]
    sums_ref[...] = jnp.zeros_like(sums_ref)
    for group in range(slot_count // TILE):
        given = rows_ref[group * TILE : (group + 1) * TILE].astype(jnp.bfloat16)
        for row in range(TILE):
            slot = group * TILE + row
            if slot % chunk == 0:
                arriving[slot // chunk].wait()
            got = lax.dot_general(
                given, weights_ref[slot], (((1,), (1,)), ((), ())), preferred_element_type=jnp.float32
            )
            sums_ref[pl.ds(slots_ref[0, slot], 1)] += got[row : row + 1]
    if few:
        for block in range(sums_ref.shape[0]):
            both = jnp.broadcast_to(sums_ref[block : block + 1], (2, LANES))
            back_ref[2 * block : 2 * block + 2] = both
    else:
        back_ref[...] = sums_ref[...]
    finish(leaving)


def ocean_kernel(
    temp_hbm, moved_hbm, keep_hbm, levels_hbm, mix_hbm, surface_hbm, ocean_hbm,
    temp_ref, keep_ref, levels_ref, mix_ref, surface_ref, semaphores, first_ref, second_ref, *, total_levels,
):
    layers, rows, columns = temp_hbm.shape
    gz = lax.axis_index("gz")
    first_level = gz * layers - HALO
    base = jnp.where(gz == 0, HALO, 1)
    count = layers + HALO - 1
    needed = begin(
        [(levels_hbm, levels_ref), (mix_hbm, mix_ref), (surface_hbm, surface_ref)], semaphores
    )
    used = len(needed)
    spans = [pl.ds(base + start, size) for start, size in pieces(count)]
    arriving = begin([(moved_hbm.at[span], first_ref.at[span]) for span in spans], semaphores, used)
    used += len(spans)
    later = begin([
        (keep_hbm.at[pl.ds(base, count)], keep_ref.at[pl.ds(base, count)]), (temp_hbm, temp_ref)
    ], semaphores, used)
    used += len(later)
    edge = jnp.where(gz == 0, HALO - 1, HALO + layers)
    first_ref[edge] = jnp.zeros_like(first_ref[0])
    second_ref[edge] = jnp.zeros_like(first_ref[0])
    finish(needed)

    def level_of(place):
        return (first_level + place).astype(jnp.float32)

    def add(place):
        level = level_of(place)
        forcing = (0.1 * depth_share(level, total_levels)) * surface_ref[1]
        first_ref[place] = first_ref[place] + jnp.where(levels_ref[...] > level, forcing, 0.0)

    for (start, size), copy in zip(pieces(count), arriving):
        copy.wait()
        in_order(base + start, size, add)

    def top_forcing():
        return jnp.where(levels_ref[...] > 0.0, 0.1 * surface_ref[0], 0.0)

    @pl.when(gz == 0)
    def _():
        first_ref[HALO] = first_ref[HALO] + top_forcing()

    later[0].wait()
    source, target = first_ref, second_ref
    for step in range(2, STEPS + 1):
        if step == STEPS:
            later[1].wait()

        def one(place, source=source, target=target, step=step):
            level = level_of(place)
            new = step_slab(
                source[place], source[place - 1], source[place + 1], keep_ref[place], mix_ref[...], levels_ref[...],
                level, depth_share(level, total_levels) * surface_ref[1],
            )
            if step < STEPS:
                target[place] = new
            else:
                index = place - HALO
                wet = levels_ref[0:rows, 0:columns] > level
                temp_ref[index] = jnp.where(wet, new[0:rows, 0:columns], temp_ref[index])

        if step < STEPS:
            in_order(jnp.where(gz == 0, HALO, step), layers + HALO - step, one)

            @pl.when(gz == 0)
            def _(target=target):
                target[HALO] = target[HALO] + top_forcing()
        else:
            leaving = []
            for start, size in pieces(layers):
                in_order(HALO + start, size, one)
                if start == 0:
                    @pl.when(gz == 0)
                    def _():
                        temp_ref[0] = temp_ref[0] + top_forcing()[0:rows, 0:columns]

                here = pl.ds(start, size)
                leaving += begin([(temp_ref.at[here], ocean_hbm.at[here])], semaphores, used)
                used += 1
            finish(leaving)
        source, target = target, source


def gather_kernel(sends_ref, returned_ref, surface_ref):
    me = lax.axis_index("gx") * lax.axis_size("gy") + lax.axis_index("gy")
    surface_ref[...] = jnp.zeros_like(surface_ref)
    blocks = sends_ref.shape[0]
    copies = returned_ref.shape[0] // blocks

    def one(block, carry):
        tile = sends_ref[me, block]
        place = jnp.maximum(tile, 0)
        got = returned_ref[pl.ds(block * copies, 1)]
        for copy in range(1, copies):
            got = got + returned_ref[pl.ds(block * copies + copy, 1)]
        surface_ref[pl.ds(place, 1)] += jnp.where(tile >= 0, got, 0.0)
        return carry

    lax.fori_loop(0, blocks, one, 0)


def call(body, outs, scratch, operands, places, out_places, cost=0):
    space = {"v": pltpu.VMEM, "s": pltpu.SMEM, "h": pl.ANY}
    assert len(places) == len(operands) and len(out_places) == len(outs)
    scratch_shapes = []
    for item in scratch:
        if isinstance(item, int):
            scratch_shapes.append(pltpu.SemaphoreType.DMA((item,)))
        elif isinstance(item, tuple):
            scratch_shapes.append(pltpu.VMEM(item, jnp.float32))
        else:
            scratch_shapes.append(item)
    return pl.pallas_call(
        body,
        out_shape=[jax.ShapeDtypeStruct(out, jnp.float32) for out in outs],
        in_specs=[pl.BlockSpec(memory_space=space[place]) for place in places],
        out_specs=[pl.BlockSpec(memory_space=space[place]) for place in out_places],
        scratch_shapes=scratch_shapes,
        compiler_params=pltpu.CompilerParams(vmem_limit_bytes=VMEM_LIMIT),
        cost_estimate=pl.CostEstimate(flops=cost, bytes_accessed=4 * cost // 16, transcendentals=0),
    )(*operands)


def like(array):
    return pltpu.VMEM(array.shape, array.dtype)


EDGES = [(dx, dy) for dx in (-1, 0, 1) for dy in (-1, 0, 1) if (dx, dy) != (0, 0)]


def toward(gx_count, gy_count, dx, dy):
    pairs = []
    for x in range(gx_count):
        for y in range(gy_count):
            if 0 <= x + dx < gx_count and 0 <= y + dy < gy_count:
                pairs.append(((x + dx) * gy_count + y + dy, x * gy_count + y))
    return pairs


def per_device(
    ocean_temp, bathy_levels, mixing, atm_flux, send_tiles, regrid_slots, regrid_weights
):
    layers, rows, columns = ocean_temp.shape
    gx_count, gy_count, gz_count = (lax.axis_size(axis) for axis in ALL_AXES)
    blocks = gx_count * gy_count
    own_tiles, fields, tile_atm = atm_flux.shape
    caps = send_tiles.shape[2]
    assert gz_count == 2 and caps == 1 and layers == GROUP and tile_atm == LANES
    assert columns == 2 * LANES and rows == 4 * TILE and regrid_weights.shape[2] == LANES
    total_levels = layers * gz_count
    few = blocks <= FEW
    sends = send_tiles.reshape(blocks, blocks)
    swap = [(0, 1), (1, 0)]
    tall = 2 * TILE + rows
    strip = (layers + 2, HALO, columns)
    slab = (rows + 2 * HALO, columns + LANES)
    slab_cost = 20 * slab[0] * slab[1]
    deep = (layers + 2 * HALO,) + slab

    high_rows = (2, layers, TILE, columns)
    low, high = call(
        rows_kernel, [strip, strip],
        [high_rows, pltpu.VMEM((2, TILE, columns), jnp.int32), (2, TILE, columns), 6],
        (ocean_temp, bathy_levels, mixing), "hhh", "vv", cost=slab_cost,
    )
    forward = [(i, i + 1) for i in range(gx_count - 1)]
    backward = [(target, source) for source, target in forward]
    before_rows = lax.ppermute(high, "gx", forward)
    after_rows = lax.ppermute(low, "gx", backward)
    outs = [(blocks, tall, LANES)] if few else [(blocks, TILE, LANES), (2, tall, LANES)]
    sides = 1 if few and gy_count == 2 else 2
    scratch = [
        pltpu.SMEM(sends.shape, jnp.int32), like(atm_flux), (sides, layers, rows, LANES),
        pltpu.VMEM((sides, rows, LANES), jnp.int32), (sides, rows, LANES), 2 + 3 * sides,
        (own_tiles, fields, LANES),
    ]
    sent = call(
        functools.partial(send_kernel, few=few, sides=sides), outs, scratch + ([(sides, tall, LANES)] if few else []),
        (sends, atm_flux, ocean_temp, bathy_levels, mixing, low), "hhhhhh", "v" * len(outs), cost=2 * slab_cost,
    )
    got = [lax.all_to_all(sent[0], BLOCKS_AXES, split_axis=0, concat_axis=0, tiled=True)]
    if not few:
        got.append(jnp.stack([
            lax.ppermute(sent[1][0 if dy > 0 else 1], BLOCKS_AXES, toward(gx_count, gy_count, dx, dy))
            for dx in (-1, 0, 1) for dy in (-1, 1)
        ]))

    strips = (4, 2 * TILE, LANES)
    packed_shape = (2, slab[0], LANES)
    partial, edges, shared, levels, mix, packed = call(
        functools.partial(regrid_kernel, few=few),
        [
            (fields, rows, columns), (2 * blocks, 2 * TILE, LANES) if few else strips,
            (TOP + HALO,) + slab, slab, slab, packed_shape,
        ],
        [
            pltpu.SMEM(regrid_slots.shape, jnp.int32), like(regrid_weights), (TOP + HALO, rows, columns),
            like(bathy_levels), like(mixing), slab, slab, packed_shape, 8 + CHUNKS,
            (rows * columns // LANES * TILE, LANES),
        ] + ([strips] if few else []),
        (
            regrid_slots, *got, regrid_weights, ocean_temp, bathy_levels, mixing, after_rows, before_rows,
        ), "h" + "v" * len(got) + "hhhhvv", "vvvhhh", cost=10 * slab_cost,
    )
    other_partial = lax.ppermute(partial, "gz", swap)
    other_shared = lax.ppermute(shared, "gz", swap)
    if few:
        edges = lax.all_to_all(edges, ALL_AXES, split_axis=0, concat_axis=0, tiled=True)
    else:
        choice = {-1: 1, 1: 0}
        around = jnp.stack([
            lax.ppermute(
                edges[choice[dx] if dx else (3 if dy < 0 else 2)], BLOCKS_AXES, toward(gx_count, gy_count, dx, dy)
            )
            for dx, dy in EDGES
        ])
        edges = jnp.stack([around, lax.ppermute(around, "gz", swap)], axis=1)
        edges = edges.reshape((2 * len(EDGES),) + strips[1:])

    top = (STEPS,) + slab
    parts = len(pieces(layers + HALO - 1))
    moved, keep, top_moved, top_keep = call(
        first_kernel, [deep, deep, top, top],
        [
            like(ocean_temp), strip, strip, packed_shape, (TOP + HALO,) + slab, slab, slab,
            deep, deep, top, top, deep, (TOP,) + slab, 9 + CHUNKS + parts,
        ],
        (ocean_temp, after_rows, before_rows, packed, other_shared, levels, mix), "h" * 7, "hhhh", cost=80 * slab_cost,
    )
    surface, back = call(
        functools.partial(skin_kernel, few=few, total_levels=total_levels),
        [(fields,) + slab, ((2 if few else 1) * blocks, LANES)],
        [
            pltpu.SMEM(regrid_slots.shape, jnp.int32), like(partial), like(partial), like(regrid_weights), slab, slab,
            top, top, (fields,) + slab, 8 + CHUNKS,
            top, top, (rows * columns // LANES, LANES), (regrid_weights.shape[0], LANES), (blocks, LANES),
        ],
        (regrid_slots, partial, other_partial, edges, regrid_weights, levels, mix, top_moved, top_keep),
        "hhhvhhhhh", "hv", cost=20 * slab_cost,
    )
    if few:
        returned = lax.all_to_all(back, ALL_AXES, split_axis=0, concat_axis=0, tiled=True)
    else:
        returned = lax.all_to_all(back, BLOCKS_AXES, split_axis=0, concat_axis=0, tiled=True)
        returned = returned + lax.ppermute(returned, "gz", swap)
    ocean, = call(
        functools.partial(ocean_kernel, total_levels=total_levels), [ocean_temp.shape],
        [like(ocean_temp), deep, slab, slab, (fields,) + slab, 5 + parts + len(pieces(layers)), deep, deep],
        (ocean_temp, moved, keep, levels, mix, surface), "h" * 6, "h", cost=120 * slab_cost,
    )
    atm_surface, = call(gather_kernel, [(own_tiles, LANES)], [], (sends, returned), "sv", "v", cost=slab_cost // 10)
    return (ocean, atm_surface)


def solution(mesh):
    return jax.shard_map(
        per_device,
        mesh=mesh,
        in_specs=(
            P(("ens", "gz"), "gx", "gy"),
            P(("ens", "gx"), "gy"),
            P(("ens", "gx"), "gy"),
            P(("ens", "gx", "gy"), None, None),
            P(),
            P(None, ("gx", "gy", "gz")),
            P(("gx", "gy", "gz"), None, None),
        ),
        out_specs=(P(("ens", "gz"), "gx", "gy"), P(("ens", "gx", "gy"), None)),
        check_vma=False,
    )
```

```python
import functools

import jax
import jax.numpy as jnp
from jax import lax
from jax.experimental import pallas as pl
from jax.experimental.pallas import tpu as pltpu
from jax.sharding import PartitionSpec as P

STEPS = 4
HALO = STEPS
WIDTH = STEPS - 1
TOP = STEPS + 1
LANES = 128
TILE = 8
GROUP = LANES // HALO
FEW = 16
UNROLL = 8
CHUNKS = 4
BLOCKS_AXES = ("gx", "gy")
ALL_AXES = ("gx", "gy", "gz")
VMEM_LIMIT = 60 * 1024 * 1024


def position_of(few, dx, dy):
    if not few:
        return (dx + 1) * 2 + (1 if dy > 0 else 0)
    gx_count, gy_count = lax.axis_size("gx"), lax.axis_size("gy")
    x = jnp.clip(lax.axis_index("gx") + dx, 0, gx_count - 1)
    y = jnp.clip(lax.axis_index("gy") + dy, 0, gy_count - 1)
    return x * gy_count + y


def side_tile(left, right, index):
    lane = lax.broadcasted_iota(jnp.int32, left.shape, 1)
    from_right = pltpu.roll(right, lax.rem(LANES - HALO * index, LANES), 1)
    from_left = pltpu.roll(left, lax.rem(2 * LANES - HALO - HALO * index, LANES), 1)
    zero = jnp.zeros_like(left)
    return jnp.where(lane < HALO, from_right, jnp.where(lane >= LANES - HALO, from_left, zero))


def put_slab(ref, own, after, before, tile):
    rows, columns = own.shape
    ref[0:rows, 0:columns] = own
    ref[rows : rows + HALO, 0:columns] = after
    ref[rows + HALO : rows + 2 * HALO, 0:columns] = before
    ref[:, columns:] = tile


def wet_around(levels, level):
    rows, lanes = levels.shape
    wet = jnp.where(levels > level, 0.1, 0.0)
    total = pltpu.roll(wet, 1, 0) + pltpu.roll(wet, rows - 1, 0)
    return total + (pltpu.roll(wet, 1, 1) + pltpu.roll(wet, lanes - 1, 1))


def keep_share(levels, mixing, level):
    above = jnp.where(level > 0.0, 1.0, 0.0)
    vertical = above + jnp.where(levels > level + 1.0, 1.0, 0.0)
    return 1.0 - wet_around(levels, level) - mixing * vertical


def step_slab(center, over, under, keep, mixing, levels, level, forcing):
    rows, lanes = center.shape
    lateral = pltpu.roll(center, 1, 0) + pltpu.roll(center, rows - 1, 0)
    lateral = lateral + (pltpu.roll(center, 1, 1) + pltpu.roll(center, lanes - 1, 1))
    if forcing is not None:
        lateral = lateral + forcing
    new = center * keep + 0.1 * lateral + mixing * (over + under)
    return jnp.where(levels > level, new, 0.0)


def last_slab(center, over, under, keep, mixing, forcing):
    rows, columns = over.shape
    tall, lanes = center.shape
    own = slice(0, rows), slice(0, columns)
    lateral = pltpu.roll(center, 1, 0)[own] + pltpu.roll(center, tall - 1, 0)[own]
    lateral = lateral + (pltpu.roll(center[0:rows], 1, 1)[own] + pltpu.roll(center[0:rows], lanes - 1, 1)[own])
    return center[own] * keep + 0.1 * (lateral + forcing) + mixing * (over + under)


def depth_share(level, total_levels):
    return jnp.exp(jnp.full((1, 1), -4.0 / total_levels, jnp.float32) * level)


def begin(copies, semaphores, first=0):
    started = []
    for index, (source, target) in enumerate(copies):
        copy = pltpu.make_async_copy(source, target, semaphores.at[first + index])
        copy.start()
        started.append(copy)
    return started


def finish(copies):
    for copy in copies:
        copy.wait()


def in_order(start, count, body):
    whole = count // UNROLL

    def group(index, carry):
        for offset in range(UNROLL):
            body(start + index * UNROLL + offset)
        return carry

    lax.fori_loop(0, whole, group, 0)
    for index in range(whole * UNROLL, count):
        body(start + index)


def rows_kernel(temp_ref, bathy_ref, mixing_ref, one_ref, two_ref, temp_rows, bathy_rows, mixing_rows, semaphores):
    layers, rows, columns = temp_ref.shape
    copies = []
    for side in range(2):
        part = pl.ds(side * (rows - TILE), TILE)
        copies += [(temp_ref.at[:, part], temp_rows.at[side]), (bathy_ref.at[part], bathy_rows.at[side])]
        copies += [(mixing_ref.at[part], mixing_rows.at[side])]
    finish(begin(copies, semaphores))
    even = lax.rem(lax.axis_index("gx"), 2) == 0
    fields = [
        (slice(0, layers), lambda side: temp_rows[side]), (layers, lambda side: bathy_rows[side].astype(jnp.float32)),
        (layers + 1, lambda side: mixing_rows[side]),
    ]
    for place, read in fields:
        low, high = read(0)[..., 0:HALO, :], read(1)[..., TILE - HALO :, :]
        one_ref[place] = jnp.where(even, high, low)
        two_ref[place] = jnp.where(even, low, high)


def send_kernel(sends_hbm, flux_hbm, temp_hbm, bathy_hbm, mixing_hbm, *refs, few, sides):
    if few:
        message_ref, sends_ref, flux_ref, temp_ref, bathy_ref, mixing_ref, semaphores, flux_scratch, strips_ref = refs
        fluxes_ref = message_ref
    else:
        (
            fluxes_ref, strips_ref, sends_ref, flux_ref, temp_ref, bathy_ref, mixing_ref, semaphores, flux_scratch,
        ) = refs
    layers, rows, columns = temp_hbm.shape
    gy, gy_count = lax.axis_index("gy"), lax.axis_size("gy")
    me = lax.axis_index("gx") * gy_count + gy
    copies = [(sends_hbm, sends_ref), (flux_hbm, flux_ref)]
    for place in range(sides):
        side = 1 - gy if sides == 1 else place
        window = pl.ds(pl.multiple_of(side * (columns - LANES), LANES), LANES)
        copies += [(bathy_hbm.at[:, window], bathy_ref.at[place]), (mixing_hbm.at[:, window], mixing_ref.at[place])]
        copies += [(temp_hbm.at[:, :, window], temp_ref.at[place])]
    copies = begin(copies, semaphores)
    lane = lax.broadcasted_iota(jnp.int32, (rows, LANES), 1)
    short = lax.broadcasted_iota(jnp.int32, (TILE, LANES), 1)
    finish(copies)
    for side in range(sides):
        base = HALO * (1 - gy) if sides == 1 else HALO * side
        strip = jnp.zeros((rows, LANES), jnp.float32)
        for index in range(layers):
            place = HALO * index
            moved = pltpu.roll(temp_ref[side, index], lax.rem(place + base, LANES), 1)
            strip = jnp.where((lane >= place) & (lane < place + HALO), moved, strip)
        strips_ref[side, 2 * TILE : 2 * TILE + rows] = strip
        plain = jnp.zeros((TILE, LANES), jnp.float32)
        for part in range(rows // TILE):
            here = slice(part * TILE, (part + 1) * TILE)
            for which, values in enumerate((bathy_ref[side, here].astype(jnp.float32), mixing_ref[side, here])):
                place = 2 * HALO * part + HALO * which
                moved = pltpu.roll(values, lax.rem(place + base, LANES), 1)
                plain = jnp.where((short >= place) & (short < place + HALO), moved, plain)
        strips_ref[side, TILE : 2 * TILE] = plain
        strips_ref[side, 0:TILE] = jnp.zeros((TILE, LANES), jnp.float32)
    flux_scratch[...] = flux_ref[...].astype(jnp.float32)
    fields = flux_ref.shape[1]

    def one(block, carry):
        tile = sends_ref[me, block]
        if few:
            side = 0 if sides == 1 else (lax.rem(block, gy_count) > gy).astype(jnp.int32)
            message_ref[block] = strips_ref[side]
        else:
            fluxes_ref[block] = jnp.zeros(fluxes_ref.shape[1:], jnp.float32)
        sent = jnp.where(tile >= 0, flux_scratch[jnp.maximum(tile, 0)], 0.0)
        fluxes_ref[block, 0:fields] = sent
        return carry

    if few:
        for block in range(fluxes_ref.shape[0]):
            one(block, 0)
    else:
        lax.fori_loop(0, fluxes_ref.shape[0], one, 0)


def regrid_kernel(
    slots_hbm, flux_hbm, weights_hbm, partial_hbm, edges_ref,
    slots_ref, flux_ref, weights_ref, partial_ref, semaphores, sums_ref, *strip_scratch, few,
):
    fields, rows, columns = partial_ref.shape
    slot_count, tile_atm, patch = weights_ref.shape
    halves = columns // LANES
    needed = begin([(slots_hbm, slots_ref), (flux_hbm.at[:, pl.ds(0, TILE)], flux_ref)], semaphores)
    chunk = slot_count // CHUNKS
    arriving = begin([
        (weights_hbm.at[pl.ds(part * chunk, chunk)], weights_ref.at[pl.ds(part * chunk, chunk)])
        for part in range(CHUNKS)
    ], semaphores, len(needed))
    sums_ref[...] = jnp.zeros_like(sums_ref)
    finish(needed)
    for slot in range(slot_count):
        if slot % chunk == 0:
            arriving[slot // chunk].wait()
        fluxes = flux_ref[slots_ref[0, slot]].astype(jnp.bfloat16)
        got = jnp.dot(fluxes, weights_ref[slot], preferred_element_type=jnp.float32)
        place = pl.multiple_of(slots_ref[1, slot] * TILE, TILE)
        sums_ref[pl.ds(place, TILE)] += got

    strips_ref = strip_scratch[0] if few else edges_ref
    strips_ref[...] = jnp.zeros_like(strips_ref)
    short = lax.broadcasted_iota(jnp.int32, (TILE, LANES), 1)
    columns_low = jnp.zeros((TILE, LANES), jnp.float32)
    columns_high = jnp.zeros((TILE, LANES), jnp.float32)
    for field in range(2):
        for half in range(halves):
            values = sums_ref[pl.ds(half * TILE + field, rows, stride=halves * TILE), :]
            partial_ref[field, :, half * LANES : (half + 1) * LANES] = values
            place = (field * 2 + half) * HALO
            strips_ref[0, place : place + WIDTH] = values[0:WIDTH]
            strips_ref[1, place : place + WIDTH] = values[rows - WIDTH : rows]
            for part in range(rows // TILE):
                block = values[part * TILE : (part + 1) * TILE]
                place = 2 * HALO * part + HALO * field
                inside = (short >= place) & (short < place + HALO)
                if half == 0:
                    columns_low = jnp.where(inside, pltpu.roll(block, place % LANES, 1), columns_low)
                if half == halves - 1:
                    columns_high = jnp.where(inside, pltpu.roll(block, (place + HALO) % LANES, 1), columns_high)
    leaving = begin([(partial_ref, partial_hbm)], semaphores, len(needed) + CHUNKS)
    strips_ref[2, 0:TILE] = columns_low
    strips_ref[3, 0:TILE] = columns_high
    if few:
        gx, gy, gy_count = lax.axis_index("gx"), lax.axis_index("gy"), lax.axis_size("gy")
        for entry in range(edges_ref.shape[0]):
            x, y = entry // 2 // gy_count, entry // 2 % gy_count
            choice = jnp.where(x < gx, 0, jnp.where(x > gx, 1, jnp.where(y < gy, 2, 3)))
            edges_ref[entry] = strips_ref[choice]

    finish(leaving)


def halo_kernel(
    sides_hbm, temp_hbm, bathy_hbm, mixing_hbm, one_hbm, two_hbm, after_ref,
    shared_ref, levels_hbm, mix_hbm, packed_hbm,
    sides_ref, temp_ref, bathy_ref, mixing_ref, pair_ref, levels_ref, mix_ref, packed_ref, semaphores, *, few,
):
    layers, rows, columns = temp_hbm.shape
    lasts = pl.ds(layers - HALO, HALO)
    needed = begin([
        (sides_hbm, sides_ref), (temp_hbm.at[pl.ds(0, TOP)], temp_ref.at[pl.ds(0, TOP)]),
        (temp_hbm.at[lasts], temp_ref.at[pl.ds(TOP, HALO)]), (bathy_hbm, bathy_ref), (mixing_hbm, mixing_ref),
        (one_hbm, pair_ref.at[0]), (two_hbm, pair_ref.at[1]),
    ], semaphores)
    odd = lax.rem(lax.axis_index("gx"), 2)
    next_ref, prev_ref = pair_ref.at[odd], pair_ref.at[1 - odd]
    finish(needed)
    gx, gx_count = lax.axis_index("gx"), lax.axis_size("gx")
    gy, gy_count = lax.axis_index("gy"), lax.axis_size("gy")
    plain = []
    for side, dy in ((0, -1), (1, 1)):
        own, after, before = (position_of(few, dx, dy) for dx in (0, 1, -1))
        packed_ref[side, 0:rows] = sides_ref[own, 2 * TILE : 2 * TILE + rows]
        packed_ref[side, rows : rows + HALO] = sides_ref[after, 2 * TILE : 2 * TILE + HALO]
        packed_ref[side, rows + HALO :] = sides_ref[before, 2 * TILE + rows - HALO : 2 * TILE + rows]
        tile = sides_ref[own, TILE : 2 * TILE]
        parts = [tile] + [pltpu.roll(tile, LANES - 2 * HALO * part, 1) for part in range(1, rows // TILE)]
        last = pltpu.roll(sides_ref[before, TILE : 2 * TILE], LANES - 2 * HALO * (rows // TILE - 1), 1)
        row = lax.broadcasted_iota(jnp.int32, (TILE, LANES), 0)
        parts.append(jnp.where(row < HALO, sides_ref[after, TILE : 2 * TILE], last))
        plain.append(jnp.concatenate(parts, axis=0))
    size = (rows + 2 * HALO, LANES)
    lane, row = (lax.broadcasted_iota(jnp.int32, size, dim) for dim in (1, 0))
    there = (lane < HALO) & (gy < gy_count - 1) | (lane >= HALO) & (gy > 0)
    there = there & ((row < rows) | (row < rows + HALO) & (gx < gx_count - 1) | (row >= rows + HALO) & (gx > 0))
    tile = jnp.where(there, side_tile(plain[0], plain[1], 0), 0.0)
    put_slab(levels_ref, bathy_ref[...].astype(jnp.float32), next_ref[layers], prev_ref[layers], tile)
    tile = side_tile(plain[0], plain[1], 1)
    put_slab(mix_ref, mixing_ref[...], next_ref[layers + 1], prev_ref[layers + 1], tile)
    leaving = begin(
        [(levels_ref, levels_hbm), (mix_ref, mix_hbm), (packed_ref, packed_hbm)], semaphores, len(needed)
    )
    for place, level in enumerate(list(range(TOP)) + list(range(layers - HALO, layers))):
        tile = side_tile(packed_ref[0], packed_ref[1], level)
        put_slab(shared_ref.at[place], temp_ref[place], next_ref[level], prev_ref[level], tile)
    finish(leaving)


def first_kernel(
    temp_hbm, one_hbm, two_hbm, packed_hbm, other_hbm, levels_hbm, mix_hbm,
    moved_hbm, keep_hbm, top_hbm, top_keep_hbm,
    temp_ref, pair_ref, packed_ref, other_ref, levels_ref, mix_ref,
    moved_ref, keep_ref, top_ref, top_keep_ref, first_ref, skin_ref, semaphores,
):
    layers = temp_hbm.shape[0]
    gz = lax.axis_index("gz")
    first_level = gz * layers - HALO
    needed = begin([
        (one_hbm, pair_ref.at[0]), (two_hbm, pair_ref.at[1]), (packed_hbm, packed_ref), (levels_hbm, levels_ref),
        (mix_hbm, mix_ref), (other_hbm, other_ref),
    ], semaphores)
    chunk = layers // CHUNKS
    parts = [pl.ds(part * chunk, chunk) for part in range(CHUNKS)]
    used = len(needed)
    arriving = begin([(temp_hbm.at[part], temp_ref.at[part]) for part in parts], semaphores, used)
    used += CHUNKS
    odd = lax.rem(lax.axis_index("gx"), 2)
    next_ref, prev_ref = pair_ref.at[odd], pair_ref.at[1 - odd]
    finish(needed)

    def level_of(place):
        return (first_level + place).astype(jnp.float32)

    def settle(place):
        level = level_of(place)
        first_ref[place] = jnp.where(levels_ref[...] > level, first_ref[place], 0.0)
        keep_ref[place] = keep_share(levels_ref[...], mix_ref[...], level)

    def own_level(index):
        tile = side_tile(packed_ref[0], packed_ref[1], index)
        put_slab(first_ref.at[index + HALO], temp_ref[index], next_ref[index], prev_ref[index], tile)
        settle(index + HALO)

    for part in range(CHUNKS):
        arriving[part].wait()
        in_order(part * chunk, chunk, own_level)

    for index in range(HALO):
        slot = jnp.where(gz == 0, index, TOP + index)
        place = jnp.where(gz == 0, HALO + layers + index, index)
        first_ref[place] = other_ref[slot]
        settle(place)

    base = jnp.where(gz == 0, HALO, 1)
    count = layers + HALO - 1
    span = pl.ds(base, count)
    leaving = begin([(keep_ref.at[span], keep_hbm.at[span])], semaphores, used)
    used += 1
    levels = levels_ref[...]
    for level in range(TOP):
        slab = jnp.where(gz == 0, first_ref[HALO + level], other_ref[level])
        skin_ref[level] = jnp.where(levels > float(level), slab, 0.0)
    for level in range(STEPS):
        top_keep_ref[level] = keep_share(levels, mix_ref[...], jnp.float32(level))
        over = skin_ref[level - 1] if level else jnp.zeros_like(levels)
        top_ref[level] = step_slab(
            skin_ref[level], over, skin_ref[level + 1], top_keep_ref[level], mix_ref[...], levels, float(level), None
        )
    leaving += begin([(top_ref, top_hbm), (top_keep_ref, top_keep_hbm)], semaphores, used)
    used += 2
    edge = jnp.where(gz == 0, HALO - 1, HALO + layers)
    first_ref[edge] = jnp.zeros_like(first_ref[0])

    def one(place):
        moved_ref[place] = step_slab(
            first_ref[place], first_ref[place - 1], first_ref[place + 1], keep_ref[place], mix_ref[...],
            levels_ref[...], level_of(place), None,
        )

    for start, size in pieces(count):
        in_order(base + start, size, one)
        here = pl.ds(base + start, size)
        leaving += begin([(moved_ref.at[here], moved_hbm.at[here])], semaphores, used)
        used += 1
    finish(leaving)


def pieces(count):
    return [(start, min(UNROLL, count - start)) for start in range(0, count, UNROLL)]


def skin_kernel(
    sends_hbm, slots_hbm, partial_hbm, other_hbm, edges_hbm, weights_hbm, levels_hbm, mix_hbm, top_hbm, top_keep_hbm,
    surface_hbm, back_ref,
    sends_ref, slots_ref, partial_ref, other_ref, edges_ref, weights_ref, levels_ref, mix_ref, top_ref, top_keep_ref, surface_ref, semaphores,
    first_ref, second_ref, sst_ref, rows_ref, *sums_scratch, few, total_levels,
):
    fields, rows, columns = partial_ref.shape
    slot_count, tile_atm, patch = weights_ref.shape
    halves = columns // LANES
    needed = begin([
        (partial_hbm, partial_ref), (other_hbm, other_ref), (levels_hbm, levels_ref), (mix_hbm, mix_ref),
        (top_hbm, top_ref), (top_keep_hbm, top_keep_ref), (slots_hbm, slots_ref),
        (sends_hbm, sends_ref), (edges_hbm, edges_ref),
    ], semaphores)
    chunk = slot_count // CHUNKS
    used = len(needed)
    arriving = begin([
        (weights_hbm.at[pl.ds(part * chunk, chunk)], weights_ref.at[pl.ds(part * chunk, chunk)])
        for part in range(CHUNKS)
    ], semaphores, used)
    used += CHUNKS

    def edge(dx, dy):
        if few:
            where = position_of(few, dx, dy)
            return edges_ref[2 * where] + edges_ref[2 * where + 1]
        where = EDGES.index((dx, dy))
        return edges_ref[2 * where] + edges_ref[2 * where + 1]

    finish(needed)
    after, before = edge(1, 0), edge(-1, 0)
    right, left = edge(0, 1), edge(0, -1)
    corners = {(dx, dy): edge(dx, dy) for dx in (1, -1) for dy in (1, -1)}
    lane = lax.broadcasted_iota(jnp.int32, (TILE, LANES), 1)
    short = lax.broadcasted_iota(jnp.int32, (HALO, LANES), 1)
    surface_ref[...] = jnp.zeros_like(surface_ref)
    for field in range(fields):
        surface_ref[field, 0:rows, 0:columns] = partial_ref[field] + other_ref[field]
        for half in range(halves):
            place = (field * 2 + half) * HALO
            here = slice(half * LANES, (half + 1) * LANES)
            surface_ref[field, rows : rows + WIDTH, here] = after[place : place + WIDTH]
            surface_ref[field, rows + 2 * HALO - WIDTH :, here] = before[place : place + WIDTH]
        for part in range(rows // TILE):
            place = 2 * HALO * part + HALO * field
            from_right = pltpu.roll(right[0:TILE], (LANES - place) % LANES, 1)
            from_left = pltpu.roll(left[0:TILE], (2 * LANES - HALO - place) % LANES, 1)
            tile = jnp.where(lane < HALO, from_right, jnp.where(lane >= LANES - HALO, from_left, 0.0))
            surface_ref[field, part * TILE : (part + 1) * TILE, columns:] = tile
        low, high = field * 2 * HALO, (field * 2 + halves - 1) * HALO
        for dx in (1, -1):
            from_right, from_left = corners[dx, 1][low : low + HALO], corners[dx, -1][high : high + HALO]
            tile = jnp.where(short < HALO, from_right, jnp.where(short >= LANES - HALO, from_left, 0.0))
            if dx == 1:
                surface_ref[field, rows : rows + WIDTH, columns:] = tile[0:WIDTH]
            else:
                surface_ref[field, rows + 2 * HALO - WIDTH :, columns:] = tile[0:WIDTH]

    leaving = begin([(surface_ref, surface_hbm)], semaphores, used)
    levels = levels_ref[...]
    forcings = [depth_share(jnp.float32(level), total_levels) * surface_ref[1] for level in range(STEPS)]
    forcings[0] = forcings[0] + surface_ref[0]
    for level in range(STEPS):
        first_ref[level] = top_ref[level] + jnp.where(levels > float(level), 0.1 * forcings[level], 0.0)
    source, target = first_ref, second_ref
    zero = jnp.zeros_like(levels)
    for step in range(2, STEPS + 1):
        for level in range(TOP - step):
            over = source[level - 1] if level else zero
            target[level] = step_slab(
                source[level], over, source[level + 1], top_keep_ref[level], mix_ref[...], levels, float(level),
                forcings[level],
            )
        source, target = target, source
    for half in range(halves):
        values = source[0, 0:rows, half * LANES : (half + 1) * LANES]
        sst_ref[half * rows : (half + 1) * rows] = values.astype(jnp.bfloat16).astype(jnp.float32)

    for slot in range(slot_count):
        tile = slots_ref[1, slot]
        place = lax.rem(tile, halves) * rows + lax.div(tile, halves)
        rows_ref[pl.ds(slot, 1)] = sst_ref[pl.ds(place, 1)]
    sums_ref = sums_scratch[0]
    sums_ref[...] = jnp.zeros_like(sums_ref)
    for group in range(slot_count // TILE):
        given = rows_ref[group * TILE : (group + 1) * TILE].astype(jnp.bfloat16)
        for row in range(TILE):
            slot = group * TILE + row
            if slot % chunk == 0:
                arriving[slot // chunk].wait()
            got = lax.dot_general(
                given, weights_ref[slot], (((1,), (1,)), ((), ())), preferred_element_type=jnp.float32
            )
            sums_ref[pl.ds(slots_ref[0, slot], 1)] += got[row : row + 1]
    me = lax.axis_index("gx") * lax.axis_size("gy") + lax.axis_index("gy")
    blocks = sums_ref.shape[0]
    copies = back_ref.shape[0] // blocks

    def place_rows(block):
        tile = sends_ref[block, me]
        back_ref[pl.ds(block * copies, copies)] = jnp.zeros((copies,) + back_ref.shape[1:], jnp.float32)

        @pl.when(tile >= 0)
        def _():
            for copy in range(copies):
                back_ref[block * copies + copy, pl.ds(tile, 1)] = sums_ref[pl.ds(block, 1)]

    if few:
        for block in range(blocks):
            place_rows(block)
    else:
        lax.fori_loop(0, blocks, lambda block, carry: (place_rows(block), carry)[1], 0)
    finish(leaving)


def ocean_kernel(
    temp_hbm, moved_hbm, keep_hbm, levels_hbm, mix_hbm, surface_hbm, ocean_hbm,
    temp_ref, keep_ref, levels_ref, mix_ref, surface_ref, semaphores, first_ref, second_ref, *, total_levels,
):
    layers, rows, columns = temp_hbm.shape
    gz = lax.axis_index("gz")
    first_level = gz * layers - HALO
    base = jnp.where(gz == 0, HALO, 1)
    count = layers + HALO - 1
    needed = begin(
        [(levels_hbm, levels_ref), (mix_hbm, mix_ref), (surface_hbm, surface_ref)], semaphores
    )
    used = len(needed)
    spans = [pl.ds(base + start, size) for start, size in pieces(count)]
    arriving = begin([(moved_hbm.at[span], first_ref.at[span]) for span in spans], semaphores, used)
    used += len(spans)
    later = begin([
        (keep_hbm.at[pl.ds(base, count)], keep_ref.at[pl.ds(base, count)]), (temp_hbm, temp_ref)
    ], semaphores, used)
    used += len(later)
    edge = jnp.where(gz == 0, HALO - 1, HALO + layers)
    first_ref[edge] = jnp.zeros_like(first_ref[0])
    second_ref[edge] = jnp.zeros_like(first_ref[0])
    finish(needed)

    def level_of(place):
        return (first_level + place).astype(jnp.float32)

    def add(place):
        level = level_of(place)
        forcing = (0.1 * depth_share(level, total_levels)) * surface_ref[1]
        first_ref[place] = first_ref[place] + jnp.where(levels_ref[...] > level, forcing, 0.0)

    for (start, size), copy in zip(pieces(count), arriving):
        copy.wait()
        in_order(base + start, size, add)

    def top_forcing():
        return jnp.where(levels_ref[...] > 0.0, 0.1 * surface_ref[0], 0.0)

    @pl.when(gz == 0)
    def _():
        first_ref[HALO] = first_ref[HALO] + top_forcing()

    later[0].wait()
    source, target = first_ref, second_ref
    for step in range(2, STEPS + 1):
        if step == STEPS:
            later[1].wait()

        def one(place, source=source, target=target, step=step):
            level = level_of(place)
            share = depth_share(level, total_levels)
            if step < STEPS:
                target[place] = step_slab(
                    source[place], source[place - 1], source[place + 1], keep_ref[place], mix_ref[...],
                    levels_ref[...], level, share * surface_ref[1],
                )
            else:
                own = slice(0, rows), slice(0, columns)
                new = last_slab(
                    source[place], source[(place - 1,) + own], source[(place + 1,) + own], keep_ref[(place,) + own],
                    mix_ref[own], share * surface_ref[(1,) + own],
                )
                index = place - HALO
                temp_ref[index] = jnp.where(levels_ref[own] > level, new, temp_ref[index])

        if step < STEPS:
            in_order(jnp.where(gz == 0, HALO, step), layers + HALO - step, one)

            @pl.when(gz == 0)
            def _(target=target):
                target[HALO] = target[HALO] + top_forcing()
        else:
            leaving = []
            for start, size in pieces(layers):
                in_order(HALO + start, size, one)
                if start == 0:
                    @pl.when(gz == 0)
                    def _():
                        temp_ref[0] = temp_ref[0] + top_forcing()[0:rows, 0:columns]

                here = pl.ds(start, size)
                leaving += begin([(temp_ref.at[here], ocean_hbm.at[here])], semaphores, used)
                used += 1
            finish(leaving)
        source, target = target, source


def call(body, outs, scratch, operands, places, out_places, cost=0):
    space = {"v": pltpu.VMEM, "s": pltpu.SMEM, "h": pl.ANY}
    assert len(places) == len(operands) and len(out_places) == len(outs)
    scratch_shapes = []
    for item in scratch:
        if isinstance(item, int):
            scratch_shapes.append(pltpu.SemaphoreType.DMA((item,)))
        elif isinstance(item, tuple):
            scratch_shapes.append(pltpu.VMEM(item, jnp.float32))
        else:
            scratch_shapes.append(item)
    return pl.pallas_call(
        body,
        out_shape=[jax.ShapeDtypeStruct(out, jnp.float32) for out in outs],
        in_specs=[pl.BlockSpec(memory_space=space[place]) for place in places],
        out_specs=[pl.BlockSpec(memory_space=space[place]) for place in out_places],
        scratch_shapes=scratch_shapes,
        compiler_params=pltpu.CompilerParams(vmem_limit_bytes=VMEM_LIMIT),
        cost_estimate=pl.CostEstimate(flops=cost, bytes_accessed=4 * cost // 16, transcendentals=0),
    )(*operands)


def like(array):
    return pltpu.VMEM(array.shape, array.dtype)


EDGES = [(dx, dy) for dx in (-1, 0, 1) for dy in (-1, 0, 1) if (dx, dy) != (0, 0)]


def toward(gx_count, gy_count, dx, dy):
    pairs = []
    for x in range(gx_count):
        for y in range(gy_count):
            if 0 <= x + dx < gx_count and 0 <= y + dy < gy_count:
                pairs.append(((x + dx) * gy_count + y + dy, x * gy_count + y))
    return pairs


def per_device(
    ocean_temp, bathy_levels, mixing, atm_flux, send_tiles, regrid_slots, regrid_weights
):
    layers, rows, columns = ocean_temp.shape
    gx_count, gy_count, gz_count = (lax.axis_size(axis) for axis in ALL_AXES)
    blocks = gx_count * gy_count
    own_tiles, fields, tile_atm = atm_flux.shape
    caps = send_tiles.shape[2]
    assert gz_count == 2 and caps == 1 and layers == GROUP and tile_atm == LANES
    assert columns == 2 * LANES and rows == 4 * TILE and regrid_weights.shape[2] == LANES
    total_levels = layers * gz_count
    few = blocks <= FEW
    sends = send_tiles.reshape(blocks, blocks)
    swap = [(0, 1), (1, 0)]
    tall = 2 * TILE + rows
    strip = (layers + 2, HALO, columns)
    slab = (rows + 2 * HALO, columns + LANES)
    slab_cost = 20 * slab[0] * slab[1]
    deep = (layers + 2 * HALO,) + slab

    high_rows = (2, layers, TILE, columns)
    one, two = call(
        rows_kernel, [strip, strip],
        [high_rows, pltpu.VMEM((2, TILE, columns), jnp.int32), (2, TILE, columns), 6],
        (ocean_temp, bathy_levels, mixing), "hhh", "vv", cost=slab_cost,
    )
    rows_one, rows_two = (
        lax.ppermute(part, "gx", [
            pair for x in range(start, gx_count - 1, 2) for pair in ((x, x + 1), (x + 1, x))
        ]) for start, part in enumerate((one, two))
    )

    outs = [(blocks, tall, LANES)] if few else [(blocks, TILE, LANES), (2, tall, LANES)]
    sides = 1 if few and gy_count == 2 else 2
    scratch = [
        pltpu.SMEM(sends.shape, jnp.int32), like(atm_flux), (sides, layers, rows, LANES),
        pltpu.VMEM((sides, rows, LANES), jnp.int32), (sides, rows, LANES), 2 + 3 * sides,
        (own_tiles, fields, LANES),
    ]
    sent = call(
        functools.partial(send_kernel, few=few, sides=sides), outs, scratch + ([(sides, tall, LANES)] if few else []),
        (sends, atm_flux, ocean_temp, bathy_levels, mixing), "hhhhh", "v" * len(outs), cost=2 * slab_cost,
    )
    got = [lax.all_to_all(sent[0], BLOCKS_AXES, split_axis=0, concat_axis=0, tiled=True)]
    if not few:
        got.append(jnp.stack([
            lax.ppermute(sent[1][0 if dy > 0 else 1], BLOCKS_AXES, toward(gx_count, gy_count, dx, dy))
            for dx in (-1, 0, 1) for dy in (-1, 1)
        ]))

    strips = (4, 2 * TILE, LANES)
    packed_shape = (2, slab[0], LANES)
    pair_shape = (2,) + strip
    partial, edges = call(
        functools.partial(regrid_kernel, few=few),
        [(fields, rows, columns), (2 * blocks, 2 * TILE, LANES) if few else strips],
        [
            pltpu.SMEM(regrid_slots.shape, jnp.int32), (blocks, TILE, LANES), like(regrid_weights),
            (fields, rows, columns), 3 + CHUNKS, (rows * columns // LANES * TILE, LANES),
        ] + ([strips] if few else []),
        (regrid_slots, got[0], regrid_weights), "hhh", "hv", cost=4 * slab_cost,
    )
    shared, levels, mix, packed = call(
        functools.partial(halo_kernel, few=few),
        [(TOP + HALO,) + slab, slab, slab, packed_shape],
        [
            got[-1].shape, (TOP + HALO, rows, columns), like(bathy_levels), like(mixing), pair_shape, slab, slab,
            packed_shape, 10,
        ],
        (got[-1], ocean_temp, bathy_levels, mixing, rows_one, rows_two, partial), "h" * 7, "vhhh", cost=slab_cost,
    )
    other_partial = lax.ppermute(partial, "gz", swap)
    other_shared = lax.ppermute(shared, "gz", swap)
    if few:
        edges = lax.all_to_all(edges, ALL_AXES, split_axis=0, concat_axis=0, tiled=True)
    else:
        choice = {-1: 1, 1: 0}
        around = jnp.stack([
            lax.ppermute(
                edges[choice[dx] if dx else (3 if dy < 0 else 2)], BLOCKS_AXES, toward(gx_count, gy_count, dx, dy)
            )
            for dx, dy in EDGES
        ])
        edges = jnp.stack([around, lax.ppermute(around, "gz", swap)], axis=1)
        edges = edges.reshape((2 * len(EDGES),) + strips[1:])

    top = (STEPS,) + slab
    parts = len(pieces(layers + HALO - 1))
    moved, keep, top_moved, top_keep = call(
        first_kernel, [deep, deep, top, top],
        [
            like(ocean_temp), pair_shape, packed_shape, (TOP + HALO,) + slab, slab, slab,
            deep, deep, top, top, deep, (TOP,) + slab, 9 + CHUNKS + parts,
        ],
        (ocean_temp, rows_one, rows_two, packed, other_shared, levels, mix), "h" * 7, "hhhh", cost=slab_cost,
    )
    surface, back = call(
        functools.partial(skin_kernel, few=few, total_levels=total_levels),
        [(fields,) + slab, ((2 if few else 1) * blocks, own_tiles, LANES)],
        [
            pltpu.SMEM(sends.shape, jnp.int32), pltpu.SMEM(regrid_slots.shape, jnp.int32), like(partial), like(partial),
            edges.shape, like(regrid_weights), slab, slab, top, top, (fields,) + slab, 10 + CHUNKS,
            top, top, (rows * columns // LANES, LANES), (regrid_weights.shape[0], LANES), (blocks, LANES),
        ],
        (sends, regrid_slots, partial, other_partial, edges, regrid_weights, levels, mix, top_moved, top_keep),
        "hhhhhhhhhh", "hv", cost=20 * slab_cost,
    )
    if few:
        returned = lax.all_to_all(back, ALL_AXES, split_axis=0, concat_axis=0, tiled=True)
    else:
        returned = lax.all_to_all(back, BLOCKS_AXES, split_axis=0, concat_axis=0, tiled=True)
        returned = returned + lax.ppermute(returned, "gz", swap)
    ocean, = call(
        functools.partial(ocean_kernel, total_levels=total_levels), [ocean_temp.shape],
        [like(ocean_temp), deep, slab, slab, (fields,) + slab, 5 + parts + len(pieces(layers)), deep, deep],
        (ocean_temp, moved, keep, levels, mix, surface), "h" * 6, "h", cost=120 * slab_cost,
    )
    atm_surface = returned.sum(axis=0)
    return (ocean, atm_surface)


def solution(mesh):
    return jax.shard_map(
        per_device,
        mesh=mesh,
        in_specs=(
            P(("ens", "gz"), "gx", "gy"),
            P(("ens", "gx"), "gy"),
            P(("ens", "gx"), "gy"),
            P(("ens", "gx", "gy"), None, None),
            P(),
            P(None, ("gx", "gy", "gz")),
            P(("gx", "gy", "gz"), None, None),
        ),
        out_specs=(P(("ens", "gz"), "gx", "gy"), P(("ens", "gx", "gy"), None)),
        check_vma=False,
    )
```

```python
import functools

import jax
import jax.numpy as jnp
from jax import lax
from jax.experimental import pallas as pl
from jax.experimental.pallas import tpu as pltpu
from jax.sharding import PartitionSpec as P

STEPS = 4
HALO = STEPS
WIDTH = STEPS - 1
TOP = STEPS + 1
LANES = 128
TILE = 8
GROUP = LANES // HALO
FEW = 16
UNROLL = 8
CHUNKS = 4
BLOCKS_AXES = ("gx", "gy")
ALL_AXES = ("gx", "gy", "gz")
VMEM_LIMIT = 60 * 1024 * 1024


def position_of(few, dx, dy):
    if not few:
        return (dx + 1) * 2 + (1 if dy > 0 else 0)
    gx_count, gy_count = lax.axis_size("gx"), lax.axis_size("gy")
    x = jnp.clip(lax.axis_index("gx") + dx, 0, gx_count - 1)
    y = jnp.clip(lax.axis_index("gy") + dy, 0, gy_count - 1)
    return x * gy_count + y


def side_tile(left, right, index):
    lane = lax.broadcasted_iota(jnp.int32, left.shape, 1)
    from_right = pltpu.roll(right, lax.rem(LANES - HALO * index, LANES), 1)
    from_left = pltpu.roll(left, lax.rem(2 * LANES - HALO - HALO * index, LANES), 1)
    zero = jnp.zeros_like(left)
    return jnp.where(lane < HALO, from_right, jnp.where(lane >= LANES - HALO, from_left, zero))


def put_slab(ref, own, after, before, tile):
    rows, columns = own.shape
    ref[0:rows, 0:columns] = own
    ref[rows : rows + HALO, 0:columns] = after
    ref[rows + HALO : rows + 2 * HALO, 0:columns] = before
    ref[:, columns:] = tile


def keep_share(levels, around_ref, mixing, level):
    wet = [jnp.where(around_ref[side] > level, 0.1, 0.0) for side in range(4)]
    wet_around = (wet[0] + wet[1]) + (wet[2] + wet[3])
    above = jnp.where(level > 0.0, 1.0, 0.0)
    vertical = above + jnp.where(levels > level + 1.0, 1.0, 0.0)
    return 1.0 - wet_around - mixing * vertical


def step_slab(center, over, under, keep, mixing, levels, level, forcing):
    rows, lanes = center.shape
    lateral = pltpu.roll(center, 1, 0) + pltpu.roll(center, rows - 1, 0)
    lateral = lateral + (pltpu.roll(center, 1, 1) + pltpu.roll(center, lanes - 1, 1))
    if forcing is not None:
        lateral = lateral + forcing
    new = center * keep + 0.1 * lateral + mixing * (over + under)
    return jnp.where(levels > level, new, 0.0)


def last_slab(center, over, under, keep, mixing, forcing):
    rows, columns = over.shape
    tall, lanes = center.shape
    own = slice(0, rows), slice(0, columns)
    lateral = pltpu.roll(center, 1, 0)[own] + pltpu.roll(center, tall - 1, 0)[own]
    lateral = lateral + (pltpu.roll(center[0:rows], 1, 1)[own] + pltpu.roll(center[0:rows], lanes - 1, 1)[own])
    return center[own] * keep + 0.1 * (lateral + forcing) + mixing * (over + under)


def depth_share(level, total_levels):
    return jnp.exp(jnp.full((1, 1), -4.0 / total_levels, jnp.float32) * level)


def begin(copies, semaphores, first=0):
    started = []
    for index, (source, target) in enumerate(copies):
        copy = pltpu.make_async_copy(source, target, semaphores.at[first + index])
        copy.start()
        started.append(copy)
    return started


def finish(copies):
    for copy in copies:
        copy.wait()


def in_order(start, count, body):
    whole = count // UNROLL

    def group(index, carry):
        for offset in range(UNROLL):
            body(start + index * UNROLL + offset)
        return carry

    lax.fori_loop(0, whole, group, 0)
    for index in range(whole * UNROLL, count):
        body(start + index)


def rows_kernel(
    temp_ref, bathy_ref, mixing_ref, one_hbm, two_hbm, temp_rows, bathy_rows, mixing_rows, one_ref, two_ref, semaphores,
):
    layers, rows, columns = temp_ref.shape
    copies = []
    for side in range(2):
        part = pl.ds(side * (rows - TILE), TILE)
        copies += [(temp_ref.at[:, part], temp_rows.at[side]), (bathy_ref.at[part], bathy_rows.at[side])]
        copies += [(mixing_ref.at[part], mixing_rows.at[side])]
    finish(begin(copies, semaphores))
    even = lax.rem(lax.axis_index("gx"), 2) == 0
    fields = [
        (slice(0, layers), lambda side: temp_rows[side]), (layers, lambda side: bathy_rows[side].astype(jnp.float32)),
        (layers + 1, lambda side: mixing_rows[side]),
    ]
    for place, read in fields:
        low, high = read(0)[..., 0:HALO, :], read(1)[..., TILE - HALO :, :]
        one_ref[place] = jnp.where(even, high, low)
        two_ref[place] = jnp.where(even, low, high)
    finish(begin([(one_ref, one_hbm), (two_ref, two_hbm)], semaphores, len(copies)))


def send_kernel(sends_hbm, flux_hbm, temp_hbm, bathy_hbm, mixing_hbm, *refs, few, sides):
    if few:
        (
            message_hbm, sends_ref, flux_ref, temp_ref, bathy_ref, mixing_ref, semaphores, flux_scratch, message_ref,
            strips_ref,
        ) = refs
        fluxes_ref = message_ref
    else:
        (
            fluxes_hbm, strips_hbm, sends_ref, flux_ref, temp_ref, bathy_ref, mixing_ref, semaphores, flux_scratch,
            fluxes_ref, strips_ref,
        ) = refs
    layers, rows, columns = temp_hbm.shape
    gy, gy_count = lax.axis_index("gy"), lax.axis_size("gy")
    me = lax.axis_index("gx") * gy_count + gy
    copies = [(sends_hbm, sends_ref), (flux_hbm, flux_ref)]
    for place in range(sides):
        side = 1 - gy if sides == 1 else place
        window = pl.ds(pl.multiple_of(side * (columns - LANES), LANES), LANES)
        copies += [(bathy_hbm.at[:, window], bathy_ref.at[place]), (mixing_hbm.at[:, window], mixing_ref.at[place])]
        copies += [(temp_hbm.at[:, :, window], temp_ref.at[place])]
    copies = begin(copies, semaphores)
    lane = lax.broadcasted_iota(jnp.int32, (rows, LANES), 1)
    short = lax.broadcasted_iota(jnp.int32, (TILE, LANES), 1)
    finish(copies)
    for side in range(sides):
        base = HALO * (1 - gy) if sides == 1 else HALO * side
        strip = jnp.zeros((rows, LANES), jnp.float32)
        for index in range(layers):
            place = HALO * index
            moved = pltpu.roll(temp_ref[side, index], lax.rem(place + base, LANES), 1)
            strip = jnp.where((lane >= place) & (lane < place + HALO), moved, strip)
        strips_ref[side, 2 * TILE : 2 * TILE + rows] = strip
        plain = jnp.zeros((TILE, LANES), jnp.float32)
        for part in range(rows // TILE):
            here = slice(part * TILE, (part + 1) * TILE)
            for which, values in enumerate((bathy_ref[side, here].astype(jnp.float32), mixing_ref[side, here])):
                place = 2 * HALO * part + HALO * which
                moved = pltpu.roll(values, lax.rem(place + base, LANES), 1)
                plain = jnp.where((short >= place) & (short < place + HALO), moved, plain)
        strips_ref[side, TILE : 2 * TILE] = plain
        strips_ref[side, 0:TILE] = jnp.zeros((TILE, LANES), jnp.float32)
    flux_scratch[...] = flux_ref[...].astype(jnp.float32)
    fields = flux_ref.shape[1]

    def one(block, carry):
        tile = sends_ref[me, block]
        if few:
            side = 0 if sides == 1 else (lax.rem(block, gy_count) > gy).astype(jnp.int32)
            message_ref[block] = strips_ref[side]
        else:
            fluxes_ref[block] = jnp.zeros(fluxes_ref.shape[1:], jnp.float32)
        sent = jnp.where(tile >= 0, flux_scratch[jnp.maximum(tile, 0)], 0.0)
        fluxes_ref[block, 0:fields] = sent
        return carry

    used = len(copies)
    if few:
        leaving = []
        for block in range(fluxes_ref.shape[0]):
            one(block, 0)
            leaving += begin([(message_ref.at[block], message_hbm.at[block])], semaphores, used + block)
    else:
        leaving = begin([(strips_ref, strips_hbm)], semaphores, used)
        lax.fori_loop(0, fluxes_ref.shape[0], one, 0)
        leaving += begin([(fluxes_ref, fluxes_hbm)], semaphores, used + 1)
    finish(leaving)


def regrid_kernel(
    slots_hbm, flux_hbm, weights_hbm, partial_hbm, edges_hbm,
    edges_ref, slots_ref, flux_ref, weights_ref, partial_ref, semaphores, sums_ref, *strip_scratch, few,
):
    fields, rows, columns = partial_ref.shape
    slot_count, tile_atm, patch = weights_ref.shape
    halves = columns // LANES
    needed = begin([(slots_hbm, slots_ref), (flux_hbm.at[:, pl.ds(0, TILE)], flux_ref)], semaphores)
    chunk = slot_count // CHUNKS
    arriving = begin([
        (weights_hbm.at[pl.ds(part * chunk, chunk)], weights_ref.at[pl.ds(part * chunk, chunk)])
        for part in range(CHUNKS)
    ], semaphores, len(needed))
    sums_ref[...] = jnp.zeros_like(sums_ref)
    finish(needed)
    for slot in range(slot_count):
        if slot % chunk == 0:
            arriving[slot // chunk].wait()
        fluxes = flux_ref[slots_ref[0, slot]].astype(jnp.bfloat16)
        got = jnp.dot(fluxes, weights_ref[slot], preferred_element_type=jnp.float32)
        place = pl.multiple_of(slots_ref[1, slot] * TILE, TILE)
        sums_ref[pl.ds(place, TILE)] += got

    strips_ref = strip_scratch[0] if few else edges_ref
    strips_ref[...] = jnp.zeros_like(strips_ref)
    short = lax.broadcasted_iota(jnp.int32, (TILE, LANES), 1)
    columns_low = jnp.zeros((TILE, LANES), jnp.float32)
    columns_high = jnp.zeros((TILE, LANES), jnp.float32)
    for field in range(2):
        for half in range(halves):
            values = sums_ref[pl.ds(half * TILE + field, rows, stride=halves * TILE), :]
            partial_ref[field, :, half * LANES : (half + 1) * LANES] = values
            place = (field * 2 + half) * HALO
            strips_ref[0, place : place + WIDTH] = values[0:WIDTH]
            strips_ref[1, place : place + WIDTH] = values[rows - WIDTH : rows]
            for part in range(rows // TILE):
                block = values[part * TILE : (part + 1) * TILE]
                place = 2 * HALO * part + HALO * field
                inside = (short >= place) & (short < place + HALO)
                if half == 0:
                    columns_low = jnp.where(inside, pltpu.roll(block, place % LANES, 1), columns_low)
                if half == halves - 1:
                    columns_high = jnp.where(inside, pltpu.roll(block, (place + HALO) % LANES, 1), columns_high)
    leaving = begin([(partial_ref, partial_hbm)], semaphores, len(needed) + CHUNKS)
    strips_ref[2, 0:TILE] = columns_low
    strips_ref[3, 0:TILE] = columns_high
    if few:
        gx, gy, gy_count = lax.axis_index("gx"), lax.axis_index("gy"), lax.axis_size("gy")
        for entry in range(edges_ref.shape[0]):
            x, y = entry // 2 // gy_count, entry // 2 % gy_count
            choice = jnp.where(x < gx, 0, jnp.where(x > gx, 1, jnp.where(y < gy, 2, 3)))
            edges_ref[entry] = strips_ref[choice]

    leaving += begin([(edges_ref, edges_hbm)], semaphores, len(needed) + CHUNKS + 1)
    finish(leaving)


def halo_kernel(
    sides_hbm, temp_hbm, bathy_hbm, mixing_hbm, one_hbm, two_hbm, after_ref,
    shared_hbm, levels_hbm, mix_hbm, packed_hbm,
    shared_ref, sides_ref, temp_ref, bathy_ref, mixing_ref, pair_ref, levels_ref, mix_ref, packed_ref, semaphores, *, few,
):
    layers, rows, columns = temp_hbm.shape
    lasts = pl.ds(layers - HALO, HALO)
    needed = begin([
        (sides_hbm, sides_ref), (temp_hbm.at[pl.ds(0, TOP)], temp_ref.at[pl.ds(0, TOP)]),
        (temp_hbm.at[lasts], temp_ref.at[pl.ds(TOP, HALO)]), (bathy_hbm, bathy_ref), (mixing_hbm, mixing_ref),
        (one_hbm, pair_ref.at[0]), (two_hbm, pair_ref.at[1]),
    ], semaphores)
    odd = lax.rem(lax.axis_index("gx"), 2)
    next_ref, prev_ref = pair_ref.at[odd], pair_ref.at[1 - odd]
    finish(needed)
    gx, gx_count = lax.axis_index("gx"), lax.axis_size("gx")
    gy, gy_count = lax.axis_index("gy"), lax.axis_size("gy")
    plain = []
    for side, dy in ((0, -1), (1, 1)):
        own, after, before = (position_of(few, dx, dy) for dx in (0, 1, -1))
        packed_ref[side, 0:rows] = sides_ref[own, 2 * TILE : 2 * TILE + rows]
        packed_ref[side, rows : rows + HALO] = sides_ref[after, 2 * TILE : 2 * TILE + HALO]
        packed_ref[side, rows + HALO :] = sides_ref[before, 2 * TILE + rows - HALO : 2 * TILE + rows]
        tile = sides_ref[own, TILE : 2 * TILE]
        parts = [tile] + [pltpu.roll(tile, LANES - 2 * HALO * part, 1) for part in range(1, rows // TILE)]
        last = pltpu.roll(sides_ref[before, TILE : 2 * TILE], LANES - 2 * HALO * (rows // TILE - 1), 1)
        row = lax.broadcasted_iota(jnp.int32, (TILE, LANES), 0)
        parts.append(jnp.where(row < HALO, sides_ref[after, TILE : 2 * TILE], last))
        plain.append(jnp.concatenate(parts, axis=0))
    size = (rows + 2 * HALO, LANES)
    lane, row = (lax.broadcasted_iota(jnp.int32, size, dim) for dim in (1, 0))
    there = (lane < HALO) & (gy < gy_count - 1) | (lane >= HALO) & (gy > 0)
    there = there & ((row < rows) | (row < rows + HALO) & (gx < gx_count - 1) | (row >= rows + HALO) & (gx > 0))
    tile = jnp.where(there, side_tile(plain[0], plain[1], 0), 0.0)
    put_slab(levels_ref, bathy_ref[...].astype(jnp.float32), next_ref[layers], prev_ref[layers], tile)
    tile = side_tile(plain[0], plain[1], 1)
    put_slab(mix_ref, mixing_ref[...], next_ref[layers + 1], prev_ref[layers + 1], tile)
    leaving = begin(
        [(levels_ref, levels_hbm), (mix_ref, mix_hbm), (packed_ref, packed_hbm)], semaphores, len(needed)
    )
    used = len(needed) + 3
    for place, level in enumerate(list(range(TOP)) + list(range(layers - HALO, layers))):
        tile = side_tile(packed_ref[0], packed_ref[1], level)
        put_slab(shared_ref.at[place], temp_ref[place], next_ref[level], prev_ref[level], tile)
        leaving += begin([(shared_ref.at[place], shared_hbm.at[place])], semaphores, used + place)
    finish(leaving)


def first_kernel(
    temp_hbm, one_hbm, two_hbm, packed_hbm, other_hbm, levels_hbm, mix_hbm,
    moved_hbm, keep_hbm, top_hbm, top_keep_hbm,
    temp_ref, pair_ref, packed_ref, other_ref, levels_ref, mix_ref,
    moved_ref, keep_ref, top_ref, top_keep_ref, first_ref, skin_ref, around_ref, semaphores,
):
    layers = temp_hbm.shape[0]
    gz = lax.axis_index("gz")
    first_level = gz * layers - HALO
    needed = begin([
        (one_hbm, pair_ref.at[0]), (two_hbm, pair_ref.at[1]), (packed_hbm, packed_ref), (levels_hbm, levels_ref),
        (mix_hbm, mix_ref), (other_hbm, other_ref),
    ], semaphores)
    chunk = layers // CHUNKS
    parts = [pl.ds(part * chunk, chunk) for part in range(CHUNKS)]
    used = len(needed)
    arriving = begin([(temp_hbm.at[part], temp_ref.at[part]) for part in parts], semaphores, used)
    used += CHUNKS
    odd = lax.rem(lax.axis_index("gx"), 2)
    next_ref, prev_ref = pair_ref.at[odd], pair_ref.at[1 - odd]
    finish(needed)
    tall, lanes = levels_ref.shape
    for side, (shift, dim) in enumerate(((1, 0), (tall - 1, 0), (1, 1), (lanes - 1, 1))):
        around_ref[side] = pltpu.roll(levels_ref[...], shift, dim)

    def level_of(place):
        return (first_level + place).astype(jnp.float32)

    def settle(place):
        level = level_of(place)
        first_ref[place] = jnp.where(levels_ref[...] > level, first_ref[place], 0.0)
        keep_ref[place] = keep_share(levels_ref[...], around_ref, mix_ref[...], level)

    def own_level(index):
        tile = side_tile(packed_ref[0], packed_ref[1], index)
        put_slab(first_ref.at[index + HALO], temp_ref[index], next_ref[index], prev_ref[index], tile)
        settle(index + HALO)

    for part in range(CHUNKS):
        arriving[part].wait()
        in_order(part * chunk, chunk, own_level)

    for index in range(HALO):
        slot = jnp.where(gz == 0, index, TOP + index)
        place = jnp.where(gz == 0, HALO + layers + index, index)
        first_ref[place] = other_ref[slot]
        settle(place)

    base = jnp.where(gz == 0, HALO, 1)
    count = layers + HALO - 1
    span = pl.ds(base, count)
    leaving = begin([(keep_ref.at[span], keep_hbm.at[span])], semaphores, used)
    used += 1
    levels = levels_ref[...]
    for level in range(TOP):
        slab = jnp.where(gz == 0, first_ref[HALO + level], other_ref[level])
        skin_ref[level] = jnp.where(levels > float(level), slab, 0.0)
    for level in range(STEPS):
        top_keep_ref[level] = keep_share(levels, around_ref, mix_ref[...], jnp.float32(level))
        over = skin_ref[level - 1] if level else jnp.zeros_like(levels)
        top_ref[level] = step_slab(
            skin_ref[level], over, skin_ref[level + 1], top_keep_ref[level], mix_ref[...], levels, float(level), None
        )
    leaving += begin([(top_ref, top_hbm), (top_keep_ref, top_keep_hbm)], semaphores, used)
    used += 2
    edge = jnp.where(gz == 0, HALO - 1, HALO + layers)
    first_ref[edge] = jnp.zeros_like(first_ref[0])

    def one(place):
        moved_ref[place] = step_slab(
            first_ref[place], first_ref[place - 1], first_ref[place + 1], keep_ref[place], mix_ref[...],
            levels_ref[...], level_of(place), None,
        )

    for start, size in pieces(count):
        in_order(base + start, size, one)
        here = pl.ds(base + start, size)
        leaving += begin([(moved_ref.at[here], moved_hbm.at[here])], semaphores, used)
        used += 1
    finish(leaving)


def pieces(count):
    return [(start, min(UNROLL, count - start)) for start in range(0, count, UNROLL)]


def skin_kernel(
    sends_hbm, slots_hbm, partial_hbm, other_hbm, edges_hbm, weights_hbm, levels_hbm, mix_hbm, top_hbm, top_keep_hbm,
    surface_hbm, back_hbm,
    back_ref, sends_ref, slots_ref, partial_ref, other_ref, edges_ref, weights_ref, levels_ref, mix_ref, top_ref, top_keep_ref, surface_ref, semaphores,
    first_ref, second_ref, sst_ref, rows_ref, *sums_scratch, few, total_levels,
):
    fields, rows, columns = partial_ref.shape
    slot_count, tile_atm, patch = weights_ref.shape
    halves = columns // LANES
    needed = begin([
        (partial_hbm, partial_ref), (other_hbm, other_ref), (levels_hbm, levels_ref), (mix_hbm, mix_ref),
        (top_hbm, top_ref), (top_keep_hbm, top_keep_ref), (slots_hbm, slots_ref),
        (sends_hbm, sends_ref), (edges_hbm, edges_ref),
    ], semaphores)
    chunk = slot_count // CHUNKS
    used = len(needed)
    arriving = begin([
        (weights_hbm.at[pl.ds(part * chunk, chunk)], weights_ref.at[pl.ds(part * chunk, chunk)])
        for part in range(CHUNKS)
    ], semaphores, used)
    used += CHUNKS

    def edge(dx, dy):
        if few:
            where = position_of(few, dx, dy)
            return edges_ref[2 * where] + edges_ref[2 * where + 1]
        where = EDGES.index((dx, dy))
        return edges_ref[2 * where] + edges_ref[2 * where + 1]

    finish(needed)
    after, before = edge(1, 0), edge(-1, 0)
    right, left = edge(0, 1), edge(0, -1)
    corners = {(dx, dy): edge(dx, dy) for dx in (1, -1) for dy in (1, -1)}
    lane = lax.broadcasted_iota(jnp.int32, (TILE, LANES), 1)
    short = lax.broadcasted_iota(jnp.int32, (HALO, LANES), 1)
    surface_ref[...] = jnp.zeros_like(surface_ref)
    for field in range(fields):
        surface_ref[field, 0:rows, 0:columns] = partial_ref[field] + other_ref[field]
        for half in range(halves):
            place = (field * 2 + half) * HALO
            here = slice(half * LANES, (half + 1) * LANES)
            surface_ref[field, rows : rows + WIDTH, here] = after[place : place + WIDTH]
            surface_ref[field, rows + 2 * HALO - WIDTH :, here] = before[place : place + WIDTH]
        for part in range(rows // TILE):
            place = 2 * HALO * part + HALO * field
            from_right = pltpu.roll(right[0:TILE], (LANES - place) % LANES, 1)
            from_left = pltpu.roll(left[0:TILE], (2 * LANES - HALO - place) % LANES, 1)
            tile = jnp.where(lane < HALO, from_right, jnp.where(lane >= LANES - HALO, from_left, 0.0))
            surface_ref[field, part * TILE : (part + 1) * TILE, columns:] = tile
        low, high = field * 2 * HALO, (field * 2 + halves - 1) * HALO
        for dx in (1, -1):
            from_right, from_left = corners[dx, 1][low : low + HALO], corners[dx, -1][high : high + HALO]
            tile = jnp.where(short < HALO, from_right, jnp.where(short >= LANES - HALO, from_left, 0.0))
            if dx == 1:
                surface_ref[field, rows : rows + WIDTH, columns:] = tile[0:WIDTH]
            else:
                surface_ref[field, rows + 2 * HALO - WIDTH :, columns:] = tile[0:WIDTH]

    leaving = begin([(surface_ref, surface_hbm)], semaphores, used)
    levels = levels_ref[...]
    forcings = [depth_share(jnp.float32(level), total_levels) * surface_ref[1] for level in range(STEPS)]
    forcings[0] = forcings[0] + surface_ref[0]
    for level in range(STEPS):
        first_ref[level] = top_ref[level] + jnp.where(levels > float(level), 0.1 * forcings[level], 0.0)
    source, target = first_ref, second_ref
    zero = jnp.zeros_like(levels)
    for step in range(2, STEPS + 1):
        for level in range(TOP - step):
            over = source[level - 1] if level else zero
            target[level] = step_slab(
                source[level], over, source[level + 1], top_keep_ref[level], mix_ref[...], levels, float(level),
                forcings[level],
            )
        source, target = target, source
    for half in range(halves):
        values = source[0, 0:rows, half * LANES : (half + 1) * LANES]
        sst_ref[half * rows : (half + 1) * rows] = values.astype(jnp.bfloat16).astype(jnp.float32)

    for slot in range(slot_count):
        tile = slots_ref[1, slot]
        place = lax.rem(tile, halves) * rows + lax.div(tile, halves)
        rows_ref[pl.ds(slot, 1)] = sst_ref[pl.ds(place, 1)]
    sums_ref = sums_scratch[0]
    sums_ref[...] = jnp.zeros_like(sums_ref)
    for group in range(slot_count // TILE):
        given = rows_ref[group * TILE : (group + 1) * TILE].astype(jnp.bfloat16)
        for row in range(TILE):
            slot = group * TILE + row
            if slot % chunk == 0:
                arriving[slot // chunk].wait()
            got = lax.dot_general(
                given, weights_ref[slot], (((1,), (1,)), ((), ())), preferred_element_type=jnp.float32
            )
            sums_ref[pl.ds(slots_ref[0, slot], 1)] += got[row : row + 1]
    me = lax.axis_index("gx") * lax.axis_size("gy") + lax.axis_index("gy")
    blocks = sums_ref.shape[0]
    copies = back_ref.shape[0] // blocks

    def place_rows(block):
        tile = sends_ref[block, me]
        back_ref[pl.ds(block * copies, copies)] = jnp.zeros((copies,) + back_ref.shape[1:], jnp.float32)

        @pl.when(tile >= 0)
        def _():
            for copy in range(copies):
                back_ref[block * copies + copy, pl.ds(tile, 1)] = sums_ref[pl.ds(block, 1)]

    if few:
        for block in range(blocks):
            place_rows(block)
    else:
        lax.fori_loop(0, blocks, lambda block, carry: (place_rows(block), carry)[1], 0)
    leaving += begin([(back_ref, back_hbm)], semaphores, used + 1)
    finish(leaving)


def ocean_kernel(
    temp_hbm, moved_hbm, keep_hbm, levels_hbm, mix_hbm, surface_hbm, ocean_hbm,
    temp_ref, keep_ref, levels_ref, mix_ref, surface_ref, semaphores, first_ref, second_ref, *, total_levels,
):
    layers, rows, columns = temp_hbm.shape
    gz = lax.axis_index("gz")
    first_level = gz * layers - HALO
    base = jnp.where(gz == 0, HALO, 1)
    count = layers + HALO - 1
    needed = begin(
        [(levels_hbm, levels_ref), (mix_hbm, mix_ref), (surface_hbm, surface_ref)], semaphores
    )
    used = len(needed)
    spans = [pl.ds(base + start, size) for start, size in pieces(count)]
    arriving = begin([(moved_hbm.at[span], first_ref.at[span]) for span in spans], semaphores, used)
    used += len(spans)
    later = begin([
        (keep_hbm.at[pl.ds(base, count)], keep_ref.at[pl.ds(base, count)]), (temp_hbm, temp_ref)
    ], semaphores, used)
    used += len(later)
    edge = jnp.where(gz == 0, HALO - 1, HALO + layers)
    first_ref[edge] = jnp.zeros_like(first_ref[0])
    second_ref[edge] = jnp.zeros_like(first_ref[0])
    finish(needed)

    def level_of(place):
        return (first_level + place).astype(jnp.float32)

    def add(place):
        level = level_of(place)
        forcing = (0.1 * depth_share(level, total_levels)) * surface_ref[1]
        first_ref[place] = first_ref[place] + jnp.where(levels_ref[...] > level, forcing, 0.0)

    for (start, size), copy in zip(pieces(count), arriving):
        copy.wait()
        in_order(base + start, size, add)

    def top_forcing():
        return jnp.where(levels_ref[...] > 0.0, 0.1 * surface_ref[0], 0.0)

    @pl.when(gz == 0)
    def _():
        first_ref[HALO] = first_ref[HALO] + top_forcing()

    later[0].wait()
    source, target = first_ref, second_ref
    for step in range(2, STEPS + 1):
        if step == STEPS:
            later[1].wait()

        def one(place, source=source, target=target, step=step):
            level = level_of(place)
            share = depth_share(level, total_levels)
            if step < STEPS:
                target[place] = step_slab(
                    source[place], source[place - 1], source[place + 1], keep_ref[place], mix_ref[...],
                    levels_ref[...], level, share * surface_ref[1],
                )
            else:
                own = slice(0, rows), slice(0, columns)
                new = last_slab(
                    source[place], source[(place - 1,) + own], source[(place + 1,) + own], keep_ref[(place,) + own],
                    mix_ref[own], share * surface_ref[(1,) + own],
                )
                index = place - HALO
                temp_ref[index] = jnp.where(levels_ref[own] > level, new, temp_ref[index])

        if step < STEPS:
            in_order(jnp.where(gz == 0, HALO, step), layers + HALO - step, one)

            @pl.when(gz == 0)
            def _(target=target):
                target[HALO] = target[HALO] + top_forcing()
        else:
            leaving = []
            for start, size in pieces(layers):
                in_order(HALO + start, size, one)
                if start == 0:
                    @pl.when(gz == 0)
                    def _():
                        temp_ref[0] = temp_ref[0] + top_forcing()[0:rows, 0:columns]

                here = pl.ds(start, size)
                leaving += begin([(temp_ref.at[here], ocean_hbm.at[here])], semaphores, used)
                used += 1
            finish(leaving)
        source, target = target, source


def call(body, outs, scratch, operands, places, out_places, cost=0):
    assert len(places) == len(operands) and len(out_places) == len(outs)
    scratch_shapes = []
    for item in scratch:
        if isinstance(item, int):
            scratch_shapes.append(pltpu.SemaphoreType.DMA((item,)))
        elif isinstance(item, tuple):
            scratch_shapes.append(pltpu.VMEM(item, jnp.float32))
        else:
            scratch_shapes.append(item)
    return pl.pallas_call(
        body,
        out_shape=[jax.ShapeDtypeStruct(out, jnp.float32) for out in outs],
        in_specs=[pl.BlockSpec(memory_space=pl.ANY) for place in places],
        out_specs=[pl.BlockSpec(memory_space=pl.ANY) for place in out_places],
        scratch_shapes=scratch_shapes,
        compiler_params=pltpu.CompilerParams(vmem_limit_bytes=VMEM_LIMIT),
        cost_estimate=pl.CostEstimate(flops=cost, bytes_accessed=4 * cost // 16, transcendentals=0),
    )(*operands)


def like(array):
    return pltpu.VMEM(array.shape, array.dtype)


EDGES = [(dx, dy) for dx in (-1, 0, 1) for dy in (-1, 0, 1) if (dx, dy) != (0, 0)]


def toward(gx_count, gy_count, dx, dy):
    pairs = []
    for x in range(gx_count):
        for y in range(gy_count):
            if 0 <= x + dx < gx_count and 0 <= y + dy < gy_count:
                pairs.append(((x + dx) * gy_count + y + dy, x * gy_count + y))
    return pairs


def per_device(
    ocean_temp, bathy_levels, mixing, atm_flux, send_tiles, regrid_slots, regrid_weights
):
    layers, rows, columns = ocean_temp.shape
    gx_count, gy_count, gz_count = (lax.axis_size(axis) for axis in ALL_AXES)
    blocks = gx_count * gy_count
    own_tiles, fields, tile_atm = atm_flux.shape
    caps = send_tiles.shape[2]
    assert gz_count == 2 and caps == 1 and layers == GROUP and tile_atm == LANES
    assert columns == 2 * LANES and rows == 4 * TILE and regrid_weights.shape[2] == LANES
    total_levels = layers * gz_count
    few = blocks <= FEW
    sends = send_tiles.reshape(blocks, blocks)
    swap = [(0, 1), (1, 0)]
    tall = 2 * TILE + rows
    strip = (layers + 2, HALO, columns)
    slab = (rows + 2 * HALO, columns + LANES)
    slab_cost = 20 * slab[0] * slab[1]
    deep = (layers + 2 * HALO,) + slab

    high_rows = (2, layers, TILE, columns)
    one, two = call(
        rows_kernel, [strip, strip],
        [high_rows, pltpu.VMEM((2, TILE, columns), jnp.int32), (2, TILE, columns), strip, strip, 8],
        (ocean_temp, bathy_levels, mixing), "hhh", "hh", cost=slab_cost,
    )
    rows_one, rows_two = (
        lax.ppermute(part, "gx", [
            pair for x in range(start, gx_count - 1, 2) for pair in ((x, x + 1), (x + 1, x))
        ]) for start, part in enumerate((one, two))
    )

    outs = [(blocks, tall, LANES)] if few else [(blocks, TILE, LANES), (2, tall, LANES)]
    sides = 1 if few and gy_count == 2 else 2
    scratch = [
        pltpu.SMEM(sends.shape, jnp.int32), like(atm_flux), (sides, layers, rows, LANES),
        pltpu.VMEM((sides, rows, LANES), jnp.int32), (sides, rows, LANES), 4 + 3 * sides + FEW,
        (own_tiles, fields, LANES), outs[0], (sides, tall, LANES),
    ]
    sent = call(
        functools.partial(send_kernel, few=few, sides=sides), outs, scratch,
        (sends, atm_flux, ocean_temp, bathy_levels, mixing), "hhhhh", "h" * len(outs), cost=2 * slab_cost,
    )
    got = [lax.all_to_all(sent[0], BLOCKS_AXES, split_axis=0, concat_axis=0, tiled=True)]
    if not few:
        got.append(jnp.stack([
            lax.ppermute(sent[1][0 if dy > 0 else 1], BLOCKS_AXES, toward(gx_count, gy_count, dx, dy))
            for dx in (-1, 0, 1) for dy in (-1, 1)
        ]))

    strips = (4, 2 * TILE, LANES)
    packed_shape = (2, slab[0], LANES)
    pair_shape = (2,) + strip
    partial, edges = call(
        functools.partial(regrid_kernel, few=few),
        [(fields, rows, columns), (2 * blocks, 2 * TILE, LANES) if few else strips],
        [
            (2 * blocks, 2 * TILE, LANES) if few else strips,
            pltpu.SMEM(regrid_slots.shape, jnp.int32), (blocks, TILE, LANES), like(regrid_weights),
            (fields, rows, columns), 4 + CHUNKS, (rows * columns // LANES * TILE, LANES),
        ] + ([strips] if few else []),
        (regrid_slots, got[0], regrid_weights), "hhh", "hh", cost=4 * slab_cost,
    )
    shared, levels, mix, packed = call(
        functools.partial(halo_kernel, few=few),
        [(TOP + HALO,) + slab, slab, slab, packed_shape],
        [
            (TOP + HALO,) + slab, got[-1].shape, (TOP + HALO, rows, columns), like(bathy_levels), like(mixing),
            pair_shape, slab, slab, packed_shape, 10 + TOP + HALO,
        ],
        (got[-1], ocean_temp, bathy_levels, mixing, rows_one, rows_two, partial), "h" * 7, "hhhh", cost=slab_cost,
    )
    other_partial = lax.ppermute(partial, "gz", swap)
    other_shared = lax.ppermute(shared, "gz", swap)
    if few:
        edges = lax.all_to_all(edges, ALL_AXES, split_axis=0, concat_axis=0, tiled=True)
    else:
        choice = {-1: 1, 1: 0}
        around = jnp.stack([
            lax.ppermute(
                edges[choice[dx] if dx else (3 if dy < 0 else 2)], BLOCKS_AXES, toward(gx_count, gy_count, dx, dy)
            )
            for dx, dy in EDGES
        ])
        edges = jnp.stack([around, lax.ppermute(around, "gz", swap)], axis=1)
        edges = edges.reshape((2 * len(EDGES),) + strips[1:])

    top = (STEPS,) + slab
    parts = len(pieces(layers + HALO - 1))
    moved, keep, top_moved, top_keep = call(
        first_kernel, [deep, deep, top, top],
        [
            like(ocean_temp), pair_shape, packed_shape, (TOP + HALO,) + slab, slab, slab,
            deep, deep, top, top, deep, (TOP,) + slab, (4,) + slab, 9 + CHUNKS + parts,
        ],
        (ocean_temp, rows_one, rows_two, packed, other_shared, levels, mix), "h" * 7, "hhhh", cost=slab_cost,
    )
    surface, back = call(
        functools.partial(skin_kernel, few=few, total_levels=total_levels),
        [(fields,) + slab, ((2 if few else 1) * blocks, own_tiles, LANES)],
        [
            ((2 if few else 1) * blocks, own_tiles, LANES),
            pltpu.SMEM(sends.shape, jnp.int32), pltpu.SMEM(regrid_slots.shape, jnp.int32), like(partial), like(partial),
            edges.shape, like(regrid_weights), slab, slab, top, top, (fields,) + slab, 11 + CHUNKS,
            top, top, (rows * columns // LANES, LANES), (regrid_weights.shape[0], LANES), (blocks, LANES),
        ],
        (sends, regrid_slots, partial, other_partial, edges, regrid_weights, levels, mix, top_moved, top_keep),
        "hhhhhhhhhh", "hh", cost=20 * slab_cost,
    )
    if few:
        returned = lax.all_to_all(back, ALL_AXES, split_axis=0, concat_axis=0, tiled=True)
    else:
        returned = lax.all_to_all(back, BLOCKS_AXES, split_axis=0, concat_axis=0, tiled=True)
        returned = returned + lax.ppermute(returned, "gz", swap)
    ocean, = call(
        functools.partial(ocean_kernel, total_levels=total_levels), [ocean_temp.shape],
        [like(ocean_temp), deep, slab, slab, (fields,) + slab, 5 + parts + len(pieces(layers)), deep, deep],
        (ocean_temp, moved, keep, levels, mix, surface), "h" * 6, "h", cost=120 * slab_cost,
    )
    atm_surface = returned.sum(axis=0)
    return (ocean, atm_surface)


def solution(mesh):
    return jax.shard_map(
        per_device,
        mesh=mesh,
        in_specs=(
            P(("ens", "gz"), "gx", "gy"),
            P(("ens", "gx"), "gy"),
            P(("ens", "gx"), "gy"),
            P(("ens", "gx", "gy"), None, None),
            P(),
            P(None, ("gx", "gy", "gz")),
            P(("gx", "gy", "gz"), None, None),
        ),
        out_specs=(P(("ens", "gz"), "gx", "gy"), P(("ens", "gx", "gy"), None)),
        check_vma=False,
    )
```

```python
import functools

import jax
import jax.numpy as jnp
from jax import lax
from jax.experimental import pallas as pl
from jax.experimental.pallas import tpu as pltpu
from jax.sharding import PartitionSpec as P

STEPS = 4
HALO = STEPS
WIDTH = STEPS - 1
TOP = STEPS + 1
LANES = 128
TILE = 8
GROUP = LANES // HALO
FEW = 16
UNROLL = 8
CHUNKS = 4
BLOCKS_AXES = ("gx", "gy")
ALL_AXES = ("gx", "gy", "gz")
VMEM_LIMIT = 60 * 1024 * 1024


def position_of(few, dx, dy):
    if not few:
        return (dx + 1) * 2 + (1 if dy > 0 else 0)
    gx_count, gy_count = lax.axis_size("gx"), lax.axis_size("gy")
    x = jnp.clip(lax.axis_index("gx") + dx, 0, gx_count - 1)
    y = jnp.clip(lax.axis_index("gy") + dy, 0, gy_count - 1)
    return x * gy_count + y


def side_tile(left, right, index):
    lane = lax.broadcasted_iota(jnp.int32, left.shape, 1)
    from_right = pltpu.roll(right, lax.rem(LANES - HALO * index, LANES), 1)
    from_left = pltpu.roll(left, lax.rem(2 * LANES - HALO - HALO * index, LANES), 1)
    zero = jnp.zeros_like(left)
    return jnp.where(lane < HALO, from_right, jnp.where(lane >= LANES - HALO, from_left, zero))


def put_slab(ref, own, after, before, tile):
    rows, columns = own.shape
    ref[0:rows, 0:columns] = own
    ref[rows : rows + HALO, 0:columns] = after
    ref[rows + HALO : rows + 2 * HALO, 0:columns] = before
    ref[:, columns:] = tile


def keep_share(levels, around_ref, mixing, level):
    wet = [jnp.where(around_ref[side] > level, 0.1, 0.0) for side in range(4)]
    wet_around = (wet[0] + wet[1]) + (wet[2] + wet[3])
    above = jnp.where(level > 0.0, 1.0, 0.0)
    vertical = above + jnp.where(levels > level + 1.0, 1.0, 0.0)
    return 1.0 - wet_around - mixing * vertical


def step_slab(center, over, under, keep, mixing, levels, level, forcing):
    rows, lanes = center.shape
    lateral = pltpu.roll(center, 1, 0) + pltpu.roll(center, rows - 1, 0)
    lateral = lateral + (pltpu.roll(center, 1, 1) + pltpu.roll(center, lanes - 1, 1))
    if forcing is not None:
        lateral = lateral + forcing
    new = center * keep + 0.1 * lateral + mixing * (over + under)
    return jnp.where(levels > level, new, 0.0)


def march(source, store, keep_ref, mix_ref, levels_ref, start, count, level_of, surface_ref, shares, size, done):
    tall, lanes = levels_ref.shape
    rows, columns = size
    row = lax.broadcasted_iota(jnp.int32, (TILE, lanes), 0)[:, 0:columns]
    tiles = tall // TILE
    for tile in range(rows // TILE):
        here, above, below = (
            slice(TILE * (place % tiles), TILE * (place % tiles) + TILE) for place in (tile, tile - 1, tile + 1)
        )
        own = here, slice(0, columns)
        mixing, levels = mix_ref[own], levels_ref[own]
        surface = None if surface_ref is None else surface_ref[(1,) + own]
        over, wide = source[(start - 1,) + own], source[start, here]
        for offset in range(count):
            place = start + offset
            level = level_of(place)
            below_wide = source[place + 1, here]
            center, under = wide[:, 0:columns], below_wide[:, 0:columns]
            up = jnp.where(row == 0, pltpu.roll(source[(place, above, own[1])], 1, 0), pltpu.roll(center, 1, 0))
            down = jnp.where(
                row == TILE - 1, pltpu.roll(source[(place, below, own[1])], TILE - 1, 0),
                pltpu.roll(center, TILE - 1, 0),
            )
            side = pltpu.roll(wide, 1, 1)[:, 0:columns] + pltpu.roll(wide, lanes - 1, 1)[:, 0:columns]
            lateral = (up + down) + side
            if surface is not None:
                lateral = lateral + shares[offset] * surface
            new = center * keep_ref[(place,) + own] + 0.1 * lateral + mixing * (over + under)
            store(place, own, levels > level, new)
            over, wide = center, below_wide
        done(tile, own)


def depth_share(level, total_levels):
    return jnp.exp(jnp.full((1, 1), -4.0 / total_levels, jnp.float32) * level)


def begin(copies, semaphores, first=0):
    started = []
    for index, (source, target) in enumerate(copies):
        copy = pltpu.make_async_copy(source, target, semaphores.at[first + index])
        copy.start()
        started.append(copy)
    return started


def finish(copies):
    for copy in copies:
        copy.wait()


def in_order(start, count, body):
    whole = count // UNROLL

    def group(index, carry):
        for offset in range(UNROLL):
            body(start + index * UNROLL + offset)
        return carry

    lax.fori_loop(0, whole, group, 0)
    for index in range(whole * UNROLL, count):
        body(start + index)


def rows_kernel(
    temp_ref, bathy_ref, mixing_ref, one_hbm, two_hbm, temp_rows, bathy_rows, mixing_rows, one_ref, two_ref, semaphores,
):
    layers, rows, columns = temp_ref.shape
    copies = []
    for side in range(2):
        part = pl.ds(side * (rows - TILE), TILE)
        copies += [(temp_ref.at[:, part], temp_rows.at[side]), (bathy_ref.at[part], bathy_rows.at[side])]
        copies += [(mixing_ref.at[part], mixing_rows.at[side])]
    finish(begin(copies, semaphores))
    even = lax.rem(lax.axis_index("gx"), 2) == 0
    fields = [
        (slice(0, layers), lambda side: temp_rows[side]), (layers, lambda side: bathy_rows[side].astype(jnp.float32)),
        (layers + 1, lambda side: mixing_rows[side]),
    ]
    for place, read in fields:
        low, high = read(0)[..., 0:HALO, :], read(1)[..., TILE - HALO :, :]
        one_ref[place] = jnp.where(even, high, low)
        two_ref[place] = jnp.where(even, low, high)
    finish(begin([(one_ref, one_hbm), (two_ref, two_hbm)], semaphores, len(copies)))


def send_kernel(sends_hbm, flux_hbm, temp_hbm, bathy_hbm, mixing_hbm, *refs, few, sides):
    if few:
        (
            message_hbm, sends_ref, flux_ref, temp_ref, bathy_ref, mixing_ref, semaphores, flux_scratch, message_ref,
            strips_ref,
        ) = refs
        fluxes_ref = message_ref
    else:
        (
            fluxes_hbm, strips_hbm, sends_ref, flux_ref, temp_ref, bathy_ref, mixing_ref, semaphores, flux_scratch,
            fluxes_ref, strips_ref,
        ) = refs
    layers, rows, columns = temp_hbm.shape
    gy, gy_count = lax.axis_index("gy"), lax.axis_size("gy")
    me = lax.axis_index("gx") * gy_count + gy
    copies = [(sends_hbm, sends_ref), (flux_hbm, flux_ref)]
    for place in range(sides):
        side = 1 - gy if sides == 1 else place
        window = pl.ds(pl.multiple_of(side * (columns - LANES), LANES), LANES)
        copies += [(bathy_hbm.at[:, window], bathy_ref.at[place]), (mixing_hbm.at[:, window], mixing_ref.at[place])]
        copies += [(temp_hbm.at[:, :, window], temp_ref.at[place])]
    copies = begin(copies, semaphores)
    lane = lax.broadcasted_iota(jnp.int32, (rows, LANES), 1)
    short = lax.broadcasted_iota(jnp.int32, (TILE, LANES), 1)
    finish(copies)
    for side in range(sides):
        base = HALO * (1 - gy) if sides == 1 else HALO * side
        strip = jnp.zeros((rows, LANES), jnp.float32)
        for index in range(layers):
            place = HALO * index
            moved = pltpu.roll(temp_ref[side, index], lax.rem(place + base, LANES), 1)
            strip = jnp.where((lane >= place) & (lane < place + HALO), moved, strip)
        strips_ref[side, 2 * TILE : 2 * TILE + rows] = strip
        plain = jnp.zeros((TILE, LANES), jnp.float32)
        for part in range(rows // TILE):
            here = slice(part * TILE, (part + 1) * TILE)
            for which, values in enumerate((bathy_ref[side, here].astype(jnp.float32), mixing_ref[side, here])):
                place = 2 * HALO * part + HALO * which
                moved = pltpu.roll(values, lax.rem(place + base, LANES), 1)
                plain = jnp.where((short >= place) & (short < place + HALO), moved, plain)
        strips_ref[side, TILE : 2 * TILE] = plain
        strips_ref[side, 0:TILE] = jnp.zeros((TILE, LANES), jnp.float32)
    flux_scratch[...] = flux_ref[...].astype(jnp.float32)
    fields = flux_ref.shape[1]

    def one(block, carry):
        tile = sends_ref[me, block]
        if few:
            side = 0 if sides == 1 else (lax.rem(block, gy_count) > gy).astype(jnp.int32)
            message_ref[block] = strips_ref[side]
        else:
            fluxes_ref[block] = jnp.zeros(fluxes_ref.shape[1:], jnp.float32)
        sent = jnp.where(tile >= 0, flux_scratch[jnp.maximum(tile, 0)], 0.0)
        fluxes_ref[block, 0:fields] = sent
        return carry

    used = len(copies)
    if few:
        leaving = []
        for block in range(fluxes_ref.shape[0]):
            one(block, 0)
            leaving += begin([(message_ref.at[block], message_hbm.at[block])], semaphores, used + block)
    else:
        leaving = begin([(strips_ref, strips_hbm)], semaphores, used)
        lax.fori_loop(0, fluxes_ref.shape[0], one, 0)
        leaving += begin([(fluxes_ref, fluxes_hbm)], semaphores, used + 1)
    finish(leaving)


def regrid_kernel(
    slots_hbm, flux_hbm, weights_hbm, partial_hbm, edges_hbm,
    edges_ref, slots_ref, flux_ref, weights_ref, partial_ref, semaphores, sums_ref, *strip_scratch, few,
):
    fields, rows, columns = partial_ref.shape
    slot_count, tile_atm, patch = weights_ref.shape
    halves = columns // LANES
    needed = begin([(slots_hbm, slots_ref), (flux_hbm.at[:, pl.ds(0, TILE)], flux_ref)], semaphores)
    chunk = slot_count // CHUNKS
    arriving = begin([
        (weights_hbm.at[pl.ds(part * chunk, chunk)], weights_ref.at[pl.ds(part * chunk, chunk)])
        for part in range(CHUNKS)
    ], semaphores, len(needed))
    sums_ref[...] = jnp.zeros_like(sums_ref)
    finish(needed)
    for slot in range(slot_count):
        if slot % chunk == 0:
            arriving[slot // chunk].wait()
        fluxes = flux_ref[slots_ref[0, slot]].astype(jnp.bfloat16)
        got = jnp.dot(fluxes, weights_ref[slot], preferred_element_type=jnp.float32)
        place = pl.multiple_of(slots_ref[1, slot] * TILE, TILE)
        sums_ref[pl.ds(place, TILE)] += got

    strips_ref = strip_scratch[0] if few else edges_ref
    strips_ref[...] = jnp.zeros_like(strips_ref)
    short = lax.broadcasted_iota(jnp.int32, (TILE, LANES), 1)
    columns_low = jnp.zeros((TILE, LANES), jnp.float32)
    columns_high = jnp.zeros((TILE, LANES), jnp.float32)
    for field in range(2):
        for half in range(halves):
            values = sums_ref[pl.ds(half * TILE + field, rows, stride=halves * TILE), :]
            partial_ref[field, :, half * LANES : (half + 1) * LANES] = values
            place = (field * 2 + half) * HALO
            strips_ref[0, place : place + WIDTH] = values[0:WIDTH]
            strips_ref[1, place : place + WIDTH] = values[rows - WIDTH : rows]
            for part in range(rows // TILE):
                block = values[part * TILE : (part + 1) * TILE]
                place = 2 * HALO * part + HALO * field
                inside = (short >= place) & (short < place + HALO)
                if half == 0:
                    columns_low = jnp.where(inside, pltpu.roll(block, place % LANES, 1), columns_low)
                if half == halves - 1:
                    columns_high = jnp.where(inside, pltpu.roll(block, (place + HALO) % LANES, 1), columns_high)
    leaving = begin([(partial_ref, partial_hbm)], semaphores, len(needed) + CHUNKS)
    strips_ref[2, 0:TILE] = columns_low
    strips_ref[3, 0:TILE] = columns_high
    if few:
        gx, gy, gy_count = lax.axis_index("gx"), lax.axis_index("gy"), lax.axis_size("gy")
        for entry in range(edges_ref.shape[0]):
            x, y = entry // 2 // gy_count, entry // 2 % gy_count
            choice = jnp.where(x < gx, 0, jnp.where(x > gx, 1, jnp.where(y < gy, 2, 3)))
            edges_ref[entry] = strips_ref[choice]

    leaving += begin([(edges_ref, edges_hbm)], semaphores, len(needed) + CHUNKS + 1)
    finish(leaving)


def halo_kernel(
    sides_hbm, temp_hbm, bathy_hbm, mixing_hbm, one_hbm, two_hbm, after_ref,
    shared_hbm, levels_hbm, mix_hbm, packed_hbm,
    shared_ref, sides_ref, temp_ref, bathy_ref, mixing_ref, pair_ref, levels_ref, mix_ref, packed_ref, semaphores, *, few,
):
    layers, rows, columns = temp_hbm.shape
    lasts = pl.ds(layers - HALO, HALO)
    needed = begin([
        (sides_hbm, sides_ref), (temp_hbm.at[pl.ds(0, TOP)], temp_ref.at[pl.ds(0, TOP)]),
        (temp_hbm.at[lasts], temp_ref.at[pl.ds(TOP, HALO)]), (bathy_hbm, bathy_ref), (mixing_hbm, mixing_ref),
        (one_hbm, pair_ref.at[0]), (two_hbm, pair_ref.at[1]),
    ], semaphores)
    odd = lax.rem(lax.axis_index("gx"), 2)
    next_ref, prev_ref = pair_ref.at[odd], pair_ref.at[1 - odd]
    finish(needed)
    gx, gx_count = lax.axis_index("gx"), lax.axis_size("gx")
    gy, gy_count = lax.axis_index("gy"), lax.axis_size("gy")
    plain = []
    for side, dy in ((0, -1), (1, 1)):
        own, after, before = (position_of(few, dx, dy) for dx in (0, 1, -1))
        packed_ref[side, 0:rows] = sides_ref[own, 2 * TILE : 2 * TILE + rows]
        packed_ref[side, rows : rows + HALO] = sides_ref[after, 2 * TILE : 2 * TILE + HALO]
        packed_ref[side, rows + HALO :] = sides_ref[before, 2 * TILE + rows - HALO : 2 * TILE + rows]
        tile = sides_ref[own, TILE : 2 * TILE]
        parts = [tile] + [pltpu.roll(tile, LANES - 2 * HALO * part, 1) for part in range(1, rows // TILE)]
        last = pltpu.roll(sides_ref[before, TILE : 2 * TILE], LANES - 2 * HALO * (rows // TILE - 1), 1)
        row = lax.broadcasted_iota(jnp.int32, (TILE, LANES), 0)
        parts.append(jnp.where(row < HALO, sides_ref[after, TILE : 2 * TILE], last))
        plain.append(jnp.concatenate(parts, axis=0))
    size = (rows + 2 * HALO, LANES)
    lane, row = (lax.broadcasted_iota(jnp.int32, size, dim) for dim in (1, 0))
    there = (lane < HALO) & (gy < gy_count - 1) | (lane >= HALO) & (gy > 0)
    there = there & ((row < rows) | (row < rows + HALO) & (gx < gx_count - 1) | (row >= rows + HALO) & (gx > 0))
    tile = jnp.where(there, side_tile(plain[0], plain[1], 0), 0.0)
    put_slab(levels_ref, bathy_ref[...].astype(jnp.float32), next_ref[layers], prev_ref[layers], tile)
    tile = side_tile(plain[0], plain[1], 1)
    put_slab(mix_ref, mixing_ref[...], next_ref[layers + 1], prev_ref[layers + 1], tile)
    leaving = begin(
        [(levels_ref, levels_hbm), (mix_ref, mix_hbm), (packed_ref, packed_hbm)], semaphores, len(needed)
    )
    used = len(needed) + 3
    for place, level in enumerate(list(range(TOP)) + list(range(layers - HALO, layers))):
        tile = side_tile(packed_ref[0], packed_ref[1], level)
        put_slab(shared_ref.at[place], temp_ref[place], next_ref[level], prev_ref[level], tile)
        leaving += begin([(shared_ref.at[place], shared_hbm.at[place])], semaphores, used + place)
    finish(leaving)


def first_kernel(
    temp_hbm, one_hbm, two_hbm, packed_hbm, other_hbm, levels_hbm, mix_hbm,
    moved_hbm, keep_hbm, top_hbm, top_keep_hbm,
    temp_ref, pair_ref, packed_ref, other_ref, levels_ref, mix_ref,
    moved_ref, keep_ref, top_ref, top_keep_ref, first_ref, skin_ref, around_ref, semaphores,
):
    layers = temp_hbm.shape[0]
    gz = lax.axis_index("gz")
    first_level = gz * layers - HALO
    needed = begin([
        (one_hbm, pair_ref.at[0]), (two_hbm, pair_ref.at[1]), (packed_hbm, packed_ref), (levels_hbm, levels_ref),
        (mix_hbm, mix_ref),
    ], semaphores)
    chunk = layers // CHUNKS
    parts = [pl.ds(part * chunk, chunk) for part in range(CHUNKS)]
    used = len(needed)
    arriving = begin([(temp_hbm.at[part], temp_ref.at[part]) for part in parts], semaphores, used)
    used += CHUNKS
    odd = lax.rem(lax.axis_index("gx"), 2)
    next_ref, prev_ref = pair_ref.at[odd], pair_ref.at[1 - odd]
    others = begin([(other_hbm, other_ref)], semaphores, used)
    used += 1
    finish(needed)
    tall, lanes = levels_ref.shape
    for side, (shift, dim) in enumerate(((1, 0), (tall - 1, 0), (1, 1), (lanes - 1, 1))):
        around_ref[side] = pltpu.roll(levels_ref[...], shift, dim)

    def level_of(place):
        return (first_level + place).astype(jnp.float32)

    def settle(place):
        level = level_of(place)
        first_ref[place] = jnp.where(levels_ref[...] > level, first_ref[place], 0.0)
        keep_ref[place] = keep_share(levels_ref[...], around_ref, mix_ref[...], level)

    def own_level(index):
        tile = side_tile(packed_ref[0], packed_ref[1], index)
        put_slab(first_ref.at[index + HALO], temp_ref[index], next_ref[index], prev_ref[index], tile)
        settle(index + HALO)

    for part in range(CHUNKS):
        arriving[part].wait()
        in_order(part * chunk, chunk, own_level)

    finish(others)
    for index in range(HALO):
        slot = jnp.where(gz == 0, index, TOP + index)
        place = jnp.where(gz == 0, HALO + layers + index, index)
        first_ref[place] = other_ref[slot]
        settle(place)

    base = jnp.where(gz == 0, HALO, 1)
    count = layers + HALO - 1
    span = pl.ds(base, count)
    leaving = begin([(keep_ref.at[span], keep_hbm.at[span])], semaphores, used)
    used += 1
    levels = levels_ref[...]
    for level in range(TOP):
        slab = jnp.where(gz == 0, first_ref[HALO + level], other_ref[level])
        skin_ref[level] = jnp.where(levels > float(level), slab, 0.0)
    for level in range(STEPS):
        top_keep_ref[level] = keep_share(levels, around_ref, mix_ref[...], jnp.float32(level))
        over = skin_ref[level - 1] if level else jnp.zeros_like(levels)
        top_ref[level] = step_slab(
            skin_ref[level], over, skin_ref[level + 1], top_keep_ref[level], mix_ref[...], levels, float(level), None
        )
    leaving += begin([(top_ref, top_hbm), (top_keep_ref, top_keep_hbm)], semaphores, used)
    used += 2
    edge = jnp.where(gz == 0, HALO - 1, HALO + layers)
    first_ref[edge] = jnp.zeros_like(first_ref[0])

    def store(place, own, wet, new):
        moved_ref[(place,) + own] = jnp.where(wet, new, 0.0)

    def done(tile, own):
        leaving.extend(begin([
            (moved_ref.at[span, pl.ds(TILE * tile, TILE)], moved_hbm.at[span, pl.ds(TILE * tile, TILE)])
        ], semaphores, used + tile))

    march(
        first_ref, store, keep_ref, mix_ref, levels_ref, base, count, level_of, None, None, levels_ref.shape, done
    )
    finish(leaving)


def pieces(count):
    return [(start, min(UNROLL, count - start)) for start in range(0, count, UNROLL)]


def skin_kernel(
    sends_hbm, slots_hbm, partial_hbm, other_hbm, edges_hbm, weights_hbm, levels_hbm, mix_hbm, top_hbm, top_keep_hbm,
    surface_hbm, back_hbm,
    back_ref, sends_ref, slots_ref, partial_ref, other_ref, edges_ref, weights_ref, levels_ref, mix_ref, top_ref, top_keep_ref, surface_ref, semaphores,
    first_ref, second_ref, sst_ref, rows_ref, *sums_scratch, few, total_levels,
):
    fields, rows, columns = partial_ref.shape
    slot_count, tile_atm, patch = weights_ref.shape
    halves = columns // LANES
    needed = begin([
        (partial_hbm, partial_ref), (other_hbm, other_ref), (levels_hbm, levels_ref), (mix_hbm, mix_ref),
        (top_hbm, top_ref), (top_keep_hbm, top_keep_ref), (slots_hbm, slots_ref),
        (sends_hbm, sends_ref), (edges_hbm, edges_ref),
    ], semaphores)
    chunk = slot_count // CHUNKS
    used = len(needed)
    arriving = begin([
        (weights_hbm.at[pl.ds(part * chunk, chunk)], weights_ref.at[pl.ds(part * chunk, chunk)])
        for part in range(CHUNKS)
    ], semaphores, used)
    used += CHUNKS

    def edge(dx, dy):
        if few:
            where = position_of(few, dx, dy)
            return edges_ref[2 * where] + edges_ref[2 * where + 1]
        where = EDGES.index((dx, dy))
        return edges_ref[2 * where] + edges_ref[2 * where + 1]

    finish(needed)
    after, before = edge(1, 0), edge(-1, 0)
    right, left = edge(0, 1), edge(0, -1)
    corners = {(dx, dy): edge(dx, dy) for dx in (1, -1) for dy in (1, -1)}
    lane = lax.broadcasted_iota(jnp.int32, (TILE, LANES), 1)
    short = lax.broadcasted_iota(jnp.int32, (HALO, LANES), 1)
    surface_ref[...] = jnp.zeros_like(surface_ref)
    for field in range(fields):
        surface_ref[field, 0:rows, 0:columns] = partial_ref[field] + other_ref[field]
        for half in range(halves):
            place = (field * 2 + half) * HALO
            here = slice(half * LANES, (half + 1) * LANES)
            surface_ref[field, rows : rows + WIDTH, here] = after[place : place + WIDTH]
            surface_ref[field, rows + 2 * HALO - WIDTH :, here] = before[place : place + WIDTH]
        for part in range(rows // TILE):
            place = 2 * HALO * part + HALO * field
            from_right = pltpu.roll(right[0:TILE], (LANES - place) % LANES, 1)
            from_left = pltpu.roll(left[0:TILE], (2 * LANES - HALO - place) % LANES, 1)
            tile = jnp.where(lane < HALO, from_right, jnp.where(lane >= LANES - HALO, from_left, 0.0))
            surface_ref[field, part * TILE : (part + 1) * TILE, columns:] = tile
        low, high = field * 2 * HALO, (field * 2 + halves - 1) * HALO
        for dx in (1, -1):
            from_right, from_left = corners[dx, 1][low : low + HALO], corners[dx, -1][high : high + HALO]
            tile = jnp.where(short < HALO, from_right, jnp.where(short >= LANES - HALO, from_left, 0.0))
            if dx == 1:
                surface_ref[field, rows : rows + WIDTH, columns:] = tile[0:WIDTH]
            else:
                surface_ref[field, rows + 2 * HALO - WIDTH :, columns:] = tile[0:WIDTH]

    leaving = begin([(surface_ref, surface_hbm)], semaphores, used)
    levels = levels_ref[...]
    forcings = [depth_share(jnp.float32(level), total_levels) * surface_ref[1] for level in range(STEPS)]
    forcings[0] = forcings[0] + surface_ref[0]
    for level in range(STEPS):
        first_ref[level] = top_ref[level] + jnp.where(levels > float(level), 0.1 * forcings[level], 0.0)
    source, target = first_ref, second_ref
    zero = jnp.zeros_like(levels)
    for step in range(2, STEPS + 1):
        for level in range(TOP - step):
            over = source[level - 1] if level else zero
            target[level] = step_slab(
                source[level], over, source[level + 1], top_keep_ref[level], mix_ref[...], levels, float(level),
                forcings[level],
            )
        source, target = target, source
    for half in range(halves):
        values = source[0, 0:rows, half * LANES : (half + 1) * LANES]
        sst_ref[half * rows : (half + 1) * rows] = values.astype(jnp.bfloat16).astype(jnp.float32)

    for slot in range(slot_count):
        tile = slots_ref[1, slot]
        place = lax.rem(tile, halves) * rows + lax.div(tile, halves)
        rows_ref[pl.ds(slot, 1)] = sst_ref[pl.ds(place, 1)]
    sums_ref = sums_scratch[0]
    sums_ref[...] = jnp.zeros_like(sums_ref)
    for group in range(slot_count // TILE):
        given = rows_ref[group * TILE : (group + 1) * TILE].astype(jnp.bfloat16)
        for row in range(TILE):
            slot = group * TILE + row
            if slot % chunk == 0:
                arriving[slot // chunk].wait()
            got = lax.dot_general(
                given, weights_ref[slot], (((1,), (1,)), ((), ())), preferred_element_type=jnp.float32
            )
            sums_ref[pl.ds(slots_ref[0, slot], 1)] += got[row : row + 1]
    me = lax.axis_index("gx") * lax.axis_size("gy") + lax.axis_index("gy")
    blocks = sums_ref.shape[0]
    copies = back_ref.shape[0] // blocks

    def place_rows(block):
        tile = sends_ref[block, me]
        back_ref[pl.ds(block * copies, copies)] = jnp.zeros((copies,) + back_ref.shape[1:], jnp.float32)

        @pl.when(tile >= 0)
        def _():
            for copy in range(copies):
                back_ref[block * copies + copy, pl.ds(tile, 1)] = sums_ref[pl.ds(block, 1)]

    if few:
        for block in range(blocks):
            place_rows(block)
    else:
        lax.fori_loop(0, blocks, lambda block, carry: (place_rows(block), carry)[1], 0)
    leaving += begin([(back_ref, back_hbm)], semaphores, used + 1)
    finish(leaving)


def ocean_kernel(
    temp_hbm, moved_hbm, keep_hbm, levels_hbm, mix_hbm, surface_hbm, ocean_hbm,
    temp_ref, keep_ref, levels_ref, mix_ref, surface_ref, semaphores, first_ref, second_ref, *, total_levels,
):
    layers, rows, columns = temp_hbm.shape
    gz = lax.axis_index("gz")
    first_level = gz * layers - HALO
    base = jnp.where(gz == 0, HALO, 1)
    count = layers + HALO - 1
    needed = begin(
        [(levels_hbm, levels_ref), (mix_hbm, mix_ref), (surface_hbm, surface_ref)], semaphores
    )
    used = len(needed)
    spans = [pl.ds(base + start, size) for start, size in pieces(count)]
    arriving = begin([(moved_hbm.at[span], first_ref.at[span]) for span in spans], semaphores, used)
    used += len(spans)
    later = begin([
        (keep_hbm.at[pl.ds(base, count)], keep_ref.at[pl.ds(base, count)]), (temp_hbm, temp_ref)
    ], semaphores, used)
    used += len(later)
    edge = jnp.where(gz == 0, HALO - 1, HALO + layers)
    first_ref[edge] = jnp.zeros_like(first_ref[0])
    second_ref[edge] = jnp.zeros_like(first_ref[0])
    finish(needed)

    def level_of(place):
        return jnp.asarray(first_level + place).astype(jnp.float32)

    def add(place):
        level = level_of(place)
        forcing = (0.1 * depth_share(level, total_levels)) * surface_ref[1]
        first_ref[place] = first_ref[place] + jnp.where(levels_ref[...] > level, forcing, 0.0)

    for (start, size), copy in zip(pieces(count), arriving):
        copy.wait()
        in_order(base + start, size, add)

    def top_forcing():
        return jnp.where(levels_ref[...] > 0.0, 0.1 * surface_ref[0], 0.0)

    @pl.when(gz == 0)
    def _():
        first_ref[HALO] = first_ref[HALO] + top_forcing()

    later[0].wait()
    leaving = []
    source, target = first_ref, second_ref
    for step in range(2, STEPS + 1):
        start = jnp.where(gz == 0, HALO, step)
        size = levels_ref.shape
        shares = [
            depth_share(level_of(start + offset), total_levels) for offset in range(layers + HALO - step)
        ]
        if step < STEPS:
            def store(place, own, wet, new, target=target):
                target[(place,) + own] = jnp.where(wet, new, 0.0)

            def done(tile, own, target=target):
                @pl.when(gz == 0)
                def _():
                    target[(HALO,) + own] = target[(HALO,) + own] + jnp.where(
                        levels_ref[own] > 0.0, 0.1 * surface_ref[(0,) + own], 0.0
                    )
        else:
            later[1].wait()
            start, size = HALO, (rows, columns)

            def store(place, own, wet, new):
                temp_ref[(place - HALO,) + own] = jnp.where(wet, new, temp_ref[(place - HALO,) + own])

            def done(tile, own):
                @pl.when(gz == 0)
                def _():
                    temp_ref[(0,) + own] = temp_ref[(0,) + own] + jnp.where(
                        levels_ref[own] > 0.0, 0.1 * surface_ref[(0,) + own], 0.0
                    )

                part = pl.ds(TILE * tile, TILE)
                leaving.extend(
                    begin([(temp_ref.at[:, part], ocean_hbm.at[:, part])], semaphores, used + tile)
                )

        march(
            source, store, keep_ref, mix_ref, levels_ref, start, layers + HALO - step, level_of, surface_ref, shares,
            size, done,
        )
        source, target = target, source
    finish(leaving)


def call(body, outs, scratch, operands, places, out_places, cost=0):
    assert len(places) == len(operands) and len(out_places) == len(outs)
    scratch_shapes = []
    for item in scratch:
        if isinstance(item, int):
            scratch_shapes.append(pltpu.SemaphoreType.DMA((item,)))
        elif isinstance(item, tuple):
            scratch_shapes.append(pltpu.VMEM(item, jnp.float32))
        else:
            scratch_shapes.append(item)
    return pl.pallas_call(
        body,
        out_shape=[jax.ShapeDtypeStruct(out, jnp.float32) for out in outs],
        in_specs=[pl.BlockSpec(memory_space=pl.ANY) for place in places],
        out_specs=[pl.BlockSpec(memory_space=pl.ANY) for place in out_places],
        scratch_shapes=scratch_shapes,
        compiler_params=pltpu.CompilerParams(vmem_limit_bytes=VMEM_LIMIT),
        cost_estimate=pl.CostEstimate(flops=cost, bytes_accessed=4 * cost // 16, transcendentals=0),
    )(*operands)


def like(array):
    return pltpu.VMEM(array.shape, array.dtype)


EDGES = [(dx, dy) for dx in (-1, 0, 1) for dy in (-1, 0, 1) if (dx, dy) != (0, 0)]


def toward(gx_count, gy_count, dx, dy):
    pairs = []
    for x in range(gx_count):
        for y in range(gy_count):
            if 0 <= x + dx < gx_count and 0 <= y + dy < gy_count:
                pairs.append(((x + dx) * gy_count + y + dy, x * gy_count + y))
    return pairs


def per_device(
    ocean_temp, bathy_levels, mixing, atm_flux, send_tiles, regrid_slots, regrid_weights
):
    layers, rows, columns = ocean_temp.shape
    gx_count, gy_count, gz_count = (lax.axis_size(axis) for axis in ALL_AXES)
    blocks = gx_count * gy_count
    own_tiles, fields, tile_atm = atm_flux.shape
    caps = send_tiles.shape[2]
    assert gz_count == 2 and caps == 1 and layers == GROUP and tile_atm == LANES
    assert columns == 2 * LANES and rows == 4 * TILE and regrid_weights.shape[2] == LANES
    total_levels = layers * gz_count
    few = blocks <= FEW
    sends = send_tiles.reshape(blocks, blocks)
    swap = [(0, 1), (1, 0)]
    tall = 2 * TILE + rows
    strip = (layers + 2, HALO, columns)
    slab = (rows + 2 * HALO, columns + LANES)
    slab_cost = 20 * slab[0] * slab[1]
    deep = (layers + 2 * HALO,) + slab

    high_rows = (2, layers, TILE, columns)
    one, two = call(
        rows_kernel, [strip, strip],
        [high_rows, pltpu.VMEM((2, TILE, columns), jnp.int32), (2, TILE, columns), strip, strip, 8],
        (ocean_temp, bathy_levels, mixing), "hhh", "hh", cost=slab_cost,
    )
    rows_one, rows_two = (
        lax.ppermute(part, "gx", [
            pair for x in range(start, gx_count - 1, 2) for pair in ((x, x + 1), (x + 1, x))
        ]) for start, part in enumerate((one, two))
    )

    outs = [(blocks, tall, LANES)] if few else [(blocks, TILE, LANES), (2, tall, LANES)]
    sides = 1 if few and gy_count == 2 else 2
    scratch = [
        pltpu.SMEM(sends.shape, jnp.int32), like(atm_flux), (sides, layers, rows, LANES),
        pltpu.VMEM((sides, rows, LANES), jnp.int32), (sides, rows, LANES), 4 + 3 * sides + FEW,
        (own_tiles, fields, LANES), outs[0], (sides, tall, LANES),
    ]
    sent = call(
        functools.partial(send_kernel, few=few, sides=sides), outs, scratch,
        (sends, atm_flux, ocean_temp, bathy_levels, mixing), "hhhhh", "h" * len(outs), cost=2 * slab_cost,
    )
    got = [lax.all_to_all(sent[0], BLOCKS_AXES, split_axis=0, concat_axis=0, tiled=True)]
    if not few:
        got.append(jnp.stack([
            lax.ppermute(sent[1][0 if dy > 0 else 1], BLOCKS_AXES, toward(gx_count, gy_count, dx, dy))
            for dx in (-1, 0, 1) for dy in (-1, 1)
        ]))

    strips = (4, 2 * TILE, LANES)
    packed_shape = (2, slab[0], LANES)
    pair_shape = (2,) + strip
    partial, edges = call(
        functools.partial(regrid_kernel, few=few),
        [(fields, rows, columns), (2 * blocks, 2 * TILE, LANES) if few else strips],
        [
            (2 * blocks, 2 * TILE, LANES) if few else strips,
            pltpu.SMEM(regrid_slots.shape, jnp.int32), (blocks, TILE, LANES), like(regrid_weights),
            (fields, rows, columns), 4 + CHUNKS, (rows * columns // LANES * TILE, LANES),
        ] + ([strips] if few else []),
        (regrid_slots, got[0], regrid_weights), "hhh", "hh", cost=4 * slab_cost,
    )
    shared, levels, mix, packed = call(
        functools.partial(halo_kernel, few=few),
        [(TOP + HALO,) + slab, slab, slab, packed_shape],
        [
            (TOP + HALO,) + slab, got[-1].shape, (TOP + HALO, rows, columns), like(bathy_levels), like(mixing),
            pair_shape, slab, slab, packed_shape, 10 + TOP + HALO,
        ],
        (got[-1], ocean_temp, bathy_levels, mixing, rows_one, rows_two, partial), "h" * 7, "hhhh", cost=slab_cost,
    )
    other_partial = lax.ppermute(partial, "gz", swap)
    other_shared = lax.ppermute(shared, "gz", swap)
    if few:
        edges = lax.all_to_all(edges, ALL_AXES, split_axis=0, concat_axis=0, tiled=True)
    else:
        choice = {-1: 1, 1: 0}
        around = jnp.stack([
            lax.ppermute(
                edges[choice[dx] if dx else (3 if dy < 0 else 2)], BLOCKS_AXES, toward(gx_count, gy_count, dx, dy)
            )
            for dx, dy in EDGES
        ])
        edges = jnp.stack([around, lax.ppermute(around, "gz", swap)], axis=1)
        edges = edges.reshape((2 * len(EDGES),) + strips[1:])

    top = (STEPS,) + slab
    parts = len(pieces(layers + HALO - 1))
    moved, keep, top_moved, top_keep = call(
        first_kernel, [deep, deep, top, top],
        [
            like(ocean_temp), pair_shape, packed_shape, (TOP + HALO,) + slab, slab, slab,
            deep, deep, top, top, deep, (TOP,) + slab, (4,) + slab, 9 + CHUNKS + parts,
        ],
        (ocean_temp, rows_one, rows_two, packed, other_shared, levels, mix), "h" * 7, "hhhh", cost=slab_cost,
    )
    surface, back = call(
        functools.partial(skin_kernel, few=few, total_levels=total_levels),
        [(fields,) + slab, ((2 if few else 1) * blocks, own_tiles, LANES)],
        [
            ((2 if few else 1) * blocks, own_tiles, LANES),
            pltpu.SMEM(sends.shape, jnp.int32), pltpu.SMEM(regrid_slots.shape, jnp.int32), like(partial), like(partial),
            edges.shape, like(regrid_weights), slab, slab, top, top, (fields,) + slab, 11 + CHUNKS,
            top, top, (rows * columns // LANES, LANES), (regrid_weights.shape[0], LANES), (blocks, LANES),
        ],
        (sends, regrid_slots, partial, other_partial, edges, regrid_weights, levels, mix, top_moved, top_keep),
        "hhhhhhhhhh", "hh", cost=20 * slab_cost,
    )
    if few:
        returned = lax.all_to_all(back, ALL_AXES, split_axis=0, concat_axis=0, tiled=True)
    else:
        returned = lax.all_to_all(back, BLOCKS_AXES, split_axis=0, concat_axis=0, tiled=True)
        returned = returned + lax.ppermute(returned, "gz", swap)
    ocean, = call(
        functools.partial(ocean_kernel, total_levels=total_levels), [ocean_temp.shape],
        [like(ocean_temp), deep, slab, slab, (fields,) + slab, 5 + parts + len(pieces(layers)), deep, deep],
        (ocean_temp, moved, keep, levels, mix, surface), "h" * 6, "h", cost=120 * slab_cost,
    )
    atm_surface = returned.sum(axis=0)
    return (ocean, atm_surface)


def solution(mesh):
    return jax.shard_map(
        per_device,
        mesh=mesh,
        in_specs=(
            P(("ens", "gz"), "gx", "gy"),
            P(("ens", "gx"), "gy"),
            P(("ens", "gx"), "gy"),
            P(("ens", "gx", "gy"), None, None),
            P(),
            P(None, ("gx", "gy", "gz")),
            P(("gx", "gy", "gz"), None, None),
        ),
        out_specs=(P(("ens", "gz"), "gx", "gy"), P(("ens", "gx", "gy"), None)),
        check_vma=False,
    )
```

```python
import functools

import jax
import jax.numpy as jnp
from jax import lax
from jax.experimental import pallas as pl
from jax.experimental.pallas import tpu as pltpu
from jax.sharding import PartitionSpec as P

STEPS = 4
HALO = STEPS
WIDTH = STEPS - 1
TOP = STEPS + 1
LANES = 128
TILE = 8
GROUP = LANES // HALO
FEW = 16
UNROLL = 8
CHUNKS = 2
BLOCKS_AXES = ("gx", "gy")
ALL_AXES = ("gx", "gy", "gz")
VMEM_LIMIT = 60 * 1024 * 1024


def position_of(few, dx, dy):
    if not few:
        return (dx + 1) * 2 + (1 if dy > 0 else 0)
    gx_count, gy_count = lax.axis_size("gx"), lax.axis_size("gy")
    x = jnp.clip(lax.axis_index("gx") + dx, 0, gx_count - 1)
    y = jnp.clip(lax.axis_index("gy") + dy, 0, gy_count - 1)
    return x * gy_count + y


def side_tile(left, right, index):
    lane = lax.broadcasted_iota(jnp.int32, left.shape, 1)
    from_right = pltpu.roll(right, lax.rem(LANES - HALO * index, LANES), 1)
    from_left = pltpu.roll(left, lax.rem(2 * LANES - HALO - HALO * index, LANES), 1)
    zero = jnp.zeros_like(left)
    return jnp.where(lane < HALO, from_right, jnp.where(lane >= LANES - HALO, from_left, zero))


def put_slab(ref, own, after, before, tile):
    rows, columns = own.shape
    ref[0:rows, 0:columns] = own
    ref[rows : rows + HALO, 0:columns] = after
    ref[rows + HALO : rows + 2 * HALO, 0:columns] = before
    ref[:, columns:] = tile


def keep_share(levels, around_ref, mixing, level):
    wet = [jnp.where(around_ref[side] > level, 0.1, 0.0) for side in range(4)]
    wet_around = (wet[0] + wet[1]) + (wet[2] + wet[3])
    above = jnp.where(level > 0.0, 1.0, 0.0)
    vertical = above + jnp.where(levels > level + 1.0, 1.0, 0.0)
    return 1.0 - wet_around - mixing * vertical


def step_slab(center, over, under, keep, mixing, levels, level, forcing):
    rows, lanes = center.shape
    lateral = pltpu.roll(center, 1, 0) + pltpu.roll(center, rows - 1, 0)
    lateral = lateral + (pltpu.roll(center, 1, 1) + pltpu.roll(center, lanes - 1, 1))
    if forcing is not None:
        lateral = lateral + forcing
    new = center * keep + 0.1 * lateral + mixing * (over + under)
    return jnp.where(levels > level, new, 0.0)


def march(source, store, keep_ref, mix_ref, levels_ref, start, count, level_of, surface_ref, shares, size, done):
    tall, lanes = levels_ref.shape
    rows, columns = size
    row = lax.broadcasted_iota(jnp.int32, (TILE, lanes), 0)[:, 0:columns]
    tiles = tall // TILE
    for tile in range(rows // TILE):
        here, above, below = (
            slice(TILE * (place % tiles), TILE * (place % tiles) + TILE) for place in (tile, tile - 1, tile + 1)
        )
        own = here, slice(0, columns)
        mixing, levels = mix_ref[own], levels_ref[own]
        surface = None if surface_ref is None else surface_ref[(1,) + own]
        over, wide = source[(start - 1,) + own], source[start, here]
        for offset in range(count):
            place = start + offset
            level = level_of(place)
            below_wide = source[place + 1, here]
            center, under = wide[:, 0:columns], below_wide[:, 0:columns]
            up = jnp.where(row == 0, pltpu.roll(source[(place, above, own[1])], 1, 0), pltpu.roll(center, 1, 0))
            down = jnp.where(
                row == TILE - 1, pltpu.roll(source[(place, below, own[1])], TILE - 1, 0),
                pltpu.roll(center, TILE - 1, 0),
            )
            side = pltpu.roll(wide, 1, 1)[:, 0:columns] + pltpu.roll(wide, lanes - 1, 1)[:, 0:columns]
            lateral = (up + down) + side
            if surface is not None:
                lateral = lateral + shares[offset] * surface
            new = center * keep_ref[(place,) + own] + 0.1 * lateral + mixing * (over + under)
            store(place, own, levels > level, new)
            over, wide = center, below_wide
        done(tile, own)


def depth_share(level, total_levels):
    return jnp.exp(jnp.full((1, 1), -4.0 / total_levels, jnp.float32) * level)


def begin(copies, semaphores, first=0):
    started = []
    for index, (source, target) in enumerate(copies):
        copy = pltpu.make_async_copy(source, target, semaphores.at[first + index])
        copy.start()
        started.append(copy)
    return started


def finish(copies):
    for copy in copies:
        copy.wait()


def in_order(start, count, body):
    whole = count // UNROLL

    def group(index, carry):
        for offset in range(UNROLL):
            body(start + index * UNROLL + offset)
        return carry

    lax.fori_loop(0, whole, group, 0)
    for index in range(whole * UNROLL, count):
        body(start + index)


def rows_kernel(
    temp_ref, bathy_ref, mixing_ref, one_hbm, two_hbm, temp_rows, bathy_rows, mixing_rows, one_ref, two_ref, semaphores,
):
    layers, rows, columns = temp_ref.shape
    copies = []
    for side in range(2):
        part = pl.ds(side * (rows - TILE), TILE)
        copies += [(temp_ref.at[:, part], temp_rows.at[side]), (bathy_ref.at[part], bathy_rows.at[side])]
        copies += [(mixing_ref.at[part], mixing_rows.at[side])]
    finish(begin(copies, semaphores))
    even = lax.rem(lax.axis_index("gx"), 2) == 0
    fields = [
        (slice(0, layers), lambda side: temp_rows[side]), (layers, lambda side: bathy_rows[side].astype(jnp.float32)),
        (layers + 1, lambda side: mixing_rows[side]),
    ]
    for place, read in fields:
        low, high = read(0)[..., 0:HALO, :], read(1)[..., TILE - HALO :, :]
        one_ref[place] = jnp.where(even, high, low)
        two_ref[place] = jnp.where(even, low, high)
    finish(begin([(one_ref, one_hbm), (two_ref, two_hbm)], semaphores, len(copies)))


def send_kernel(sends_hbm, flux_hbm, temp_hbm, bathy_hbm, mixing_hbm, *refs, few, sides):
    if few:
        (
            message_hbm, sends_ref, flux_ref, temp_ref, bathy_ref, mixing_ref, semaphores, flux_scratch, message_ref,
            strips_ref,
        ) = refs
        fluxes_ref = message_ref
    else:
        (
            fluxes_hbm, strips_hbm, sends_ref, flux_ref, temp_ref, bathy_ref, mixing_ref, semaphores, flux_scratch,
            fluxes_ref, strips_ref,
        ) = refs
    layers, rows, columns = temp_hbm.shape
    gy, gy_count = lax.axis_index("gy"), lax.axis_size("gy")
    me = lax.axis_index("gx") * gy_count + gy
    copies = [(sends_hbm, sends_ref), (flux_hbm, flux_ref)]
    for place in range(sides):
        side = 1 - gy if sides == 1 else place
        window = pl.ds(pl.multiple_of(side * (columns - LANES), LANES), LANES)
        copies += [(bathy_hbm.at[:, window], bathy_ref.at[place]), (mixing_hbm.at[:, window], mixing_ref.at[place])]
        copies += [(temp_hbm.at[:, :, window], temp_ref.at[place])]
    copies = begin(copies, semaphores)
    lane = lax.broadcasted_iota(jnp.int32, (rows, LANES), 1)
    short = lax.broadcasted_iota(jnp.int32, (TILE, LANES), 1)
    finish(copies)
    for side in range(sides):
        base = HALO * (1 - gy) if sides == 1 else HALO * side
        strip = jnp.zeros((rows, LANES), jnp.float32)
        for index in range(layers):
            place = HALO * index
            moved = pltpu.roll(temp_ref[side, index], lax.rem(place + base, LANES), 1)
            strip = jnp.where((lane >= place) & (lane < place + HALO), moved, strip)
        strips_ref[side, 2 * TILE : 2 * TILE + rows] = strip
        plain = jnp.zeros((TILE, LANES), jnp.float32)
        for part in range(rows // TILE):
            here = slice(part * TILE, (part + 1) * TILE)
            for which, values in enumerate((bathy_ref[side, here].astype(jnp.float32), mixing_ref[side, here])):
                place = 2 * HALO * part + HALO * which
                moved = pltpu.roll(values, lax.rem(place + base, LANES), 1)
                plain = jnp.where((short >= place) & (short < place + HALO), moved, plain)
        strips_ref[side, TILE : 2 * TILE] = plain
        strips_ref[side, 0:TILE] = jnp.zeros((TILE, LANES), jnp.float32)
    flux_scratch[...] = flux_ref[...].astype(jnp.float32)
    fields = flux_ref.shape[1]

    def one(block, carry):
        tile = sends_ref[me, block]
        if few:
            side = 0 if sides == 1 else (lax.rem(block, gy_count) > gy).astype(jnp.int32)
            message_ref[block] = strips_ref[side]
        else:
            fluxes_ref[block] = jnp.zeros(fluxes_ref.shape[1:], jnp.float32)
        sent = jnp.where(tile >= 0, flux_scratch[jnp.maximum(tile, 0)], 0.0)
        fluxes_ref[block, 0:fields] = sent
        return carry

    used = len(copies)
    if few:
        leaving = []
        for block in range(fluxes_ref.shape[0]):
            one(block, 0)
            leaving += begin([(message_ref.at[block], message_hbm.at[block])], semaphores, used + block)
    else:
        leaving = begin([(strips_ref, strips_hbm)], semaphores, used)
        lax.fori_loop(0, fluxes_ref.shape[0], one, 0)
        leaving += begin([(fluxes_ref, fluxes_hbm)], semaphores, used + 1)
    finish(leaving)


def regrid_kernel(
    slots_hbm, flux_hbm, weights_hbm, partial_hbm, edges_hbm,
    edges_ref, slots_ref, flux_ref, weights_ref, partial_ref, semaphores, sums_ref, *strip_scratch, few,
):
    fields, rows, columns = partial_ref.shape
    slot_count, tile_atm, patch = weights_ref.shape
    halves = columns // LANES
    needed = begin([(slots_hbm, slots_ref), (flux_hbm.at[:, pl.ds(0, TILE)], flux_ref)], semaphores)
    chunk = slot_count // CHUNKS
    arriving = begin([
        (weights_hbm.at[pl.ds(part * chunk, chunk)], weights_ref.at[pl.ds(part * chunk, chunk)])
        for part in range(CHUNKS)
    ], semaphores, len(needed))
    sums_ref[...] = jnp.zeros_like(sums_ref)
    finish(needed)
    for slot in range(slot_count):
        if slot % chunk == 0:
            arriving[slot // chunk].wait()
        fluxes = flux_ref[slots_ref[0, slot]].astype(jnp.bfloat16)
        got = jnp.dot(fluxes, weights_ref[slot], preferred_element_type=jnp.float32)
        place = pl.multiple_of(slots_ref[1, slot] * TILE, TILE)
        sums_ref[pl.ds(place, TILE)] += got

    strips_ref = strip_scratch[0] if few else edges_ref
    strips_ref[...] = jnp.zeros_like(strips_ref)
    short = lax.broadcasted_iota(jnp.int32, (TILE, LANES), 1)
    columns_low = jnp.zeros((TILE, LANES), jnp.float32)
    columns_high = jnp.zeros((TILE, LANES), jnp.float32)
    for field in range(2):
        for half in range(halves):
            values = sums_ref[pl.ds(half * TILE + field, rows, stride=halves * TILE), :]
            partial_ref[field, :, half * LANES : (half + 1) * LANES] = values
            place = (field * 2 + half) * HALO
            strips_ref[0, place : place + WIDTH] = values[0:WIDTH]
            strips_ref[1, place : place + WIDTH] = values[rows - WIDTH : rows]
            for part in range(rows // TILE):
                block = values[part * TILE : (part + 1) * TILE]
                place = 2 * HALO * part + HALO * field
                inside = (short >= place) & (short < place + HALO)
                if half == 0:
                    columns_low = jnp.where(inside, pltpu.roll(block, place % LANES, 1), columns_low)
                if half == halves - 1:
                    columns_high = jnp.where(inside, pltpu.roll(block, (place + HALO) % LANES, 1), columns_high)
    leaving = begin([(partial_ref, partial_hbm)], semaphores, len(needed) + CHUNKS)
    strips_ref[2, 0:TILE] = columns_low
    strips_ref[3, 0:TILE] = columns_high
    if few:
        gx, gy, gy_count = lax.axis_index("gx"), lax.axis_index("gy"), lax.axis_size("gy")
        for entry in range(edges_ref.shape[0]):
            x, y = entry // 2 // gy_count, entry // 2 % gy_count
            choice = jnp.where(x < gx, 0, jnp.where(x > gx, 1, jnp.where(y < gy, 2, 3)))
            edges_ref[entry] = strips_ref[choice]

    leaving += begin([(edges_ref, edges_hbm)], semaphores, len(needed) + CHUNKS + 1)
    finish(leaving)


def halo_kernel(
    sides_hbm, temp_hbm, bathy_hbm, mixing_hbm, one_hbm, two_hbm, after_ref,
    shared_hbm, levels_hbm, mix_hbm, packed_hbm,
    shared_ref, sides_ref, temp_ref, bathy_ref, mixing_ref, pair_ref, levels_ref, mix_ref, packed_ref, semaphores, *, few,
):
    layers, rows, columns = temp_hbm.shape
    lasts = pl.ds(layers - HALO, HALO)
    needed = begin([
        (sides_hbm, sides_ref), (temp_hbm.at[pl.ds(0, TOP)], temp_ref.at[pl.ds(0, TOP)]),
        (temp_hbm.at[lasts], temp_ref.at[pl.ds(TOP, HALO)]), (bathy_hbm, bathy_ref), (mixing_hbm, mixing_ref),
        (one_hbm, pair_ref.at[0]), (two_hbm, pair_ref.at[1]),
    ], semaphores)
    odd = lax.rem(lax.axis_index("gx"), 2)
    next_ref, prev_ref = pair_ref.at[odd], pair_ref.at[1 - odd]
    finish(needed)
    gx, gx_count = lax.axis_index("gx"), lax.axis_size("gx")
    gy, gy_count = lax.axis_index("gy"), lax.axis_size("gy")
    plain = []
    for side, dy in ((0, -1), (1, 1)):
        own, after, before = (position_of(few, dx, dy) for dx in (0, 1, -1))
        packed_ref[side, 0:rows] = sides_ref[own, 2 * TILE : 2 * TILE + rows]
        packed_ref[side, rows : rows + HALO] = sides_ref[after, 2 * TILE : 2 * TILE + HALO]
        packed_ref[side, rows + HALO :] = sides_ref[before, 2 * TILE + rows - HALO : 2 * TILE + rows]
        tile = sides_ref[own, TILE : 2 * TILE]
        parts = [tile] + [pltpu.roll(tile, LANES - 2 * HALO * part, 1) for part in range(1, rows // TILE)]
        last = pltpu.roll(sides_ref[before, TILE : 2 * TILE], LANES - 2 * HALO * (rows // TILE - 1), 1)
        row = lax.broadcasted_iota(jnp.int32, (TILE, LANES), 0)
        parts.append(jnp.where(row < HALO, sides_ref[after, TILE : 2 * TILE], last))
        plain.append(jnp.concatenate(parts, axis=0))
    size = (rows + 2 * HALO, LANES)
    lane, row = (lax.broadcasted_iota(jnp.int32, size, dim) for dim in (1, 0))
    there = (lane < HALO) & (gy < gy_count - 1) | (lane >= HALO) & (gy > 0)
    there = there & ((row < rows) | (row < rows + HALO) & (gx < gx_count - 1) | (row >= rows + HALO) & (gx > 0))
    tile = jnp.where(there, side_tile(plain[0], plain[1], 0), 0.0)
    put_slab(levels_ref, bathy_ref[...].astype(jnp.float32), next_ref[layers], prev_ref[layers], tile)
    tile = side_tile(plain[0], plain[1], 1)
    put_slab(mix_ref, mixing_ref[...], next_ref[layers + 1], prev_ref[layers + 1], tile)
    leaving = begin(
        [(levels_ref, levels_hbm), (mix_ref, mix_hbm), (packed_ref, packed_hbm)], semaphores, len(needed)
    )
    used = len(needed) + 3
    for place, level in enumerate(list(range(TOP)) + list(range(layers - HALO, layers))):
        tile = side_tile(packed_ref[0], packed_ref[1], level)
        put_slab(shared_ref.at[place], temp_ref[place], next_ref[level], prev_ref[level], tile)
        leaving += begin([(shared_ref.at[place], shared_hbm.at[place])], semaphores, used + place)
    finish(leaving)


def first_kernel(
    temp_hbm, one_hbm, two_hbm, packed_hbm, other_hbm, levels_hbm, mix_hbm,
    moved_hbm, keep_hbm, top_hbm, top_keep_hbm,
    temp_ref, pair_ref, packed_ref, other_ref, levels_ref, mix_ref,
    moved_ref, keep_ref, top_ref, top_keep_ref, first_ref, skin_ref, around_ref, semaphores,
):
    layers = temp_hbm.shape[0]
    gz = lax.axis_index("gz")
    first_level = gz * layers - HALO
    needed = begin([
        (one_hbm, pair_ref.at[0]), (two_hbm, pair_ref.at[1]), (packed_hbm, packed_ref), (levels_hbm, levels_ref),
        (mix_hbm, mix_ref),
    ], semaphores)
    chunk = layers // CHUNKS
    parts = [pl.ds(part * chunk, chunk) for part in range(CHUNKS)]
    used = len(needed)
    arriving = begin([(temp_hbm.at[part], temp_ref.at[part]) for part in parts], semaphores, used)
    used += CHUNKS
    odd = lax.rem(lax.axis_index("gx"), 2)
    next_ref, prev_ref = pair_ref.at[odd], pair_ref.at[1 - odd]
    others = begin([(other_hbm, other_ref)], semaphores, used)
    used += 1
    finish(needed)
    tall, lanes = levels_ref.shape
    for side, (shift, dim) in enumerate(((1, 0), (tall - 1, 0), (1, 1), (lanes - 1, 1))):
        around_ref[side] = pltpu.roll(levels_ref[...], shift, dim)

    def level_of(place):
        return (first_level + place).astype(jnp.float32)

    def settle(place):
        level = level_of(place)
        first_ref[place] = jnp.where(levels_ref[...] > level, first_ref[place], 0.0)
        keep_ref[place] = keep_share(levels_ref[...], around_ref, mix_ref[...], level)

    def own_level(index):
        tile = side_tile(packed_ref[0], packed_ref[1], index)
        put_slab(first_ref.at[index + HALO], temp_ref[index], next_ref[index], prev_ref[index], tile)
        settle(index + HALO)

    for part in range(CHUNKS):
        arriving[part].wait()
        in_order(part * chunk, chunk, own_level)

    finish(others)
    for index in range(HALO):
        slot = jnp.where(gz == 0, index, TOP + index)
        place = jnp.where(gz == 0, HALO + layers + index, index)
        first_ref[place] = other_ref[slot]
        settle(place)

    base = jnp.where(gz == 0, HALO, 1)
    count = layers + HALO - 1
    span = pl.ds(base, count)
    leaving = begin([(keep_ref.at[span], keep_hbm.at[span])], semaphores, used)
    used += 1
    levels = levels_ref[...]
    for level in range(TOP):
        slab = jnp.where(gz == 0, first_ref[HALO + level], other_ref[level])
        skin_ref[level] = jnp.where(levels > float(level), slab, 0.0)
    for level in range(STEPS):
        top_keep_ref[level] = keep_share(levels, around_ref, mix_ref[...], jnp.float32(level))
        over = skin_ref[level - 1] if level else jnp.zeros_like(levels)
        top_ref[level] = step_slab(
            skin_ref[level], over, skin_ref[level + 1], top_keep_ref[level], mix_ref[...], levels, float(level), None
        )
    leaving += begin([(top_ref, top_hbm), (top_keep_ref, top_keep_hbm)], semaphores, used)
    used += 2
    edge = jnp.where(gz == 0, HALO - 1, HALO + layers)
    first_ref[edge] = jnp.zeros_like(first_ref[0])

    def store(place, own, wet, new):
        moved_ref[(place,) + own] = jnp.where(wet, new, 0.0)

    def done(tile, own):
        leaving.extend(begin([
            (moved_ref.at[span, pl.ds(TILE * tile, TILE)], moved_hbm.at[span, pl.ds(TILE * tile, TILE)])
        ], semaphores, used + tile))

    march(
        first_ref, store, keep_ref, mix_ref, levels_ref, base, count, level_of, None, None, levels_ref.shape, done
    )
    finish(leaving)


def pieces(count):
    return [(start, min(UNROLL, count - start)) for start in range(0, count, UNROLL)]


def skin_kernel(
    sends_hbm, slots_hbm, partial_hbm, other_hbm, edges_hbm, weights_hbm, levels_hbm, mix_hbm, top_hbm, top_keep_hbm,
    surface_hbm, back_hbm,
    back_ref, sends_ref, slots_ref, partial_ref, other_ref, edges_ref, weights_ref, levels_ref, mix_ref, top_ref, top_keep_ref, surface_ref, semaphores,
    first_ref, second_ref, sst_ref, rows_ref, *sums_scratch, few, total_levels,
):
    fields, rows, columns = partial_ref.shape
    slot_count, tile_atm, patch = weights_ref.shape
    halves = columns // LANES
    needed = begin([
        (partial_hbm, partial_ref), (other_hbm, other_ref), (levels_hbm, levels_ref), (mix_hbm, mix_ref),
        (top_hbm, top_ref), (top_keep_hbm, top_keep_ref), (slots_hbm, slots_ref),
        (sends_hbm, sends_ref), (edges_hbm, edges_ref),
    ], semaphores)
    chunk = slot_count // CHUNKS
    used = len(needed)
    arriving = begin([
        (weights_hbm.at[pl.ds(part * chunk, chunk)], weights_ref.at[pl.ds(part * chunk, chunk)])
        for part in range(CHUNKS)
    ], semaphores, used)
    used += CHUNKS

    def edge(dx, dy):
        if few:
            where = position_of(few, dx, dy)
            return edges_ref[2 * where] + edges_ref[2 * where + 1]
        where = EDGES.index((dx, dy))
        return edges_ref[2 * where] + edges_ref[2 * where + 1]

    finish(needed)
    after, before = edge(1, 0), edge(-1, 0)
    right, left = edge(0, 1), edge(0, -1)
    corners = {(dx, dy): edge(dx, dy) for dx in (1, -1) for dy in (1, -1)}
    lane = lax.broadcasted_iota(jnp.int32, (TILE, LANES), 1)
    short = lax.broadcasted_iota(jnp.int32, (HALO, LANES), 1)
    surface_ref[...] = jnp.zeros_like(surface_ref)
    for field in range(fields):
        surface_ref[field, 0:rows, 0:columns] = partial_ref[field] + other_ref[field]
        for half in range(halves):
            place = (field * 2 + half) * HALO
            here = slice(half * LANES, (half + 1) * LANES)
            surface_ref[field, rows : rows + WIDTH, here] = after[place : place + WIDTH]
            surface_ref[field, rows + 2 * HALO - WIDTH :, here] = before[place : place + WIDTH]
        for part in range(rows // TILE):
            place = 2 * HALO * part + HALO * field
            from_right = pltpu.roll(right[0:TILE], (LANES - place) % LANES, 1)
            from_left = pltpu.roll(left[0:TILE], (2 * LANES - HALO - place) % LANES, 1)
            tile = jnp.where(lane < HALO, from_right, jnp.where(lane >= LANES - HALO, from_left, 0.0))
            surface_ref[field, part * TILE : (part + 1) * TILE, columns:] = tile
        low, high = field * 2 * HALO, (field * 2 + halves - 1) * HALO
        for dx in (1, -1):
            from_right, from_left = corners[dx, 1][low : low + HALO], corners[dx, -1][high : high + HALO]
            tile = jnp.where(short < HALO, from_right, jnp.where(short >= LANES - HALO, from_left, 0.0))
            if dx == 1:
                surface_ref[field, rows : rows + WIDTH, columns:] = tile[0:WIDTH]
            else:
                surface_ref[field, rows + 2 * HALO - WIDTH :, columns:] = tile[0:WIDTH]

    leaving = begin([(surface_ref, surface_hbm)], semaphores, used)
    levels = levels_ref[...]
    forcings = [depth_share(jnp.float32(level), total_levels) * surface_ref[1] for level in range(STEPS)]
    forcings[0] = forcings[0] + surface_ref[0]
    for level in range(STEPS):
        first_ref[level] = top_ref[level] + jnp.where(levels > float(level), 0.1 * forcings[level], 0.0)
    source, target = first_ref, second_ref
    zero = jnp.zeros_like(levels)
    for step in range(2, STEPS + 1):
        for level in range(TOP - step):
            over = source[level - 1] if level else zero
            target[level] = step_slab(
                source[level], over, source[level + 1], top_keep_ref[level], mix_ref[...], levels, float(level),
                forcings[level],
            )
        source, target = target, source
    for half in range(halves):
        values = source[0, 0:rows, half * LANES : (half + 1) * LANES]
        sst_ref[half * rows : (half + 1) * rows] = values.astype(jnp.bfloat16).astype(jnp.float32)

    for slot in range(slot_count):
        tile = slots_ref[1, slot]
        place = lax.rem(tile, halves) * rows + lax.div(tile, halves)
        rows_ref[pl.ds(slot, 1)] = sst_ref[pl.ds(place, 1)]
    sums_ref = sums_scratch[0]
    sums_ref[...] = jnp.zeros_like(sums_ref)
    for group in range(slot_count // TILE):
        given = rows_ref[group * TILE : (group + 1) * TILE].astype(jnp.bfloat16)
        for row in range(TILE):
            slot = group * TILE + row
            if slot % chunk == 0:
                arriving[slot // chunk].wait()
            got = lax.dot_general(
                given, weights_ref[slot], (((1,), (1,)), ((), ())), preferred_element_type=jnp.float32
            )
            sums_ref[pl.ds(slots_ref[0, slot], 1)] += got[row : row + 1]
    me = lax.axis_index("gx") * lax.axis_size("gy") + lax.axis_index("gy")
    blocks = sums_ref.shape[0]
    copies = back_ref.shape[0] // blocks

    def place_rows(block):
        tile = sends_ref[block, me]
        back_ref[pl.ds(block * copies, copies)] = jnp.zeros((copies,) + back_ref.shape[1:], jnp.float32)

        @pl.when(tile >= 0)
        def _():
            for copy in range(copies):
                back_ref[block * copies + copy, pl.ds(tile, 1)] = sums_ref[pl.ds(block, 1)]

    if few:
        for block in range(blocks):
            place_rows(block)
    else:
        lax.fori_loop(0, blocks, lambda block, carry: (place_rows(block), carry)[1], 0)
    leaving += begin([(back_ref, back_hbm)], semaphores, used + 1)
    finish(leaving)


def ocean_kernel(
    temp_hbm, moved_hbm, keep_hbm, levels_hbm, mix_hbm, surface_hbm, ocean_hbm,
    temp_ref, keep_ref, levels_ref, mix_ref, surface_ref, semaphores, first_ref, second_ref, *, total_levels,
):
    layers, rows, columns = temp_hbm.shape
    gz = lax.axis_index("gz")
    first_level = gz * layers - HALO
    base = jnp.where(gz == 0, HALO, 1)
    count = layers + HALO - 1
    needed = begin(
        [(levels_hbm, levels_ref), (mix_hbm, mix_ref), (surface_hbm, surface_ref)], semaphores
    )
    used = len(needed)
    spans = [pl.ds(base + start, size) for start, size in pieces(count)]
    arriving = begin([(moved_hbm.at[span], first_ref.at[span]) for span in spans], semaphores, used)
    used += len(spans)
    later = begin([
        (keep_hbm.at[pl.ds(base, count)], keep_ref.at[pl.ds(base, count)]), (temp_hbm, temp_ref)
    ], semaphores, used)
    used += len(later)
    edge = jnp.where(gz == 0, HALO - 1, HALO + layers)
    first_ref[edge] = jnp.zeros_like(first_ref[0])
    second_ref[edge] = jnp.zeros_like(first_ref[0])
    finish(needed)

    def level_of(place):
        return jnp.asarray(first_level + place).astype(jnp.float32)

    def add(place):
        level = level_of(place)
        forcing = (0.1 * depth_share(level, total_levels)) * surface_ref[1]
        first_ref[place] = first_ref[place] + jnp.where(levels_ref[...] > level, forcing, 0.0)

    for (start, size), copy in zip(pieces(count), arriving):
        copy.wait()
        in_order(base + start, size, add)

    def top_forcing():
        return jnp.where(levels_ref[...] > 0.0, 0.1 * surface_ref[0], 0.0)

    @pl.when(gz == 0)
    def _():
        first_ref[HALO] = first_ref[HALO] + top_forcing()

    later[0].wait()
    leaving = []
    source, target = first_ref, second_ref
    for step in range(2, STEPS + 1):
        start = jnp.where(gz == 0, HALO, step)
        size = levels_ref.shape
        shares = [
            depth_share(level_of(start + offset), total_levels) for offset in range(layers + HALO - step)
        ]
        if step < STEPS:
            def store(place, own, wet, new, target=target):
                target[(place,) + own] = jnp.where(wet, new, 0.0)

            def done(tile, own, target=target):
                @pl.when(gz == 0)
                def _():
                    target[(HALO,) + own] = target[(HALO,) + own] + jnp.where(
                        levels_ref[own] > 0.0, 0.1 * surface_ref[(0,) + own], 0.0
                    )
        else:
            later[1].wait()
            start, size = HALO, (rows, columns)

            def store(place, own, wet, new):
                temp_ref[(place - HALO,) + own] = jnp.where(wet, new, temp_ref[(place - HALO,) + own])

            def done(tile, own):
                @pl.when(gz == 0)
                def _():
                    temp_ref[(0,) + own] = temp_ref[(0,) + own] + jnp.where(
                        levels_ref[own] > 0.0, 0.1 * surface_ref[(0,) + own], 0.0
                    )

                part = pl.ds(TILE * tile, TILE)
                leaving.extend(
                    begin([(temp_ref.at[:, part], ocean_hbm.at[:, part])], semaphores, used + tile)
                )

        march(
            source, store, keep_ref, mix_ref, levels_ref, start, layers + HALO - step, level_of, surface_ref, shares,
            size, done,
        )
        source, target = target, source
    finish(leaving)


def call(body, outs, scratch, operands, places, out_places, cost=0):
    assert len(places) == len(operands) and len(out_places) == len(outs)
    scratch_shapes = []
    for item in scratch:
        if isinstance(item, int):
            scratch_shapes.append(pltpu.SemaphoreType.DMA((item,)))
        elif isinstance(item, tuple):
            scratch_shapes.append(pltpu.VMEM(item, jnp.float32))
        else:
            scratch_shapes.append(item)
    return pl.pallas_call(
        body,
        out_shape=[jax.ShapeDtypeStruct(out, jnp.float32) for out in outs],
        in_specs=[pl.BlockSpec(memory_space=pl.ANY) for place in places],
        out_specs=[pl.BlockSpec(memory_space=pl.ANY) for place in out_places],
        scratch_shapes=scratch_shapes,
        compiler_params=pltpu.CompilerParams(vmem_limit_bytes=VMEM_LIMIT),
        cost_estimate=pl.CostEstimate(flops=cost, bytes_accessed=4 * cost // 16, transcendentals=0),
    )(*operands)


def like(array):
    return pltpu.VMEM(array.shape, array.dtype)


EDGES = [(dx, dy) for dx in (-1, 0, 1) for dy in (-1, 0, 1) if (dx, dy) != (0, 0)]


def toward(gx_count, gy_count, dx, dy):
    pairs = []
    for x in range(gx_count):
        for y in range(gy_count):
            if 0 <= x + dx < gx_count and 0 <= y + dy < gy_count:
                pairs.append(((x + dx) * gy_count + y + dy, x * gy_count + y))
    return pairs


def per_device(
    ocean_temp, bathy_levels, mixing, atm_flux, send_tiles, regrid_slots, regrid_weights
):
    layers, rows, columns = ocean_temp.shape
    gx_count, gy_count, gz_count = (lax.axis_size(axis) for axis in ALL_AXES)
    blocks = gx_count * gy_count
    own_tiles, fields, tile_atm = atm_flux.shape
    caps = send_tiles.shape[2]
    assert gz_count == 2 and caps == 1 and layers == GROUP and tile_atm == LANES
    assert columns == 2 * LANES and rows == 4 * TILE and regrid_weights.shape[2] == LANES
    total_levels = layers * gz_count
    few = blocks <= FEW
    sends = send_tiles.reshape(blocks, blocks)
    swap = [(0, 1), (1, 0)]
    tall = 2 * TILE + rows
    strip = (layers + 2, HALO, columns)
    slab = (rows + 2 * HALO, columns + LANES)
    slab_cost = 20 * slab[0] * slab[1]
    deep = (layers + 2 * HALO,) + slab

    high_rows = (2, layers, TILE, columns)
    one, two = call(
        rows_kernel, [strip, strip],
        [high_rows, pltpu.VMEM((2, TILE, columns), jnp.int32), (2, TILE, columns), strip, strip, 8],
        (ocean_temp, bathy_levels, mixing), "hhh", "hh", cost=slab_cost,
    )
    rows_one, rows_two = (
        lax.ppermute(part, "gx", [
            pair for x in range(start, gx_count - 1, 2) for pair in ((x, x + 1), (x + 1, x))
        ]) for start, part in enumerate((one, two))
    )

    outs = [(blocks, tall, LANES)] if few else [(blocks, TILE, LANES), (2, tall, LANES)]
    sides = 1 if few and gy_count == 2 else 2
    scratch = [
        pltpu.SMEM(sends.shape, jnp.int32), like(atm_flux), (sides, layers, rows, LANES),
        pltpu.VMEM((sides, rows, LANES), jnp.int32), (sides, rows, LANES), 4 + 3 * sides + FEW,
        (own_tiles, fields, LANES), outs[0], (sides, tall, LANES),
    ]
    sent = call(
        functools.partial(send_kernel, few=few, sides=sides), outs, scratch,
        (sends, atm_flux, ocean_temp, bathy_levels, mixing), "hhhhh", "h" * len(outs), cost=2 * slab_cost,
    )
    got = [lax.all_to_all(sent[0], BLOCKS_AXES, split_axis=0, concat_axis=0, tiled=True)]
    if not few:
        got.append(jnp.stack([
            lax.ppermute(sent[1][0 if dy > 0 else 1], BLOCKS_AXES, toward(gx_count, gy_count, dx, dy))
            for dx in (-1, 0, 1) for dy in (-1, 1)
        ]))

    strips = (4, 2 * TILE, LANES)
    packed_shape = (2, slab[0], LANES)
    pair_shape = (2,) + strip
    partial, edges = call(
        functools.partial(regrid_kernel, few=few),
        [(fields, rows, columns), (2 * blocks, 2 * TILE, LANES) if few else strips],
        [
            (2 * blocks, 2 * TILE, LANES) if few else strips,
            pltpu.SMEM(regrid_slots.shape, jnp.int32), (blocks, TILE, LANES), like(regrid_weights),
            (fields, rows, columns), 4 + CHUNKS, (rows * columns // LANES * TILE, LANES),
        ] + ([strips] if few else []),
        (regrid_slots, got[0], regrid_weights), "hhh", "hh", cost=4 * slab_cost,
    )
    shared, levels, mix, packed = call(
        functools.partial(halo_kernel, few=few),
        [(TOP + HALO,) + slab, slab, slab, packed_shape],
        [
            (TOP + HALO,) + slab, got[-1].shape, (TOP + HALO, rows, columns), like(bathy_levels), like(mixing),
            pair_shape, slab, slab, packed_shape, 10 + TOP + HALO,
        ],
        (got[-1], ocean_temp, bathy_levels, mixing, rows_one, rows_two, partial), "h" * 7, "hhhh", cost=slab_cost,
    )
    other_partial = lax.ppermute(partial, "gz", swap)
    other_shared = lax.ppermute(shared, "gz", swap)
    if few:
        edges = lax.all_to_all(edges, ALL_AXES, split_axis=0, concat_axis=0, tiled=True)
    else:
        choice = {-1: 1, 1: 0}
        around = jnp.stack([
            lax.ppermute(
                edges[choice[dx] if dx else (3 if dy < 0 else 2)], BLOCKS_AXES, toward(gx_count, gy_count, dx, dy)
            )
            for dx, dy in EDGES
        ])
        edges = jnp.stack([around, lax.ppermute(around, "gz", swap)], axis=1)
        edges = edges.reshape((2 * len(EDGES),) + strips[1:])

    top = (STEPS,) + slab
    parts = len(pieces(layers + HALO - 1))
    moved, keep, top_moved, top_keep = call(
        first_kernel, [deep, deep, top, top],
        [
            like(ocean_temp), pair_shape, packed_shape, (TOP + HALO,) + slab, slab, slab,
            deep, deep, top, top, deep, (TOP,) + slab, (4,) + slab, 9 + CHUNKS + parts,
        ],
        (ocean_temp, rows_one, rows_two, packed, other_shared, levels, mix), "h" * 7, "hhhh", cost=slab_cost,
    )
    surface, back = call(
        functools.partial(skin_kernel, few=few, total_levels=total_levels),
        [(fields,) + slab, ((2 if few else 1) * blocks, own_tiles, LANES)],
        [
            ((2 if few else 1) * blocks, own_tiles, LANES),
            pltpu.SMEM(sends.shape, jnp.int32), pltpu.SMEM(regrid_slots.shape, jnp.int32), like(partial), like(partial),
            edges.shape, like(regrid_weights), slab, slab, top, top, (fields,) + slab, 11 + CHUNKS,
            top, top, (rows * columns // LANES, LANES), (regrid_weights.shape[0], LANES), (blocks, LANES),
        ],
        (sends, regrid_slots, partial, other_partial, edges, regrid_weights, levels, mix, top_moved, top_keep),
        "hhhhhhhhhh", "hh", cost=20 * slab_cost,
    )
    if few:
        returned = lax.all_to_all(back, ALL_AXES, split_axis=0, concat_axis=0, tiled=True)
    else:
        returned = lax.all_to_all(back, BLOCKS_AXES, split_axis=0, concat_axis=0, tiled=True)
        returned = returned + lax.ppermute(returned, "gz", swap)
    ocean, = call(
        functools.partial(ocean_kernel, total_levels=total_levels), [ocean_temp.shape],
        [like(ocean_temp), deep, slab, slab, (fields,) + slab, 5 + parts + len(pieces(layers)), deep, deep],
        (ocean_temp, moved, keep, levels, mix, surface), "h" * 6, "h", cost=120 * slab_cost,
    )
    atm_surface = returned.sum(axis=0)
    return (ocean, atm_surface)


def solution(mesh):
    return jax.shard_map(
        per_device,
        mesh=mesh,
        in_specs=(
            P(("ens", "gz"), "gx", "gy"),
            P(("ens", "gx"), "gy"),
            P(("ens", "gx"), "gy"),
            P(("ens", "gx", "gy"), None, None),
            P(),
            P(None, ("gx", "gy", "gz")),
            P(("gx", "gy", "gz"), None, None),
        ),
        out_specs=(P(("ens", "gz"), "gx", "gy"), P(("ens", "gx", "gy"), None)),
        check_vma=False,
    )
```
